32 devices in a mesh: section: 2 (over core), dp: 16 (over z, y, x).
Axes of the slice: x: 2, y: 2, z: 4, core: 2. Of those that a mesh axis runs over, the one named last changes fastest.
Arguments:
- inputs: bfloat16 [2, 16, 512, 768], P(None, 'dp'), may hold values from -8 to 8
- cotangent: bfloat16 [2, 16, 512, 768], P(None, 'dp'), may hold values from -6 to 6
- lengths: int32 [2, 16, 2], P(None, 'dp'), may hold values from 0 to 512, as said below
- weight_in: bfloat16 [2, 5376, 768], P('section', 'dp'), may hold values from -0.21875 to 0.21875
- weight_out: bfloat16 [2, 3840, 768], P('section', 'dp'), may hold values from -1.6329932 to 1.6329932
- scales: bfloat16 [2, 896], P('section', 'dp'), may hold values from 0.099609375 to 1.8984375
Outputs:
- layer_outputs: bfloat16 [2, 2, 16, 512, 768], P('section', None, 'dp')
- input_grads: bfloat16 [2, 2, 16, 512, 768], P('section', None, 'dp')
- weight_in_grad: float32 [2, 5376, 768], P('section', 'dp')
- weight_out_grad: float32 [2, 3840, 768], P('section', 'dp')
- scales_grad: float32 [2, 896], P('section', 'dp')
- statistics: float32 [2, 3], P('section')
The draws below stay inside these ranges and needn't reach their ends.
Inputs may be any that keep to these rules, and one draw needn't show every extreme that they name: lengths[m, s] = (a, b): the first image takes slots [0, a), the second [a, a + b), a >= 1 and a + b <= 512; every micro-batch has a buffer holding one image of 512 tokens and an empty second.
All inputs are finite; a program needn't handle non-finite values.
Results may differ from the reference program's by a relative error of at most 0.017.
Values may be sent and summed in bfloat16 or wider, within the bound.
No kernel may reach another device: no remote copies, remote signals or barrier semaphores. Data moves between devices by JAX's collectives and lax.ppermute only.
A program may use at most 256 MiB of HBM per device.

```python
import math
import jax
import jax.numpy as jnp
from jax import lax

D = 768
FF = 3072
HEADS = 12
HEAD = 64
LAYERS = 2
MICRO = 2
LEN = 512
SEQS = 16


def draw_inputs(key, part):
    key = jax.random.fold_in(key, 11)
    array_shape = (MICRO, SEQS, LEN, D)
    position_ramp = jnp.arange(SEQS, dtype=jnp.float32) / max(SEQS - 1, 1)
    entries = jnp.clip(jax.random.normal(key, array_shape, jnp.float32), -4.0, 4.0)
    factor = 0.6 + 1.2 * position_ramp
    return (entries * factor[None, :, None, None]).astype(jnp.bfloat16)


def draw_lengths(key, part):
    key = jax.random.fold_in(key, 23)
    key_list = jax.random.split(key, 4)
    array_shape = (MICRO, SEQS)
    first_length = jax.random.randint(key_list[0], array_shape, LEN // 4, LEN // 2 + 1)
    second = jax.random.randint(key_list[1], array_shape, LEN // 4, LEN // 2 + 1)
    single = jax.random.randint(key_list[2], array_shape, 0, 4) == 0
    chosen = jax.random.randint(key_list[3], (MICRO, 1), 0, SEQS)
    single = jnp.logical_or(single, jnp.arange(SEQS)[None, :] == chosen)
    first_length = jnp.where(single, LEN, first_length)
    second = jnp.where(single, 0, second)
    return jnp.stack([first_length, second], axis=-1).astype(jnp.int32)


def draw_weight_out(key, part):
    key = jax.random.fold_in(key, 37)
    array_shape = (LAYERS, D + FF, D)
    row_index = jnp.arange(D + FF)
    spread = jnp.where(row_index < D, math.sqrt(LEN / (4.0 * D)), 1.5 / math.sqrt(FF)).astype(jnp.float32)
    entries = jnp.clip(jax.random.normal(key, array_shape, jnp.float32), -4.0, 4.0)
    return (entries * spread[None, :, None]).astype(jnp.bfloat16)


def block_levels(stream_key, dims, cuts, least, high):
    factor_of = 1.0
    for axis_at, blocks in cuts:
        draws = jax.random.uniform(jax.random.fold_in(jax.random.fold_in(stream_key, 6), axis_at), (blocks,), jnp.float32, least / len(cuts), high / len(cuts))
        factor_of = factor_of * jnp.repeat(jnp.exp(draws), dims[axis_at] // blocks).reshape((-1,) + (1,) * (len(dims) - 1 - axis_at))
    return factor_of


def scatter_about(rng, dims, scale, limit, cuts=(), kind=jnp.bfloat16):
    array = scale * jax.random.normal(rng, dims, jnp.float32)
    if cuts:
        array = array * block_levels(rng, dims, cuts, -0.22, 0.18)
    return jnp.clip(array, -limit, limit).astype(kind)


def setup_inputs(seed: int = 0) -> dict:
    keys = jax.random.split(jax.random.key(seed), 7)
    return {
        "inputs": draw_inputs(jax.random.fold_in(keys[6], 71), 0),
        "cotangent": scatter_about(keys[1], (MICRO, SEQS, LEN, D), 1.0, 6.0, ((1, 16),)),
        "lengths": draw_lengths(jax.random.fold_in(keys[6], 71), 0),
        "weight_in": scatter_about(keys[3], (LAYERS, 3 * D + FF, D), D ** -0.5, 0.21875, ((0, 2), (1, 16))),
        "weight_out": draw_weight_out(jax.random.fold_in(keys[6], 71), 0),
        "scales": jnp.clip(1.0 + 0.18 * jax.random.normal(keys[5], (LAYERS, D + 2 * HEAD), jnp.float32), 0.099609375, 1.8984375).astype(jnp.bfloat16),
    }


@jax.custom_vjp
def low(v):
    return lax.optimization_barrier(v.astype(jnp.bfloat16)).astype(jnp.float32)

@jax.custom_vjp
def low_back(v):
    return v

def low_keep(v):
    return (low(v), None)

def low_pass(kept, grad):
    return (grad,)

def back_keep(v):
    return (v, None)

def back_low(kept, grad):
    return (low(grad),)
low.defvjp(low_keep, low_pass)
low_back.defvjp(back_keep, back_low)
EPSILON = 1e-06
MASKED = -1e+30

def normalize(values, scale_vector):
    average = lax.optimization_barrier(jnp.mean(values, axis=-1, keepdims=True))
    centred = values - average
    inverse = lax.rsqrt(lax.optimization_barrier(jnp.mean(centred * centred, axis=-1, keepdims=True)) + EPSILON)
    return centred * inverse * scale_vector

def attend(pieces):
    queries, keys_low, values_low, segment = pieces
    scores = jnp.einsum('qhd,khd->hqk', queries, keys_low, precision=lax.Precision.HIGHEST) * HEAD ** (-0.5)
    scores = low_back(scores)
    allowed = segment[:, None] == segment[None, :]
    scores = jnp.where(allowed[None, :, :], scores, MASKED)
    probabilities = low(jax.nn.softmax(scores, axis=-1))
    return jnp.einsum('hqk,khd->qhd', probabilities, values_low, precision=lax.Precision.HIGHEST)

def layer(row_values, layer_weight_in, layer_weight_out, scale_values, segment, valid_rows):
    group_size = row_values.shape[0]
    gain_vector = scale_values[:D]
    query_scale = scale_values[D:D + HEAD]
    key_scale = scale_values[D + HEAD:]
    normed = low(normalize(row_values, gain_vector))
    projected = low_back(jnp.einsum('gtd,fd->gtf', normed, layer_weight_in, precision=lax.Precision.HIGHEST))
    split_shape = (group_size, LEN, HEADS, HEAD)
    queries = low(normalize(projected[..., :D].reshape(split_shape), query_scale))
    keys_low = low(normalize(projected[..., D:2 * D].reshape(split_shape), key_scale))
    values_low = low(projected[..., 2 * D:3 * D].reshape(split_shape))
    hidden = jax.nn.gelu(projected[..., 3 * D:], approximate=False)
    attended = lax.map(jax.checkpoint(attend), (queries, keys_low, values_low, segment))
    joined = low_back(low(jnp.concatenate([attended.reshape(group_size, LEN, D), hidden], axis=-1)))
    attend_branch = jnp.einsum('gtf,fd->gtd', joined[..., :D], layer_weight_out[:D], precision=lax.Precision.HIGHEST)
    feed_branch = jnp.einsum('gtf,fd->gtd', joined[..., D:], layer_weight_out[D:], precision=lax.Precision.HIGHEST)
    result = row_values + attend_branch + feed_branch
    row_mask = valid_rows[..., None]
    square_sums = jnp.stack([jnp.sum(result * result * row_mask), jnp.sum(attend_branch * attend_branch * row_mask), jnp.sum(feed_branch * feed_branch * row_mask)])
    return (result, square_sums)

def forward(first_in, pad_zero, weights_in, weights_out, scale_sets, block_segment, block_valid):
    first_out, first_sums = layer(first_in, weights_in[0], weights_out[0], scale_sets[0], block_segment, block_valid)
    first_low = low(first_out)
    sent = low_back(first_low) + pad_zero
    second_out, second_sums = layer(sent, weights_in[1], weights_out[1], scale_sets[1], block_segment, block_valid)
    return (second_out, (first_low, jnp.stack([first_sums, second_sums])))

def reference(inputs, cotangent, lengths, weight_in, weight_out, scales):
    seq_total = MICRO * SEQS
    group_size = math.gcd(seq_total, max(1, 4096 // LEN))
    group_count = seq_total // group_size
    position = jnp.arange(LEN, dtype=jnp.int32)
    length_pairs = lengths.reshape(seq_total, 2).astype(jnp.int32)
    first_end = length_pairs[:, 0:1]
    second_end = first_end + length_pairs[:, 1:2]
    segment = (position[None, :] >= first_end).astype(jnp.int32) + (position[None, :] >= second_end).astype(jnp.int32)
    valid_rows = (segment < 2).astype(jnp.float32)
    params = (weight_in.astype(jnp.float32), weight_out.astype(jnp.float32), scales.astype(jnp.float32))

    def one_group(running, pieces):
        block_in, block_cot, block_segment, block_valid = pieces

        def closed(first_in, pad_zero, weights_in, weights_out, scale_sets):
            return forward(first_in, pad_zero, weights_in, weights_out, scale_sets, block_segment, block_valid)
        pad_zero = jnp.zeros(block_in.shape, jnp.float32)
        final_out, pullback, extras = jax.vjp(closed, block_in.astype(jnp.float32), pad_zero, params[0], params[1], params[2], has_aux=True)
        gradients = pullback(block_cot.astype(jnp.float32) * block_valid[..., None])
        first_low, square_sums = extras
        updated = (running[0] + gradients[2], running[1] + gradients[3], running[2] + gradients[4], running[3] + square_sums)
        results = (first_low.astype(jnp.bfloat16), final_out.astype(jnp.bfloat16), gradients[0].astype(jnp.bfloat16), gradients[1].astype(jnp.bfloat16))
        return (updated, results)
    start_state = (jnp.zeros(params[0].shape, jnp.float32), jnp.zeros(params[1].shape, jnp.float32), jnp.zeros(params[2].shape, jnp.float32), jnp.zeros((LAYERS, 3), jnp.float32))
    blocks = (inputs.reshape(group_count, group_size, LEN, D), cotangent.reshape(group_count, group_size, LEN, D), segment.reshape(group_count, group_size, LEN), valid_rows.reshape(group_count, group_size, LEN))
    running, results = lax.scan(one_group, start_state, blocks)
    whole_shape = (MICRO, SEQS, LEN, D)
    layer_outputs = jnp.stack([results[0].reshape(whole_shape), results[1].reshape(whole_shape)])
    input_grads = jnp.stack([results[2].reshape(whole_shape), results[3].reshape(whole_shape)])
    token_count = jnp.sum(valid_rows) * D
    statistics = jnp.sqrt(running[3] / token_count)
    return (layer_outputs, input_grads, running[0], running[1], running[2], statistics)
```

```python
import jax
import jax.numpy as jnp
from jax import lax
from jax.sharding import Mesh, PartitionSpec as P

HEADS = 12
HEAD = 64
EPSILON = 1e-06
MASKED = -1e30
F32 = jnp.float32
BF16 = jnp.bfloat16
DP = ("z", "y", "x")
ALL = ("section",) + DP


def normalize(values, scale_vector):
    average = jnp.mean(values, axis=-1, keepdims=True)
    centred = values - average
    inverse = lax.rsqrt(jnp.mean(centred * centred, axis=-1, keepdims=True) + EPSILON)
    return centred * inverse * scale_vector


def gelu(values):
    return jax.nn.gelu(values, approximate=False)


def dot(left, right, contract):
    return lax.dot_general(left, right, (contract, ((), ())), preferred_element_type=F32)


def forward(rows_in, allowed, weight_in, weight_out, scales):
    length, width = rows_in.shape
    rows = rows_in.astype(F32)
    gain, query_scale, key_scale = scales[:width], scales[width : width + HEAD], scales[width + HEAD :]
    normed = normalize(rows, gain).astype(BF16)
    projected = dot(normed, weight_in, ((1,), (1,)))
    heads = lambda v: v.reshape(length, HEADS, HEAD)
    query_raw, key_raw = heads(projected[:, :width]), heads(projected[:, width : 2 * width])
    value = heads(projected[:, 2 * width : 3 * width]).astype(BF16)
    feed = projected[:, 3 * width :]
    query = normalize(query_raw, query_scale).astype(BF16)
    key = normalize(key_raw, key_scale).astype(BF16)
    scores = jnp.einsum("qhd,khd->hqk", query, key, preferred_element_type=F32) * HEAD**-0.5
    probs = jax.nn.softmax(jnp.where(allowed[None], scores, MASKED), axis=-1)
    attended = jnp.einsum("hqk,khd->qhd", probs.astype(BF16), value, preferred_element_type=F32)
    joined = jnp.concatenate([attended.reshape(length, width), gelu(feed)], axis=1).astype(BF16)
    attend_branch = dot(joined[:, :width], weight_out[:width], ((1,), (0,)))
    feed_branch = dot(joined[:, width:], weight_out[width:], ((1,), (0,)))
    result = rows + attend_branch + feed_branch
    kept = (rows, gain, query_scale, key_scale, normed, query_raw, key_raw, query, key, value, feed, probs, joined)
    return result, attend_branch, feed_branch, kept


def backward(grad, kept, weight_in, weight_out):
    rows, gain, query_scale, key_scale, normed, query_raw, key_raw, query, key, value, feed, probs, joined = kept
    length, width = rows.shape
    grad_joined = dot(grad, weight_out, ((1,), (1,))).astype(BF16)
    grad_attended = grad_joined[:, :width].reshape(length, HEADS, HEAD)
    grad_feed = jax.vjp(gelu, feed)[1](grad_joined[:, width:].astype(F32))[0]
    grad_probs = jnp.einsum("qhd,khd->hqk", grad_attended, value, preferred_element_type=F32)
    grad_value = jnp.einsum("hqk,qhd->khd", probs.astype(BF16), grad_attended, preferred_element_type=F32)
    delta = jnp.sum(probs * grad_probs, axis=-1, keepdims=True)
    grad_scores = (probs * (grad_probs - delta)).astype(BF16)
    grad_query = jnp.einsum("hqk,khd->qhd", grad_scores, key, preferred_element_type=F32) * HEAD**-0.5
    grad_key = jnp.einsum("hqk,qhd->khd", grad_scores, query, preferred_element_type=F32) * HEAD**-0.5
    query_back, query_scale_back = jax.vjp(normalize, query_raw, query_scale)[1](grad_query)
    key_back, key_scale_back = jax.vjp(normalize, key_raw, key_scale)[1](grad_key)
    flat = lambda v: v.reshape(length, width)
    grad_projected = jnp.concatenate(
        [flat(query_back), flat(key_back), flat(grad_value), grad_feed], axis=1
    ).astype(BF16)
    grad_normed = dot(grad_projected, weight_in, ((1,), (0,)))
    grad_rows, grad_gain = jax.vjp(normalize, rows, gain)[1](grad_normed)
    grad_in = (grad.astype(F32) + grad_rows).astype(BF16)
    weight_in_grad = dot(grad_projected, normed, ((0,), (0,))).astype(BF16)
    weight_out_grad = dot(joined, grad, ((0,), (0,))).astype(BF16)
    return grad_in, weight_in_grad, weight_out_grad, jnp.concatenate([grad_gain, query_scale_back, key_scale_back])


def body(inputs, cotangent, lengths, weight_in, weight_out, scales):
    length, width = inputs.shape[2], inputs.shape[3]
    core = lax.axis_index("section")
    rows_first = lax.dynamic_index_in_dim(inputs, core, 0, False)[0]
    grad_last = lax.dynamic_index_in_dim(cotangent, core, 0, False)[0]
    pair = lax.dynamic_index_in_dim(lengths, core, 0, False)[0]
    position = lax.broadcasted_iota(jnp.int32, (length, 1), 0)
    segment = (position >= pair[0]).astype(jnp.int32) + (position >= pair[0] + pair[1]).astype(jnp.int32)
    allowed = segment == segment.reshape(1, length)
    valid = (segment < 2).astype(F32)
    gather = lambda v: lax.all_gather(v[0], ALL, axis=0, tiled=True).reshape((2, -1) + v.shape[2:])
    weight_in_all, weight_out_all = gather(weight_in), gather(weight_out)
    scales_all = gather(scales).astype(F32)
    outputs, kept, sums = [], [], []
    rows = rows_first
    for layer in range(2):
        result, attend, feed, keep = forward(rows, allowed, weight_in_all[layer], weight_out_all[layer], scales_all[layer])
        rows = result.astype(BF16)
        outputs.append(rows)
        kept.append(keep)
        sums.append(jnp.stack([jnp.sum(v * v * valid) for v in (result, attend, feed)]))
    grad = (grad_last.astype(F32) * valid).astype(BF16)
    grads, in_grads, out_grads, scale_grads = [None] * 2, [None] * 2, [None] * 2, [None] * 2
    for layer in (1, 0):
        grad, in_grads[layer], out_grads[layer], scale_grads[layer] = backward(
            grad, kept[layer], weight_in_all[layer], weight_out_all[layer]
        )
        grads[layer] = grad
    scatter = lambda pieces: lax.psum_scatter(
        jnp.concatenate(pieces, axis=0), ALL, scatter_dimension=0, tiled=True
    ).astype(F32)[None]
    small = jnp.concatenate([jnp.stack(sums).reshape(-1), jnp.sum(pair).astype(F32)[None]])
    for axis in ALL:
        small = lax.psum(small, axis)
    statistics = jnp.sqrt(lax.dynamic_slice(small, (3 * core,), (3,)) / (small[6] * width))
    def spread(pieces):
        mine = jnp.where(core == 0, pieces[0], pieces[1])
        other = jnp.where(core == 0, pieces[1], pieces[0])
        other = lax.ppermute(other, "section", [(0, 1), (1, 0)])
        return jnp.stack([jnp.where(core == 0, mine, other), jnp.where(core == 0, other, mine)])[None, :, None]
    return (
        spread(outputs),
        spread(grads),
        scatter(in_grads),
        scatter(out_grads),
        scatter(scale_grads),
        statistics[None],
    )


def solution(mesh):
    count = mesh.shape["dp"]
    fine = Mesh(mesh.devices.reshape(2, count // 4, 2, 2), ALL)
    return jax.shard_map(
        body,
        mesh=fine,
        in_specs=(
            P(None, DP, None, None),
            P(None, DP, None, None),
            P(None, DP, None),
            P("section", DP, None),
            P("section", DP, None),
            P("section", DP),
        ),
        out_specs=(
            P("section", None, DP, None, None),
            P("section", None, DP, None, None),
            P("section", DP, None),
            P("section", DP, None),
            P("section", DP),
            P("section", None),
        ),
        check_vma=False,
    )
```

```python
import functools

import jax
import jax.numpy as jnp
from jax import lax
from jax.experimental import pallas as pl
from jax.experimental.pallas import tpu as pltpu
from jax.sharding import Mesh, PartitionSpec as P

HEADS = 12
HEAD = 64
GROUP = 4
GROUPS = HEADS // GROUP
LANES = GROUP * HEAD
EPSILON = 1e-06
MASKED = -1e30
FACTOR = HEAD**-0.5
F32 = jnp.float32
BF16 = jnp.bfloat16
DP = ("z", "y", "x")
ALL = ("section",) + DP
VMEM_MIB = 56
ANY = pl.BlockSpec(memory_space=pl.ANY)
VMEM = pl.BlockSpec(memory_space=pltpu.VMEM)


def nn(left, right):
    return lax.dot_general(left, right, (((1,), (0,)), ((), ())), preferred_element_type=F32)


def nt(left, right):
    return lax.dot_general(left, right, (((1,), (1,)), ((), ())), preferred_element_type=F32)


def tn(left, right):
    return lax.dot_general(left, right, (((0,), (0,)), ((), ())), preferred_element_type=F32)


def launch(kernel, values, *, name, micros, grid=(), in_specs, out_specs, out_shape, scratch=()):
    return pl.pallas_call(
        kernel,
        grid=grid,
        in_specs=in_specs,
        out_specs=out_specs,
        out_shape=out_shape,
        scratch_shapes=scratch,
        cost_estimate=pl.CostEstimate(flops=int(micros * 1150000000.0), bytes_accessed=int(micros * 1000000.0), transcendentals=0),
        compiler_params=pltpu.CompilerParams(
            vmem_limit_bytes=VMEM_MIB * 1024 * 1024, dimension_semantics=("arbitrary",) * len(grid)
        ),
        name=name,
    )(*values)


def array(shape, dtype=BF16):
    return jax.ShapeDtypeStruct(shape, dtype)


def row_norm(rows):
    average = jnp.mean(rows, axis=1, keepdims=True)
    centred = rows - average
    inverse = lax.rsqrt(jnp.mean(centred * centred, axis=1, keepdims=True) + EPSILON)
    return centred * inverse, inverse


def column_norm(columns):
    average = jnp.mean(columns, axis=0, keepdims=True)
    centred = columns - average
    inverse = lax.rsqrt(jnp.mean(centred * centred, axis=0, keepdims=True) + EPSILON)
    return centred * inverse, inverse


def norm_back(normal, inverse, grad, scale, axis):
    scaled = grad * scale
    average = jnp.mean(scaled, axis=axis, keepdims=True)
    along_normal = jnp.mean(scaled * normal, axis=axis, keepdims=True)
    return inverse * (scaled - average - normal * along_normal)


def segment_at(pair_ref, position):
    first_end = pair_ref[0, 0]
    second_end = first_end + pair_ref[0, 1]
    return (position >= first_end).astype(jnp.int32) + (position >= second_end).astype(jnp.int32)


def fill_bias(pair_ref, bias_ref):
    length = bias_ref.shape[0]
    down = segment_at(pair_ref, lax.broadcasted_iota(jnp.int32, (length, length), 0))
    sideways = segment_at(pair_ref, lax.broadcasted_iota(jnp.int32, (length, length), 1))
    bias_ref[...] = jnp.where(down == sideways, 0.0, MASKED).astype(F32)


def whole(*shape):
    return pl.BlockSpec(shape, lambda *_: (0,) * len(shape))


def attend_kernel(
    pair_ref, rows_ref, gain_ref, query_scale_ref, key_scale_ref, weight_ref,
    normed_ref, raw_ref, value_ref, attended_ref, log_ref, bias_ref,
):
    @pl.when(pl.program_id(0) == 0)
    def _():
        normal, _ = row_norm(rows_ref[...].astype(F32))
        normed_ref[...] = (normal * gain_ref[...]).astype(BF16)
        fill_bias(pair_ref, bias_ref)

    normed = normed_ref[...]
    width = normed.shape[1]
    projected = nt(weight_ref[...].reshape(3 * LANES, width), normed)
    raw_ref[...] = projected[: 2 * LANES].reshape(raw_ref.shape)
    value_ref[...] = projected[2 * LANES :].astype(BF16)
    for head in range(GROUP):
        at = slice(head * HEAD, (head + 1) * HEAD)
        query = column_norm(projected[:LANES][at])[0] * query_scale_ref[...]
        query = query.astype(BF16) * BF16(FACTOR)
        key = (column_norm(projected[LANES : 2 * LANES][at])[0] * key_scale_ref[...]).astype(BF16)
        scores = tn(key, query) + bias_ref[...]
        peak = jnp.max(scores, axis=0, keepdims=True)
        exponent = jnp.exp(scores - peak)
        total = jnp.sum(exponent, axis=0, keepdims=True)
        attended = nn(value_ref[at, :], exponent.astype(BF16)) * (1.0 / total)
        attended_ref[at, :] = attended.astype(BF16)
        log_ref[0, head : head + 1, :] = peak + jnp.log(total)


def attend(layer, pair, rows, gain, query_scale, key_scale, weight_in):
    length, width = rows.shape
    return launch(
        attend_kernel,
        (pair, rows, gain, query_scale, key_scale, weight_in.reshape(2, -1, GROUPS, LANES, width)),
        name="attend",
        micros=12,
        grid=(GROUPS,),
        in_specs=[
            pl.BlockSpec(memory_space=pltpu.SMEM),
            whole(length, width),
            whole(1, width),
            whole(HEAD, 1),
            whole(HEAD, 1),
            pl.BlockSpec((1, 3, 1, LANES, width), lambda g: (layer, 0, g, 0, 0)),
        ],
        out_specs=[
            whole(length, width),
            pl.BlockSpec((2, 1, LANES, length), lambda g: (0, g, 0, 0)),
            pl.BlockSpec((LANES, length), lambda g: (g, 0)),
            pl.BlockSpec((LANES, length), lambda g: (g, 0)),
            pl.BlockSpec((1, 8, length), lambda g: (g, 0, 0)),
        ],
        out_shape=[
            array((length, width)),
            array((2, GROUPS, LANES, length), F32),
            array((width, length)),
            array((width, length)),
            array((GROUPS, 8, length), F32),
        ],
        scratch=[pltpu.VMEM((length, length), F32)],
    )


def hidden_kernel(normed_ref, weight_ref, hidden_ref, slope_ref):
    feed = nt(weight_ref[...], normed_ref[...])
    half = 0.5 * lax.erf(feed * (0.5**0.5)) + 0.5
    hidden_ref[...] = (feed * half).astype(BF16)
    density = jnp.exp(feed * feed * -0.5) * ((2.0 * jnp.pi) ** -0.5)
    slope_ref[...] = (half + feed * density).astype(BF16)


def hidden(layer, normed, weight_in):
    length, width = normed.shape
    blocks = weight_in.shape[0] // width // 2
    first, count = layer * blocks + 3, blocks - 3
    return launch(
        hidden_kernel,
        (normed, weight_in),
        name="hidden",
        micros=8,
        grid=(count,),
        in_specs=[whole(length, width), pl.BlockSpec((width, width), lambda i: (i + first, 0))],
        out_specs=[pl.BlockSpec((width, length), lambda i: (i, 0))] * 2,
        out_shape=[array((count * width, length))] * 2,
    )


def output_kernel(pair_ref, rows_ref, attended_ref, hidden_ref, weight_ref, result_ref, sums_ref, attend_ref, feed_ref):
    step = pl.program_id(0)

    @pl.when(step == 0)
    def _():
        attend_ref[...] = tn(attended_ref[...], weight_ref[...])

    @pl.when(step == 1)
    def _():
        feed_ref[...] = tn(hidden_ref[...], weight_ref[...])

    @pl.when(step > 1)
    def _():
        feed_ref[...] += tn(hidden_ref[...], weight_ref[...])

    @pl.when(step == pl.num_programs(0) - 1)
    def _():
        length, width = attend_ref.shape
        position = lax.broadcasted_iota(jnp.int32, (length, 1), 0)
        valid = (segment_at(pair_ref, position) < 2).astype(F32)
        branch, feed = attend_ref[...], feed_ref[...]
        result = rows_ref[...].astype(F32) + branch + feed
        result_ref[...] = result.astype(BF16)
        for at, value in enumerate((result, branch, feed)):
            squares = (value * value * valid).reshape(length // 8, 8, width)
            sums_ref[at] = jnp.sum(squares, axis=0)


def output(pair, rows, attended, hid, weight):
    length, width = rows.shape
    count = weight.shape[0] // width
    return launch(
        output_kernel,
        (pair, rows, attended, hid, weight),
        name="output",
        micros=9,
        grid=(count,),
        in_specs=[
            pl.BlockSpec(memory_space=pltpu.SMEM),
            whole(length, width),
            whole(width, length),
            pl.BlockSpec((width, length), lambda i: (jnp.maximum(i - 1, 0), 0)),
            pl.BlockSpec((width, width), lambda i: (i, 0)),
        ],
        out_specs=[whole(length, width), whole(3, 8, width)],
        out_shape=[array((length, width)), array((3, 8, width), F32)],
        scratch=[pltpu.VMEM((length, width), F32)] * 2,
    )


def feed_back_kernel(grad_ref, slope_ref, weight_in_ref, weight_out_ref, grad_normed_ref, grad_feed_ref):
    step = pl.program_id(0)
    grad_hidden = nt(weight_out_ref[...], grad_ref[...]).astype(BF16).astype(F32)
    grad_feed = (grad_hidden * slope_ref[...].astype(F32)).astype(BF16)
    grad_feed_ref[...] = grad_feed
    part = tn(grad_feed, weight_in_ref[...])

    @pl.when(step == 0)
    def _():
        grad_normed_ref[...] = part

    @pl.when(step > 0)
    def _():
        grad_normed_ref[...] += part


def feed_back(layer, grad, slope, weight_in, weight_out):
    length, width = grad.shape
    count = slope.shape[0] // width
    first = layer * (weight_in.shape[0] // width // 2) + 3
    rows = pl.BlockSpec((width, length), lambda i: (i, 0))
    return launch(
        feed_back_kernel,
        (grad, slope, weight_in, weight_out),
        name="feed_back",
        micros=11,
        grid=(count,),
        in_specs=[
            whole(length, width),
            rows,
            pl.BlockSpec((width, width), lambda i: (i + first, 0)),
            pl.BlockSpec((width, width), lambda i: (i + 1, 0)),
        ],
        out_specs=[whole(length, width), rows],
        out_shape=[array((length, width), F32), array(slope.shape)],
    )


def attend_back_kernel(
    pair_ref, rows_ref, grad_ref, gain_ref, query_scale_ref, key_scale_ref, raw_ref, value_ref,
    attended_ref, log_ref, weight_out_ref, weight_in_ref, feed_grad_ref,
    projected_ref, grad_in_ref, gain_grad_ref, scale_grad_ref, bias_ref, grad_normed_ref,
):
    step = pl.program_id(0)

    @pl.when(step == 0)
    def _():
        fill_bias(pair_ref, bias_ref)
        grad_normed_ref[...] = feed_grad_ref[...]
        scale_grad_ref[...] = jnp.zeros_like(scale_grad_ref)

    length, width = grad_ref.shape
    query_scale, key_scale = query_scale_ref[...], key_scale_ref[...]
    grad_attended = nt(weight_out_ref[0], grad_ref[...]).astype(BF16)
    for head in range(GROUP):
        at = slice(head * HEAD, (head + 1) * HEAD)
        query_normal, query_inverse = column_norm(raw_ref[0, 0, at, :])
        key_normal, key_inverse = column_norm(raw_ref[1, 0, at, :])
        query = (query_normal * query_scale).astype(BF16) * BF16(FACTOR)
        key = (key_normal * key_scale).astype(BF16)
        value = value_ref[at, :]
        probs = jnp.exp(tn(key, query) + bias_ref[...] - log_ref[0, head : head + 1, :])
        grad_out = grad_attended[at]
        grad_probs = tn(value, grad_out)
        grad_value = nt(grad_out, probs.astype(BF16))
        delta = jnp.sum(grad_out.astype(F32) * attended_ref[at, :].astype(F32), axis=0, keepdims=True)
        grad_scores = (probs * (grad_probs - delta)).astype(BF16)
        grad_query = nn(key, grad_scores) * FACTOR
        grad_key = nt(query, grad_scores)
        for place_at, term in enumerate((grad_query * query_normal, grad_key * key_normal)):
            for lane in range(0, length, 128):
                scale_grad_ref[place_at] += term[:, lane : lane + 128]
        projected_ref[0, 0, at, :] = norm_back(query_normal, query_inverse, grad_query, query_scale, 0).astype(BF16)
        projected_ref[1, 0, at, :] = norm_back(key_normal, key_inverse, grad_key, key_scale, 0).astype(BF16)
        projected_ref[2, 0, at, :] = grad_value.astype(BF16)
    projected = projected_ref[...].reshape(3 * LANES, length)
    grad_normed_ref[...] += tn(projected, weight_in_ref[...].reshape(3 * LANES, width))

    @pl.when(step == pl.num_programs(0) - 1)
    def _():
        normal, inverse = row_norm(rows_ref[...].astype(F32))
        grad_normed = grad_normed_ref[...]
        grad_rows = norm_back(normal, inverse, grad_normed, gain_ref[...], 1)
        grad_in_ref[...] = (grad_ref[...].astype(F32) + grad_rows).astype(BF16)
        gain_grad_ref[...] = jnp.sum((grad_normed * normal).reshape(length // 8, 8, width), axis=0)


def attend_back(layer, pair, rows, grad, gain, query_scale, key_scale, raw, value, attended, logs, weight_out,
                weight_in, feed_grad):
    length, width = grad.shape
    group_rows = pl.BlockSpec((LANES, length), lambda g: (g, 0))
    projected, *others = launch(
        attend_back_kernel,
        (pair, rows, grad, gain, query_scale, key_scale, raw, value, attended, logs,
         weight_out.reshape(-1, LANES, width), weight_in.reshape(2, -1, GROUPS, LANES, width), feed_grad),
        name="attend_back",
        micros=17,
        grid=(GROUPS,),
        in_specs=[
            pl.BlockSpec(memory_space=pltpu.SMEM),
            whole(length, width),
            whole(length, width),
            whole(1, width),
            whole(HEAD, 1),
            whole(HEAD, 1),
            pl.BlockSpec((2, 1, LANES, length), lambda g: (0, g, 0, 0)),
            group_rows,
            group_rows,
            pl.BlockSpec((1, 8, length), lambda g: (g, 0, 0)),
            pl.BlockSpec((1, LANES, width), lambda g: (g, 0, 0)),
            pl.BlockSpec((1, 3, 1, LANES, width), lambda g: (layer, 0, g, 0, 0)),
            whole(length, width),
        ],
        out_specs=[
            pl.BlockSpec((3, 1, LANES, length), lambda g: (0, g, 0, 0)),
            whole(length, width),
            whole(8, width),
            whole(2, HEAD, 128),
        ],
        out_shape=[
            array((3, GROUPS, LANES, length)),
            array((length, width)),
            array((8, width), F32),
            array((2, HEAD, 128), F32),
        ],
        scratch=[pltpu.VMEM((length, length), F32), pltpu.VMEM((length, width), F32)],
    )
    return projected.reshape(3 * width, length), *others


def sends(fine, first, second):
    _, depth, high, wide = fine
    number = lambda c, z, y, x: ((c * depth + z) * high + y) * wide + x
    return [
        (number(c, z, y, x), number(c, *(first, second)[c](z, y, x)))
        for c in range(2)
        for z in range(depth)
        for y in range(high)
        for x in range(wide)
    ]


def next_x(z, y, x):
    return z, y, 1 - x


def next_y(z, y, x):
    return z, 1 - y, x


def sideways(value, fine):
    return lax.ppermute(value, ALL, sends(fine, next_x, next_y))


def turned(value, fine):
    return lax.ppermute(value, ALL, sends(fine, next_y, next_x))


def along(value, fine):
    depth = fine[1]
    return lax.ppermute(
        value, ALL, sends(fine, lambda z, y, x: ((z + 1) % depth, y, x), lambda z, y, x: ((z - 1) % depth, y, x))
    )


def opposite(value, fine):
    depth = fine[1]
    return lax.ppermute(value, "z", [(z, (z + 2) % depth) for z in range(depth)])


def swap(value):
    return lax.ppermute(value, "section", [(0, 1), (1, 0)])


def place():
    return [lax.axis_index(axis) for axis in ALL]


def either(condition, make_first, make_second):
    @pl.when(condition)
    def _():
        make_first().start()

    @pl.when(jnp.logical_not(condition))
    def _():
        make_second().start()


def slot_copy(slot, keep_ref, pass_ref, owner, target, sem, rows=None):
    index = slot % 2 if isinstance(slot, int) else lax.rem(slot, 2)
    view = (lambda ref: ref.at[index]) if rows is None else (lambda ref: ref.at[index, rows])
    kept = pltpu.make_async_copy(view(keep_ref), target, sem)
    either(slot // 2 == owner, lambda: kept, lambda: pltpu.make_async_copy(view(pass_ref), target, sem))
    return kept


def half_of(rows):
    return -(-rows // 32) * 16


def pick_kernel(layer, own_ref, other_ref, *refs):
    extra, (shard_ref, half_ref, sem) = refs[:-3], refs[-3:]
    core = lax.axis_index("section")
    count, rows, half = own_ref.shape[0], shard_ref.shape[0], half_ref.shape[0]
    goal = shard_ref.at[pl.ds(0, count)]
    copy = pltpu.make_async_copy(own_ref, goal, sem)
    either(core == layer, lambda: copy, lambda: pltpu.make_async_copy(other_ref, goal, sem))
    if extra:
        shard_ref[count:] = extra[0][...]
    copy.wait()

    @pl.when(core == 0)
    def _():
        half_ref[...] = shard_ref[:half]

    @pl.when(core == 1)
    def _():
        half_ref[...] = shard_ref[rows - half :]


def pick(layer, own, other, *extra):
    rows, width = own.shape[0] + sum(value.shape[0] for value in extra), own.shape[1]
    return launch(
        functools.partial(pick_kernel, layer), (own, other, *extra), name="pick", micros=1.5,
        in_specs=[ANY] * 2 + [VMEM] * len(extra), out_specs=[VMEM] * 2,
        out_shape=[array((rows, width)), array((half_of(rows), width))],
        scratch=[pltpu.SemaphoreType.DMA],
    )


def line_kernel(own_ref, near_ref, other_ref, far_ref, far_other_ref, keep_ref, pass_ref, line_ref, sems):
    core, z = lax.axis_index("section"), lax.axis_index("z")
    depth = line_ref.shape[0]
    half = far_ref.shape[0]
    below, above, far = lax.rem(z + depth - 1, depth), lax.rem(z + 1, depth), lax.rem(z + 2, depth)
    near_at, other_at = jnp.where(core == 0, below, above), jnp.where(core == 0, above, below)
    rest = own_ref.shape[0] - half
    first, second = pl.multiple_of(core * rest, 16), pl.multiple_of((1 - core) * half, 16)
    skipped = pl.multiple_of((1 - core) * (half - rest), 16)
    copies = [
        pltpu.make_async_copy(own_ref, line_ref.at[z], sems.at[0]),
        pltpu.make_async_copy(near_ref, line_ref.at[near_at], sems.at[1]),
        pltpu.make_async_copy(other_ref, line_ref.at[other_at], sems.at[2]),
        pltpu.make_async_copy(far_ref, line_ref.at[far, pl.ds(first, half)], sems.at[3]),
        pltpu.make_async_copy(far_other_ref.at[pl.ds(skipped, rest)], line_ref.at[far, pl.ds(second, rest)], sems.at[4]),
    ]
    for copy in copies:
        copy.start()
    for copy in copies:
        copy.wait()
    keep_ref[...] = line_ref[pl.ds(2 * core, 2)]
    pass_ref[...] = line_ref[pl.ds(2 - 2 * core, 2)]


def line_of(own, near, near_other, far, far_other):
    rows, width = own.shape
    return launch(
        line_kernel, (own, near, near_other, far, far_other), name="line", micros=2.5,
        in_specs=[ANY] * 5, out_specs=[VMEM] * 2, out_shape=[array((2, rows, width))] * 2,
        scratch=[pltpu.VMEM((4, rows, width), BF16), pltpu.SemaphoreType.DMA((5,))],
    )


def place_kernel(
    line_keep, line_pass, side_keep, side_pass, turn_keep, turn_pass, corner, corner_other, full_ref, sems
):
    core, y, x = lax.axis_index("section"), lax.axis_index("y"), lax.axis_index("x")
    at = pl.program_id(0)
    take = pl.ds(line_keep.shape[1] - full_ref.shape[3], full_ref.shape[3])
    side_y, side_x = jnp.where(core == 0, y, 1 - y), jnp.where(core == 0, 1 - x, x)
    copies = [
        slot_copy(at, line_keep, line_pass, core, full_ref.at[0, y, x], sems.at[0], take),
        slot_copy(at, side_keep, side_pass, core, full_ref.at[0, side_y, side_x], sems.at[1], take),
        slot_copy(at, turn_keep, turn_pass, 1 - core, full_ref.at[0, 1 - side_y, 1 - side_x], sems.at[2], take),
        slot_copy(at, corner_other, corner, core, full_ref.at[0, 1 - y, 1 - x], sems.at[3], take),
    ]
    for copy in copies:
        copy.wait()


def placed(pieces, fine, rows):
    width = pieces[0].shape[-1]
    full = launch(
        place_kernel, pieces, name="place", micros=5, grid=(fine[1],),
        in_specs=[ANY] * 8,
        out_specs=pl.BlockSpec((1, *fine[2:], rows, width), lambda i: (i, 0, 0, 0, 0)),
        out_shape=array((*fine[1:], rows, width)),
        scratch=[pltpu.SemaphoreType.DMA((4,))],
    )
    return full.reshape(-1, width)


def rows_copy(low_ref, high_ref, start, count, target_ref, at, sem, crossing):
    split = low_ref.shape[0]
    goal = target_ref.at[pl.ds(at, count)]
    copy = pltpu.make_async_copy(low_ref.at[pl.ds(0, count)], goal, sem)

    @pl.when(start + count <= split)
    def _():
        pltpu.make_async_copy(low_ref.at[pl.ds(pl.multiple_of(start, 16), count)], goal, sem).start()

    @pl.when(start >= split)
    def _():
        pltpu.make_async_copy(high_ref.at[pl.ds(pl.multiple_of(start - split, 16), count)], goal, sem).start()

    for first in crossing:
        if first < split < first + count:
            low = split - first

            @pl.when(start == first)
            def _():
                pltpu.make_async_copy(low_ref.at[pl.ds(first, low)], target_ref.at[pl.ds(at, low)], sem).start()
                rest = target_ref.at[pl.ds(at + low, count - low)]
                pltpu.make_async_copy(high_ref.at[pl.ds(0, count - low)], rest, sem).start()

    return copy


def partial_kernel(
    fine, own_low, own_high, other_low, other_high, right_ref, right_other_ref,
    turn_ref, keep_ref, pass_ref, near_ref, half_ref, left_ref, sems,
):
    core, z, y, x = place()
    depth, high, wide = fine[1:]
    split = own_low.shape[0]
    rows = keep_ref.shape[1]
    half = half_ref.shape[1]
    step = pl.program_id(0)
    side_y, side_x = jnp.where(core == 0, y, 1 - y), jnp.where(core == 0, 1 - x, x)
    near, far = lax.rem(z + jnp.where(core == 0, 1, depth - 1), depth), lax.rem(z + 2, depth)
    whole_at = (split // rows) * rows
    crossing = (whole_at, whole_at + rows - half)

    def row(slot, line_y, line_x):
        return ((slot * high + line_y) * wide + line_x) * rows

    kept, passed = 2 * core, 2 - 2 * core
    parts = [(row(passed + at, 1 - y, 1 - x), rows) for at in range(2)]
    parts += [(row(kept + at, side_y, side_x), rows) for at in range(2)]
    parts += [(row(passed + at, side_y, side_x), rows) for at in range(2)]
    parts += [(row(near, y, x), rows)]
    parts += [(row(slot, y, x) + core * (rows - half), half) for slot in (z, far)]
    sides = ((own_low, own_high), (other_low, other_high))

    def copies():
        at = 0
        for index, (start, count) in enumerate(parts):
            for side, (low, up) in enumerate(sides):
                yield index, low, up, start, count, left_ref.at[side], at, sems.at[side, index]
            at += count

    @pl.when(step == 0)
    def _():
        for _, *what in copies():
            rows_copy(*what, crossing)

    def wait(indices):
        for index, low, _, _, count, target, at, sem in copies():
            if index in indices:
                pltpu.make_async_copy(low.at[pl.ds(0, count)], target.at[pl.ds(at, count)], sem).wait()

    def product(first, count):
        own = nn(left_ref[0, first : first + count], right_ref[...])
        return (own + nn(left_ref[1, first : first + count], right_other_ref[...])).astype(BF16)

    for at, out in enumerate((turn_ref, keep_ref, pass_ref)):

        @pl.when(step == at)
        def _():
            wait((2 * at, 2 * at + 1))
            out[...] = product(2 * at * rows, 2 * rows).reshape(out.shape)

    @pl.when(step == 3)
    def _():
        wait((6, 7, 8))
        last = product(6 * rows, rows + 2 * half)
        near_ref[...] = last[:rows]
        half_ref[...] = last[rows:].reshape(half_ref.shape)


def partial(fine, own_low, own_high, other_low, other_high, right, right_other):
    length, width = right.shape
    features = own_low.shape[0] + own_high.shape[0]
    rows = features // (fine[1] * fine[2] * fine[3])
    half = half_of(rows)
    shapes = [(2, rows, width)] * 3 + [(rows, width), (2, half, width)]
    return launch(
        functools.partial(partial_kernel, fine), (own_low, own_high, other_low, other_high, right, right_other),
        name="partial", micros=features / 700, grid=(4,),
        in_specs=[ANY] * 4 + [whole(length, width)] * 2,
        out_specs=[whole(*shape) for shape in shapes],
        out_shape=[array(shape) for shape in shapes],
        scratch=[pltpu.VMEM((2, 7 * rows + 2 * half, length), BF16), pltpu.SemaphoreType.DMA((2, 9))],
    )


def depth_kernel(
    near_ref, half_ref, keep_ref, pass_ref, keep_other, pass_other,
    near_out, far_out, own_out, near_got, half_got, sems,
):
    core, z = lax.axis_index("section"), lax.axis_index("z")
    depth = 4
    half = half_ref.shape[1]
    near = lax.rem(z + jnp.where(core == 0, 1, depth - 1), depth)
    part = pl.ds(pl.multiple_of(core * (near_ref.shape[0] - half), 16), half)
    copies = []
    for at, (keep, pass_, owner) in enumerate(((keep_ref, pass_ref, core), (keep_other, pass_other, 1 - core))):
        copies.append(slot_copy(near, keep, pass_, owner, near_got.at[at], sems.at[3 * at]))
        for index, slot in enumerate((z, lax.rem(z + 2, depth))):
            copies.append(slot_copy(slot, keep, pass_, owner, half_got.at[at, index], sems.at[3 * at + 1 + index], part))
    for copy in copies:
        copy.wait()
    near_total = near_ref[...].astype(F32) + near_got[0].astype(F32) + near_got[1].astype(F32)
    near_out[...] = near_total.astype(BF16)
    for index, out in enumerate((own_out, far_out)):
        total = half_ref[index].astype(F32) + half_got[0, index].astype(F32) + half_got[1, index].astype(F32)
        out[...] = total.astype(BF16)


def depth_sums(near, halves, keep, passed, keep_other, passed_other):
    rows, width = near.shape
    half = halves.shape[1]
    return launch(
        depth_kernel, (near, halves, keep, passed, keep_other, passed_other), name="depth", micros=2,
        in_specs=[VMEM] * 2 + [ANY] * 4, out_specs=[VMEM] * 3,
        out_shape=[array((rows, width)), array((half, width)), array((half, width))],
        scratch=[
            pltpu.VMEM((2, rows, width), BF16),
            pltpu.VMEM((2, 2, half, width), BF16),
            pltpu.SemaphoreType.DMA((6,)),
        ],
    )


def total_kernel(near_ref, near_other, far_ref, far_other, own_ref, own_other, *refs):
    second, out_ref = refs[:-1], refs[-1]
    core = lax.axis_index("section")
    rows, half = near_ref.shape[0], far_ref.shape[0]
    near = near_ref[...].astype(F32) + near_other[...].astype(F32)
    mine = far_ref[...].astype(F32) + own_ref[...].astype(F32)
    other = far_other[...].astype(F32) + own_other[...].astype(F32)
    low, high = jnp.where(core == 0, mine, other), jnp.where(core == 0, other, mine)
    out_ref[:half] = near[:half] + low
    out_ref[half:] = near[half:] + high[2 * half - rows :]
    if second:

        @pl.when(core == 1)
        def _():
            out_ref[...] = second[0][...]


def total(near, near_other, far, far_other, own, own_other, *second):
    values = (near, near_other, far, far_other, own, own_other, *second)
    return launch(
        total_kernel, values, name="total", micros=1.5,
        in_specs=[VMEM] * len(values), out_specs=VMEM, out_shape=array(near.shape, F32),
    )


class Order:
    def __init__(self, first):
        self.last = first
        self.moving = []

    def run(self, function, *values):
        values, _ = lax.optimization_barrier((values, self.last))
        return self.fence(function(*values))

    def fence(self, *result):
        due = [value for value, left in self.moving if left == 0]
        self.moving = [(value, left - 1) for value, left in self.moving if left > 0]
        result, self.last, _ = lax.optimization_barrier((result, self.last, due))
        if result:
            self.last = jax.tree.leaves(result)[0]
            return result[0]

    def move(self, way, *values, count=1):
        values, _ = lax.optimization_barrier((values, self.last))
        moved = [way(value) for value in values]
        self.moving += [(value, count - 1) for value in moved]
        return moved if len(values) > 1 else moved[0]

    def swap(self, *values, count=1):
        return self.move(swap, *values, count=count)


def total_along(value, axis, size):
    return sum([lax.ppermute(value, axis, [(i, (i + k) % size) for i in range(size)]) for k in range(1, size)], value)


def total_of(value, fine):
    for axis, size in zip(ALL, fine):
        value = total_along(value, axis, size) if size < 8 else lax.psum(value, axis)
    return value


def added(first, second):
    return (first.astype(F32) + second.astype(F32)).astype(BF16)


class Gather:
    def __init__(self, order, fine, shard, half):
        self.order, self.fine, self.shard, self.half = order, fine, shard, half

    def along(self):
        self.near = self.order.move(functools.partial(along, fine=self.fine), self.shard)
        self.far = self.order.move(functools.partial(opposite, fine=self.fine), self.half)

    def across(self):
        self.near_other, self.far_other = self.order.swap(self.near, self.far)

    def line(self):
        self.keep, self.passed = self.order.run(
            line_of, self.shard, self.near, self.near_other, self.far, self.far_other
        )

    def side(self):
        self.side_passed = self.order.move(functools.partial(sideways, fine=self.fine), self.passed)
        self.side_keep = self.order.move(functools.partial(sideways, fine=self.fine), self.keep)

    def turn(self):
        self.corner = self.order.move(functools.partial(turned, fine=self.fine), self.side_passed)
        self.turn_keep, self.turn_passed = self.order.swap(self.side_keep, self.side_passed)

    def meet(self):
        self.corner_other = self.order.swap(self.corner)

    def place(self):
        pieces = (
            self.keep, self.passed, self.side_keep, self.side_passed, self.turn_keep, self.turn_passed,
            self.corner, self.corner_other,
        )
        return self.order.run(lambda *values: placed(values, self.fine, self.shard.shape[0]), *pieces)


class Scatter:
    def __init__(self, order, fine, values):
        self.order, self.fine = order, fine
        self.turn, self.keep, self.passed, self.near, self.halves = values

    def start(self):
        self.turn = self.order.move(functools.partial(turned, fine=self.fine), self.turn)
        self.keep = self.order.move(functools.partial(sideways, fine=self.fine), self.keep)

    def add(self):
        self.passed = self.order.run(added, self.passed, self.turn)

    def pass_on(self):
        self.passed = self.order.move(functools.partial(sideways, fine=self.fine), self.passed)
        self.keep_other = self.order.swap(self.keep)

    def meet(self):
        self.passed_other = self.order.swap(self.passed)

    def parts(self):
        return self.near, self.halves, self.keep, self.passed, self.keep_other, self.passed_other

    def along(self, values, count=1):
        near, far, self.own = values
        self.near = self.order.move(functools.partial(along, fine=self.fine), near, count=count)
        self.far = self.order.move(functools.partial(opposite, fine=self.fine), far, count=count)
        self.own_other = self.order.swap(self.own)

    def across(self):
        self.near_other, self.far_other = self.order.swap(self.near, self.far)

    def ends(self):
        return self.near, self.near_other, self.far, self.far_other, self.own, self.own_other


def body(fine, inputs, cotangent, lengths, weight_in, weight_out, scales):
    length, width = inputs.shape[2], inputs.shape[3]
    core, z, y, x = place()
    depth = fine[1]
    device = (z * fine[2] + y) * fine[3] + x
    pair = lax.dynamic_index_in_dim(lengths, core, 0, False)
    scale_count = scales.shape[1]
    whole_scales = scale_count * depth * fine[2] * fine[3]
    by_core = lambda first, second: (jnp.where(core == 0, first, second), jnp.where(core == 0, second, first))

    shift = lambda axis: lambda value: lax.ppermute(value, axis, [(0, 1), (1, 0)])
    spread = lambda mine, other: jnp.stack(by_core(mine, other))[None, :, None]
    chip = functools.partial(partial, fine)

    weight_in_all = lax.all_gather(weight_in[0], ALL, axis=0, tiled=True)

    def padded(flat):
        return jnp.pad(flat, (0, -flat.shape[0] % 1024)).reshape(-1, 128)

    own_scales = lax.dynamic_update_slice(
        jnp.zeros((2 * whole_scales,), F32), scales[0].astype(F32), (core * whole_scales + device * scale_count,)
    )
    scale = total_of(padded(own_scales), fine).reshape(-1)[: 2 * whole_scales].reshape(2, whole_scales)
    vectors_0, vectors_1 = [(s[None, :width], s[width : width + HEAD, None], s[width + HEAD :, None]) for s in scale]
    rows_0 = lax.dynamic_index_in_dim(inputs, core, 0, False)[0]
    grad = lax.dynamic_index_in_dim(cotangent, core, 0, False)[0]
    position = lax.broadcasted_iota(jnp.int32, (length, 1), 0)
    grad_1 = jnp.where(position < pair[0, 0] + pair[0, 1], grad, jnp.zeros_like(grad))

    order = Order(grad_1)
    if depth == 4:
        other_out = order.swap(weight_out[0])
        grad_1_other = order.swap(grad_1)
        order.fence()
        first = Gather(order, fine, *order.run(functools.partial(pick, 0), weight_out[0], other_out))
        first.along()
        second = Gather(order, fine, *order.run(functools.partial(pick, 1), weight_out[0], other_out))
        first.across()
        order.fence()
        first.line()
        first.side()
        second.along()
        order.fence()
        first.turn()
        second.across()
        order.fence()
        first.meet()
        second.line()
        second.side()
        weight_out_0 = first.place()
        second.turn()
        order.fence()
        second.meet()
        order.fence()
        weight_out_1 = second.place()
    else:
        weight_out_0, weight_out_1 = jnp.split(lax.all_gather(weight_out[0], ALL, axis=0, tiled=True), 2)
    out = functools.partial(output, pair)
    normed_0, raw_0, value_0, attended_0, logs_0 = order.run(
        functools.partial(attend, 0, pair), rows_0, *vectors_0, weight_in_all
    )
    attended_0_other, normed_0_other = order.swap(attended_0, normed_0)
    hidden_0, slope_0 = order.run(functools.partial(hidden, 0), normed_0, weight_in_all)
    hidden_0_other = order.swap(hidden_0)
    rows_1, squares_0 = order.run(out, rows_0, attended_0, hidden_0, weight_out_0)
    normed_1, raw_1, value_1, attended_1, logs_1 = order.run(
        functools.partial(attend, 1, pair), rows_1, *vectors_1, weight_in_all
    )
    attended_1_other, normed_1_other = order.swap(attended_1, normed_1)
    hidden_1, slope_1 = order.run(functools.partial(hidden, 1), normed_1, weight_in_all)
    back_1, back_0 = functools.partial(attend_back, 1, pair), functools.partial(attend_back, 0, pair)
    kept_1 = (rows_1, grad_1, *vectors_1, raw_1, value_1, attended_1, logs_1, weight_out_1, weight_in_all)

    def small_sums(squares_0, squares_1, gain_0, heads_0, gain_1, heads_1):
        sums = [jnp.sum(squares, axis=(1, 2)) for squares in (squares_0, squares_1)]
        scale_grads = [
            jnp.concatenate([jnp.sum(gain, axis=0), jnp.sum(heads, axis=2).reshape(-1)])
            for gain, heads in ((gain_0, heads_0), (gain_1, heads_1))
        ]
        return padded(jnp.concatenate([jnp.sum(pair).astype(F32)[None], *sums, *scale_grads]))

    if depth == 4:
        hidden_1_other = order.swap(hidden_1)
        feed_1, low_1 = order.run(functools.partial(feed_back, 1), grad_1, slope_1, weight_in_all, weight_out_1)
        low_1_other = order.swap(low_1)
        out_1 = Scatter(order, fine, order.run(
            chip, attended_1, hidden_1, attended_1_other, hidden_1_other, grad_1, grad_1_other
        ))
        out_1.start()
        top_1, grad_0, gain_1, heads_1 = order.run(back_1, *kept_1, feed_1)
        grad_0_other, top_1_other = order.swap(grad_0, top_1, count=2)
        out_1.add()
        out_1.pass_on()
        feed_0, low_0 = order.run(functools.partial(feed_back, 0), grad_0, slope_0, weight_in_all, weight_out_0)
        low_0_other = order.swap(low_0)
        out_1.meet()
        out_0 = Scatter(order, fine, order.run(
            chip, attended_0, hidden_0, attended_0_other, hidden_0_other, grad_0, grad_0_other
        ))
        out_0.start()
        in_1, ends = order.run(
            lambda values, parts: (chip(*values), depth_sums(*parts)),
            (top_1, low_1, top_1_other, low_1_other, normed_1, normed_1_other), out_1.parts(),
        )
        in_1 = Scatter(order, fine, in_1)
        out_0.add()
        out_0.pass_on()
        in_1.start()
        out_1.along(ends)
        kept_0 = (rows_0, grad_0, *vectors_0, raw_0, value_0, attended_0, logs_0, weight_out_0, weight_in_all)
        (top_0, grad_first, gain_0, heads_0), (result_1, squares_1) = order.run(
            lambda kept, late: (back_0(*kept), out(*late)), (*kept_0, feed_0), (rows_1, attended_1, hidden_1, weight_out_1)
        )
        top_0_other = order.swap(top_0, count=2)
        in_1.add()
        in_1.pass_on()
        out_0.meet()
        out_1.across()
        small, (rows_kept, rows_given), (grads_kept, grads_given) = order.run(
            lambda *values: (small_sums(*values[:6]), by_core(*values[6:8]), by_core(*values[8:])),
            squares_0, squares_1, gain_0, heads_0, gain_1, heads_1, rows_1, result_1, grad_first, grad_0,
        )
        in_1.meet()
        in_0, ends = order.run(
            lambda values, parts: (chip(*values), depth_sums(*parts)),
            (top_0, low_0, top_0_other, low_0_other, normed_0, normed_0_other), out_0.parts(),
        )
        in_0 = Scatter(order, fine, in_0)
        in_0.start()
        out_0.along(ends)
        small_other = order.move(shift("x"), small)
        rows_got, grads_got = order.swap(rows_given, grads_given)
        ends, out_grad_1 = order.run(
            lambda parts, sums: (depth_sums(*parts), total(*sums)), in_1.parts(), out_1.ends()
        )
        small = small + small_other
        small_other = order.move(shift("y"), small)
        in_0.add()
        in_0.pass_on()
        in_1.along(ends, count=2)
        out_0.across()
        outputs, input_grads = order.run(lambda *v: (spread(*v[:2]), spread(*v[2:])), rows_kept, rows_got, grads_kept, grads_got)
        in_0.meet()
        out_grad = order.run(total, *out_0.ends(), out_grad_1)
        ends = order.run(depth_sums, *in_0.parts())
        in_0.along(ends)
        in_1.across()
        small = small + small_other
        ring = [
            order.move(lambda v, k=k: lax.ppermute(v, "z", [(i, (i + k) % depth) for i in range(depth)]), small)
            for k in range(1, depth)
        ]
        order.fence()
        in_0.across()
        small = sum(ring, small)
        small_other = order.swap(small)
        in_grad_1 = order.run(total, *in_1.ends())
        in_grad = order.run(total, *in_0.ends(), in_grad_1)[None]
        out_grad = out_grad[None]
        small = small + small_other
    else:
        feed_1, low_1 = order.run(functools.partial(feed_back, 1), grad_1, slope_1, weight_in_all, weight_out_1)
        top_1, grad_0, gain_1, heads_1 = order.run(back_1, *kept_1, feed_1)
        feed_0, low_0 = order.run(functools.partial(feed_back, 0), grad_0, slope_0, weight_in_all, weight_out_0)
        kept_0 = (rows_0, grad_0, *vectors_0, raw_0, value_0, attended_0, logs_0, weight_out_0, weight_in_all)
        top_0, grad_first, gain_0, heads_0 = order.run(back_0, *kept_0, feed_0)
        result_1, squares_1 = order.run(out, rows_1, attended_1, hidden_1, weight_out_1)
        own = lambda low, high, right: nn(jnp.concatenate([low, high]), right).astype(BF16)
        summed = lambda first, second: lax.psum_scatter(
            jnp.concatenate([first, second]), ALL, scatter_dimension=0, tiled=True
        ).astype(F32)[None]
        in_grad = summed(own(top_0, low_0, normed_0), own(top_1, low_1, normed_1))
        out_grad = summed(own(attended_0, hidden_0, grad_0), own(attended_1, hidden_1, grad_1))
        small = small_sums(squares_0, squares_1, gain_0, heads_0, gain_1, heads_1)
        for axis in ALL:
            small = lax.psum(small, axis)
        outputs, input_grads = [
            spread(mine, swap(given)) for mine, given in (by_core(rows_1, result_1), by_core(grad_first, grad_0))
        ]
    small = small.reshape(-1)
    statistics = jnp.sqrt(lax.dynamic_slice(small, (1 + 3 * core,), (3,)) / (small[0] * width))
    scale_grad = lax.dynamic_slice(small, (7 + core * whole_scales + device * scale_count,), (scale_count,))
    return outputs, input_grads, in_grad, out_grad, scale_grad[None], statistics[None]


def solution(mesh):
    count = mesh.shape["dp"]
    fine = Mesh(mesh.devices.reshape(2, count // 4, 2, 2), ALL)
    return jax.shard_map(
        functools.partial(body, (2, count // 4, 2, 2)),
        mesh=fine,
        in_specs=(
            P(None, DP, None, None),
            P(None, DP, None, None),
            P(None, DP, None),
            P("section", DP, None),
            P("section", DP, None),
            P("section", DP),
        ),
        out_specs=(
            P("section", None, DP, None, None),
            P("section", None, DP, None, None),
            P("section", DP, None),
            P("section", DP, None),
            P("section", DP),
            P("section", None),
        ),
        check_vma=False,
    )
```

```python
import functools

import jax
import jax.numpy as jnp
from jax import lax
from jax.experimental import pallas as pl
from jax.experimental.pallas import tpu as pltpu
from jax.sharding import Mesh, PartitionSpec as P

HEADS = 12
HEAD = 64
GROUP = 4
GROUPS = HEADS // GROUP
LANES = GROUP * HEAD
EPSILON = 1e-06
MASKED = -1e30
FACTOR = HEAD**-0.5
F32 = jnp.float32
BF16 = jnp.bfloat16
DP = ("z", "y", "x")
ALL = ("section",) + DP
VMEM_MIB = 56
ANY = pl.BlockSpec(memory_space=pl.ANY)
VMEM = pl.BlockSpec(memory_space=pltpu.VMEM)


def nn(left, right):
    return lax.dot_general(left, right, (((1,), (0,)), ((), ())), preferred_element_type=F32)


def nt(left, right):
    return lax.dot_general(left, right, (((1,), (1,)), ((), ())), preferred_element_type=F32)


def tn(left, right):
    return lax.dot_general(left, right, (((0,), (0,)), ((), ())), preferred_element_type=F32)


def launch(kernel, values, *, name, micros, grid=(), in_specs, out_specs, out_shape, scratch=()):
    return pl.pallas_call(
        kernel,
        grid=grid,
        in_specs=in_specs,
        out_specs=out_specs,
        out_shape=out_shape,
        scratch_shapes=scratch,
        cost_estimate=pl.CostEstimate(flops=int(micros * 1150000000.0), bytes_accessed=int(micros * 1000000.0), transcendentals=0),
        compiler_params=pltpu.CompilerParams(
            vmem_limit_bytes=VMEM_MIB * 1024 * 1024, dimension_semantics=("arbitrary",) * len(grid)
        ),
        name=name,
    )(*values)


def array(shape, dtype=BF16):
    return jax.ShapeDtypeStruct(shape, dtype)


def row_norm(rows):
    average = jnp.mean(rows, axis=1, keepdims=True)
    centred = rows - average
    inverse = lax.rsqrt(jnp.mean(centred * centred, axis=1, keepdims=True) + EPSILON)
    return centred * inverse, inverse


def column_norm(columns):
    average = jnp.mean(columns, axis=0, keepdims=True)
    centred = columns - average
    inverse = lax.rsqrt(jnp.mean(centred * centred, axis=0, keepdims=True) + EPSILON)
    return centred * inverse, inverse


def norm_back(normal, inverse, grad, scale, axis):
    scaled = grad * scale
    average = jnp.mean(scaled, axis=axis, keepdims=True)
    along_normal = jnp.mean(scaled * normal, axis=axis, keepdims=True)
    return inverse * (scaled - average - normal * along_normal)


def segment_at(pair_ref, position):
    first_end = pair_ref[0, 0]
    second_end = first_end + pair_ref[0, 1]
    return (position >= first_end).astype(jnp.int32) + (position >= second_end).astype(jnp.int32)


def fill_bias(pair_ref, bias_ref):
    length = bias_ref.shape[0]
    down = segment_at(pair_ref, lax.broadcasted_iota(jnp.int32, (length, length), 0))
    sideways = segment_at(pair_ref, lax.broadcasted_iota(jnp.int32, (length, length), 1))
    bias_ref[...] = jnp.where(down == sideways, 0.0, MASKED).astype(F32)


def whole(*shape):
    return pl.BlockSpec(shape, lambda *_: (0,) * len(shape))


def attend_kernel(in_rows, pair_ref, rows_ref, gain_ref, query_scale_ref, key_scale_ref, *refs):
    step = pl.program_id(0)
    if in_rows is None:
        weight_ref, normed_ref, raw_ref, value_ref, attended_ref, log_ref, bias_ref = refs
        weight = weight_ref[...].reshape(3 * LANES, rows_ref.shape[1])
    else:
        pieces, refs = refs[:8], refs[8:]
        normed_ref, raw_ref, value_ref, attended_ref, log_ref, full_ref, bias_ref, weight_ref, sems, full_sems = refs
        load_weight(step, pieces, weight_ref, sems, in_rows, full_ref, full_sems, (0, 0, 1, 1))
        starts = [pl.multiple_of(rows_ref.shape[1] * third + LANES * step, LANES) for third in range(3)]
        weight = jnp.concatenate([weight_ref[pl.ds(start, LANES)] for start in starts])

    @pl.when(step == 0)
    def _():
        normal, _ = row_norm(rows_ref[...].astype(F32))
        normed_ref[...] = (normal * gain_ref[...]).astype(BF16)
        fill_bias(pair_ref, bias_ref)

    normed = normed_ref[...]
    projected = nt(weight, normed)
    raw_ref[...] = projected[: 2 * LANES].reshape(raw_ref.shape)
    value_ref[...] = projected[2 * LANES :].astype(BF16)
    for head in range(GROUP):
        at = slice(head * HEAD, (head + 1) * HEAD)
        query = column_norm(projected[:LANES][at])[0] * query_scale_ref[...]
        query = query.astype(BF16) * BF16(FACTOR)
        key = (column_norm(projected[LANES : 2 * LANES][at])[0] * key_scale_ref[...]).astype(BF16)
        scores = tn(key, query) + bias_ref[...]
        peak = jnp.max(scores, axis=0, keepdims=True)
        exponent = jnp.exp(scores - peak)
        total = jnp.sum(exponent, axis=0, keepdims=True)
        attended = nn(value_ref[at, :], exponent.astype(BF16)) * (1.0 / total)
        attended_ref[at, :] = attended.astype(BF16)
        log_ref[0, head : head + 1, :] = peak + jnp.log(total)


def attend(in_rows, pair, rows, gain, query_scale, key_scale, *weights):
    length, width = rows.shape
    gathered = in_rows is not None
    features = 16 * in_rows if gathered else weights[0].shape[0]
    if not gathered:
        weights = (weights[0].reshape(-1, GROUPS, LANES, width),)
    return launch(
        functools.partial(attend_kernel, in_rows),
        (pair, rows, gain, query_scale, key_scale, *weights),
        name="attend",
        micros=13,
        grid=(GROUPS,),
        in_specs=[
            pl.BlockSpec(memory_space=pltpu.SMEM),
            whole(length, width),
            whole(1, width),
            whole(HEAD, 1),
            whole(HEAD, 1),
            *([ANY] * 8 if gathered else [pl.BlockSpec((3, 1, LANES, width), lambda g: (0, g, 0, 0))]),
        ],
        out_specs=[
            whole(length, width),
            pl.BlockSpec((2, 1, LANES, length), lambda g: (0, g, 0, 0)),
            pl.BlockSpec((LANES, length), lambda g: (g, 0)),
            pl.BlockSpec((LANES, length), lambda g: (g, 0)),
            pl.BlockSpec((1, 8, length), lambda g: (g, 0, 0)),
            *[ANY] * gathered,
        ],
        out_shape=[
            array((length, width)),
            array((2, GROUPS, LANES, length), F32),
            array((width, length)),
            array((width, length)),
            array((GROUPS, 8, length), F32),
            *[array((features, width))] * gathered,
        ],
        scratch=[
            pltpu.VMEM((length, length), F32),
            *(weight_scratch(features, width) if gathered else ()),
        ],
    )


def hidden_kernel(normed_ref, weight_ref, hidden_ref, slope_ref):
    feed = nt(weight_ref[...], normed_ref[...])
    half = 0.5 * lax.erf(feed * (0.5**0.5)) + 0.5
    hidden_ref[...] = (feed * half).astype(BF16)
    density = jnp.exp(feed * feed * -0.5) * ((2.0 * jnp.pi) ** -0.5)
    slope_ref[...] = (half + feed * density).astype(BF16)


def hidden(normed, weight_in):
    length, width = normed.shape
    count = weight_in.shape[0] // width - 3
    return launch(
        hidden_kernel,
        (normed, weight_in),
        name="hidden",
        micros=8,
        grid=(count,),
        in_specs=[whole(length, width), pl.BlockSpec((width, width), lambda i: (i + 3, 0))],
        out_specs=[pl.BlockSpec((width, length), lambda i: (i, 0))] * 2,
        out_shape=[array((count * width, length))] * 2,
    )


def load_weight(step, pieces, target, sems, rows, full_ref, full_sems, steps):
    @pl.when(step == 0)
    def _():
        piece_copies(pieces, target, sems, rows)

    size = 4 * rows
    out = [
        pltpu.make_async_copy(target.at[pl.ds(size * slot, size)], full_ref.at[pl.ds(size * slot, size)], full_sems.at[slot])
        for slot in range(4)
    ]
    for slot in range(4):

        @pl.when(step == steps[slot])
        def _():
            for at in range(4):
                goal = target.at[pl.ds(size * slot + rows * at, rows)]
                pltpu.make_async_copy(pieces[0].at[0, pl.ds(0, rows)], goal, sems.at[4 * slot + at]).wait()
            out[slot].start()

    @pl.when(step == pl.num_programs(0) - 1)
    def _():
        for copy in out:
            copy.wait()


def output_kernel(out_rows, pair_ref, rows_ref, attended_ref, hidden_ref, *refs):
    step, last = pl.program_id(0), pl.num_programs(0) - 1
    width = rows_ref.shape[1]
    if out_rows is None:
        weight_ref, result_ref, sums_ref, attend_ref, feed_ref = refs
        weight = weight_ref[...]
    else:
        pieces, (result_ref, sums_ref, full_ref, attend_ref, feed_ref, all_ref, sems, full_sems) = refs[:8], refs[8:]
        load_weight(step, pieces, all_ref, sems, out_rows, full_ref, full_sems, (0, 1, 2, 3))
        weight = all_ref[pl.ds(pl.multiple_of(step * width, width), width)]

    @pl.when(step == 0)
    def _():
        attend_ref[...] = tn(attended_ref[...], weight)

    @pl.when(step == 1)
    def _():
        feed_ref[...] = tn(hidden_ref[...], weight)

    @pl.when(step > 1)
    def _():
        feed_ref[...] += tn(hidden_ref[...], weight)

    @pl.when(step == last)
    def _():
        length = attend_ref.shape[0]
        position = lax.broadcasted_iota(jnp.int32, (length, 1), 0)
        valid = (segment_at(pair_ref, position) < 2).astype(F32)
        branch, feed = attend_ref[...], feed_ref[...]
        result = rows_ref[...].astype(F32) + branch + feed
        result_ref[...] = result.astype(BF16)
        for at, value in enumerate((result, branch, feed)):
            squares = (value * value * valid).reshape(length // 8, 8, width)
            sums_ref[at] = jnp.sum(squares, axis=0)


def weight_scratch(features, width):
    return [pltpu.VMEM((features, width), BF16), pltpu.SemaphoreType.DMA((16,)), pltpu.SemaphoreType.DMA((4,))]


def output(pair, out_rows, rows, attended, hid, *weights):
    length, width = rows.shape
    features = hid.shape[0] + width
    count = features // width
    gathered = out_rows is not None
    return launch(
        functools.partial(output_kernel, out_rows),
        (pair, rows, attended, hid, *weights),
        name="output",
        micros=9,
        grid=(count,),
        in_specs=[
            pl.BlockSpec(memory_space=pltpu.SMEM),
            whole(length, width),
            whole(width, length),
            pl.BlockSpec((width, length), lambda i: (jnp.maximum(i - 1, 0), 0)),
            *([ANY] * 8 if gathered else [pl.BlockSpec((width, width), lambda i: (i, 0))]),
        ],
        out_specs=[whole(length, width), whole(3, 8, width), *[ANY] * gathered],
        out_shape=[array((length, width)), array((3, 8, width), F32), *[array((features, width))] * gathered],
        scratch=[
            *[pltpu.VMEM((length, width), F32)] * 2,
            *(weight_scratch(features, width) if gathered else ()),
        ],
    )


def feed_back_kernel(out_rows, grad_ref, slope_ref, weight_in_ref, *refs):
    step = pl.program_id(0)
    width = grad_ref.shape[1]
    if out_rows is None:
        weight_ref, grad_normed_ref, grad_feed_ref = refs
        weight_out = weight_ref[...]
    else:
        pieces, (grad_normed_ref, grad_feed_ref, full_ref, all_ref, sems, full_sems) = refs[:8], refs[8:]
        load_weight(step, pieces, all_ref, sems, out_rows, full_ref, full_sems, (0, 0, 1, 2))
        weight_out = all_ref[pl.ds(pl.multiple_of((step + 1) * width, width), width)]
    grad_hidden = nt(weight_out, grad_ref[...]).astype(BF16).astype(F32)
    grad_feed = (grad_hidden * slope_ref[...].astype(F32)).astype(BF16)
    grad_feed_ref[...] = grad_feed
    part = tn(grad_feed, weight_in_ref[...])

    @pl.when(step == 0)
    def _():
        grad_normed_ref[...] = part

    @pl.when(step > 0)
    def _():
        grad_normed_ref[...] += part


def feed_back(out_rows, grad, slope, weight_in, *weights):
    length, width = grad.shape
    features = slope.shape[0] + width
    count = slope.shape[0] // width
    gathered = out_rows is not None
    rows = pl.BlockSpec((width, length), lambda i: (i, 0))
    return launch(
        functools.partial(feed_back_kernel, out_rows),
        (grad, slope, weight_in, *weights),
        name="feed_back",
        micros=11,
        grid=(count,),
        in_specs=[
            whole(length, width),
            rows,
            pl.BlockSpec((width, width), lambda i: (i + 3, 0)),
            *([ANY] * 8 if gathered else [pl.BlockSpec((width, width), lambda i: (i + 1, 0))]),
        ],
        out_specs=[whole(length, width), rows, *[ANY] * gathered],
        out_shape=[array((length, width), F32), array(slope.shape), *[array((features, width))] * gathered],
        scratch=weight_scratch(features, width) if gathered else (),
    )


def attend_back_kernel(
    pair_ref, rows_ref, grad_ref, gain_ref, query_scale_ref, key_scale_ref, raw_ref, value_ref,
    attended_ref, log_ref, weight_out_ref, weight_in_ref, feed_grad_ref,
    projected_ref, grad_in_ref, gain_grad_ref, scale_grad_ref, bias_ref, grad_normed_ref,
):
    step = pl.program_id(0)

    @pl.when(step == 0)
    def _():
        fill_bias(pair_ref, bias_ref)
        grad_normed_ref[...] = feed_grad_ref[...]
        scale_grad_ref[...] = jnp.zeros_like(scale_grad_ref)

    length, width = grad_ref.shape
    query_scale, key_scale = query_scale_ref[...], key_scale_ref[...]
    grad_attended = nt(weight_out_ref[0], grad_ref[...]).astype(BF16)
    for head in range(GROUP):
        at = slice(head * HEAD, (head + 1) * HEAD)
        query_normal, query_inverse = column_norm(raw_ref[0, 0, at, :])
        key_normal, key_inverse = column_norm(raw_ref[1, 0, at, :])
        query = (query_normal * query_scale).astype(BF16) * BF16(FACTOR)
        key = (key_normal * key_scale).astype(BF16)
        value = value_ref[at, :]
        probs = jnp.exp(tn(key, query) + bias_ref[...] - log_ref[0, head : head + 1, :])
        grad_out = grad_attended[at]
        grad_probs = tn(value, grad_out)
        grad_value = nt(grad_out, probs.astype(BF16))
        delta = jnp.sum(grad_out.astype(F32) * attended_ref[at, :].astype(F32), axis=0, keepdims=True)
        grad_scores = (probs * (grad_probs - delta)).astype(BF16)
        grad_query = nn(key, grad_scores) * FACTOR
        grad_key = nt(query, grad_scores)
        for place_at, term in enumerate((grad_query * query_normal, grad_key * key_normal)):
            for lane in range(0, length, 128):
                scale_grad_ref[place_at] += term[:, lane : lane + 128]
        projected_ref[0, 0, at, :] = norm_back(query_normal, query_inverse, grad_query, query_scale, 0).astype(BF16)
        projected_ref[1, 0, at, :] = norm_back(key_normal, key_inverse, grad_key, key_scale, 0).astype(BF16)
        projected_ref[2, 0, at, :] = grad_value.astype(BF16)
    projected = projected_ref[...].reshape(3 * LANES, length)
    grad_normed_ref[...] += tn(projected, weight_in_ref[...].reshape(3 * LANES, width))

    @pl.when(step == pl.num_programs(0) - 1)
    def _():
        normal, inverse = row_norm(rows_ref[...].astype(F32))
        grad_normed = grad_normed_ref[...]
        grad_rows = norm_back(normal, inverse, grad_normed, gain_ref[...], 1)
        grad_in_ref[...] = (grad_ref[...].astype(F32) + grad_rows).astype(BF16)
        gain_grad_ref[...] = jnp.sum((grad_normed * normal).reshape(length // 8, 8, width), axis=0)


def attend_back(pair, rows, grad, gain, query_scale, key_scale, raw, value, attended, logs, weight_out,
                weight_in, feed_grad):
    length, width = grad.shape
    group_rows = pl.BlockSpec((LANES, length), lambda g: (g, 0))
    projected, *others = launch(
        attend_back_kernel,
        (pair, rows, grad, gain, query_scale, key_scale, raw, value, attended, logs,
         weight_out.reshape(-1, LANES, width), weight_in.reshape(-1, GROUPS, LANES, width), feed_grad),
        name="attend_back",
        micros=17,
        grid=(GROUPS,),
        in_specs=[
            pl.BlockSpec(memory_space=pltpu.SMEM),
            whole(length, width),
            whole(length, width),
            whole(1, width),
            whole(HEAD, 1),
            whole(HEAD, 1),
            pl.BlockSpec((2, 1, LANES, length), lambda g: (0, g, 0, 0)),
            group_rows,
            group_rows,
            pl.BlockSpec((1, 8, length), lambda g: (g, 0, 0)),
            pl.BlockSpec((1, LANES, width), lambda g: (g, 0, 0)),
            pl.BlockSpec((3, 1, LANES, width), lambda g: (0, g, 0, 0)),
            whole(length, width),
        ],
        out_specs=[
            pl.BlockSpec((3, 1, LANES, length), lambda g: (0, g, 0, 0)),
            whole(length, width),
            whole(8, width),
            whole(2, HEAD, 128),
        ],
        out_shape=[
            array((3, GROUPS, LANES, length)),
            array((length, width)),
            array((8, width), F32),
            array((2, HEAD, 128), F32),
        ],
        scratch=[pltpu.VMEM((length, length), F32), pltpu.VMEM((length, width), F32)],
    )
    return projected.reshape(3 * width, length), *others


def sends(fine, first, second):
    _, depth, high, wide = fine
    number = lambda c, z, y, x: ((c * depth + z) * high + y) * wide + x
    return [
        (number(c, z, y, x), number(c, *(first, second)[c](z, y, x)))
        for c in range(2)
        for z in range(depth)
        for y in range(high)
        for x in range(wide)
    ]


def next_x(z, y, x):
    return z, y, 1 - x


def next_y(z, y, x):
    return z, 1 - y, x


def sideways(value, fine):
    return lax.ppermute(value, ALL, sends(fine, next_x, next_y))


def turned(value, fine):
    return lax.ppermute(value, ALL, sends(fine, next_y, next_x))


def along(value, fine):
    depth = fine[1]
    return lax.ppermute(
        value, ALL, sends(fine, lambda z, y, x: ((z + 1) % depth, y, x), lambda z, y, x: ((z - 1) % depth, y, x))
    )


def opposite(value, fine):
    depth = fine[1]
    return lax.ppermute(value, "z", [(z, (z + 2) % depth) for z in range(depth)])


def swap(value):
    return lax.ppermute(value, "section", [(0, 1), (1, 0)])


def place():
    return [lax.axis_index(axis) for axis in ALL]


def either(condition, make_first, make_second):
    @pl.when(condition)
    def _():
        make_first().start()

    @pl.when(jnp.logical_not(condition))
    def _():
        make_second().start()


def slot_copy(slot, keep_ref, pass_ref, owner, target, sem, rows=None):
    index = slot % 2 if isinstance(slot, int) else lax.rem(slot, 2)
    view = (lambda ref: ref.at[index]) if rows is None else (lambda ref: ref.at[index, rows])
    kept = pltpu.make_async_copy(view(keep_ref), target, sem)
    either(slot // 2 == owner, lambda: kept, lambda: pltpu.make_async_copy(view(pass_ref), target, sem))
    return kept


def half_of(rows):
    return -(-rows // 32) * 16


def pick_kernel(layer, own_ref, other_ref, *refs):
    extra, (shard_ref, half_ref, sem) = refs[:-3], refs[-3:]
    core = lax.axis_index("section")
    count, rows, half = own_ref.shape[0], shard_ref.shape[0], half_ref.shape[0]
    goal = shard_ref.at[pl.ds(0, count)]
    copy = pltpu.make_async_copy(own_ref, goal, sem)
    either(core == layer, lambda: copy, lambda: pltpu.make_async_copy(other_ref, goal, sem))
    if extra:
        shard_ref[count:] = extra[0][...]
    copy.wait()

    @pl.when(core == 0)
    def _():
        half_ref[...] = shard_ref[:half]

    @pl.when(core == 1)
    def _():
        half_ref[...] = shard_ref[rows - half :]


def pick(layer, own, other, *extra):
    rows, width = own.shape[0] + sum(value.shape[0] for value in extra), own.shape[1]
    return launch(
        functools.partial(pick_kernel, layer), (own, other, *extra), name="pick", micros=1.5,
        in_specs=[ANY] * 2 + [VMEM] * len(extra), out_specs=[VMEM] * 2,
        out_shape=[array((rows, width)), array((half_of(rows), width))],
        scratch=[pltpu.SemaphoreType.DMA],
    )


def line_kernel(own_ref, near_ref, other_ref, far_ref, far_other_ref, keep_ref, pass_ref, line_ref, sems):
    core, z = lax.axis_index("section"), lax.axis_index("z")
    depth = line_ref.shape[0]
    half = far_ref.shape[0]
    below, above, far = lax.rem(z + depth - 1, depth), lax.rem(z + 1, depth), lax.rem(z + 2, depth)
    near_at, other_at = jnp.where(core == 0, below, above), jnp.where(core == 0, above, below)
    rest = own_ref.shape[0] - half
    first, second = pl.multiple_of(core * rest, 16), pl.multiple_of((1 - core) * half, 16)
    skipped = pl.multiple_of((1 - core) * (half - rest), 16)
    copies = [
        pltpu.make_async_copy(own_ref, line_ref.at[z], sems.at[0]),
        pltpu.make_async_copy(near_ref, line_ref.at[near_at], sems.at[1]),
        pltpu.make_async_copy(other_ref, line_ref.at[other_at], sems.at[2]),
        pltpu.make_async_copy(far_ref, line_ref.at[far, pl.ds(first, half)], sems.at[3]),
        pltpu.make_async_copy(far_other_ref.at[pl.ds(skipped, rest)], line_ref.at[far, pl.ds(second, rest)], sems.at[4]),
    ]
    for copy in copies:
        copy.start()
    for copy in copies:
        copy.wait()
    keep_ref[...] = line_ref[pl.ds(2 * core, 2)]
    pass_ref[...] = line_ref[pl.ds(2 - 2 * core, 2)]


def line_of(own, near, near_other, far, far_other):
    rows, width = own.shape
    return launch(
        line_kernel, (own, near, near_other, far, far_other), name="line", micros=2.5,
        in_specs=[ANY] * 5, out_specs=[VMEM] * 2, out_shape=[array((2, rows, width))] * 2,
        scratch=[pltpu.VMEM((4, rows, width), BF16), pltpu.SemaphoreType.DMA((5,))],
    )


def piece_copies(pieces, target, sems, rows):
    line_keep, line_pass, side_keep, side_pass, turn_keep, turn_pass, corner, corner_other = pieces
    core, _, y, x = place()
    high, wide = 2, 2
    take = pl.ds(0, rows)
    side_y, side_x = jnp.where(core == 0, y, 1 - y), jnp.where(core == 0, 1 - x, x)
    copies = []
    for slot in range(4):
        lines = (
            (line_keep, line_pass, core, y, x),
            (side_keep, side_pass, core, side_y, side_x),
            (turn_keep, turn_pass, 1 - core, 1 - side_y, 1 - side_x),
            (corner_other, corner, core, 1 - y, 1 - x),
        )
        for at, (keep, passed, owner, line_y, line_x) in enumerate(lines):
            start = pl.multiple_of(((slot * high + line_y) * wide + line_x) * rows, 8)
            goal = target.at[pl.ds(start, rows)]
            copies.append(slot_copy(slot, keep, passed, owner, goal, sems.at[4 * slot + at], take))
    return copies


def rows_copy(low_ref, high_ref, start, count, target_ref, at, sem, crossing):
    split = low_ref.shape[0]
    goal = target_ref.at[pl.ds(at, count)]
    copy = pltpu.make_async_copy(low_ref.at[pl.ds(0, count)], goal, sem)

    @pl.when(start + count <= split)
    def _():
        pltpu.make_async_copy(low_ref.at[pl.ds(pl.multiple_of(start, 16), count)], goal, sem).start()

    @pl.when(start >= split)
    def _():
        pltpu.make_async_copy(high_ref.at[pl.ds(pl.multiple_of(start - split, 16), count)], goal, sem).start()

    for first in crossing:
        if first < split < first + count:
            low = split - first

            @pl.when(start == first)
            def _():
                pltpu.make_async_copy(low_ref.at[pl.ds(first, low)], target_ref.at[pl.ds(at, low)], sem).start()
                rest = target_ref.at[pl.ds(at + low, count - low)]
                pltpu.make_async_copy(high_ref.at[pl.ds(0, count - low)], rest, sem).start()

    return copy


def partial_kernel(
    fine, own_low, own_high, other_low, other_high, right_ref, right_other_ref,
    turn_ref, keep_ref, pass_ref, near_ref, half_ref, left_ref, sems,
):
    core, z, y, x = place()
    depth, high, wide = fine[1:]
    split = own_low.shape[0]
    rows = keep_ref.shape[1]
    half = half_ref.shape[1]
    step = pl.program_id(0)
    side_y, side_x = jnp.where(core == 0, y, 1 - y), jnp.where(core == 0, 1 - x, x)
    near, far = lax.rem(z + jnp.where(core == 0, 1, depth - 1), depth), lax.rem(z + 2, depth)
    whole_at = (split // rows) * rows
    crossing = (whole_at, whole_at + rows - half)

    def row(slot, line_y, line_x):
        return ((slot * high + line_y) * wide + line_x) * rows

    kept, passed = 2 * core, 2 - 2 * core
    parts = [(row(passed + at, 1 - y, 1 - x), rows) for at in range(2)]
    parts += [(row(kept + at, side_y, side_x), rows) for at in range(2)]
    parts += [(row(passed + at, side_y, side_x), rows) for at in range(2)]
    parts += [(row(near, y, x), rows)]
    parts += [(row(slot, y, x) + core * (rows - half), half) for slot in (z, far)]
    sides = ((own_low, own_high), (other_low, other_high))

    def copies():
        at = 0
        for index, (start, count) in enumerate(parts):
            for side, (low, up) in enumerate(sides):
                yield index, low, up, start, count, left_ref.at[side], at, sems.at[side, index]
            at += count

    @pl.when(step == 0)
    def _():
        for _, *what in copies():
            rows_copy(*what, crossing)

    def wait(indices):
        for index, low, _, _, count, target, at, sem in copies():
            if index in indices:
                pltpu.make_async_copy(low.at[pl.ds(0, count)], target.at[pl.ds(at, count)], sem).wait()

    def product(first, count):
        own = nn(left_ref[0, first : first + count], right_ref[...])
        return (own + nn(left_ref[1, first : first + count], right_other_ref[...])).astype(BF16)

    for at, out in enumerate((turn_ref, keep_ref, pass_ref)):

        @pl.when(step == at)
        def _():
            wait((2 * at, 2 * at + 1))
            out[...] = product(2 * at * rows, 2 * rows).reshape(out.shape)

    @pl.when(step == 3)
    def _():
        wait((6, 7, 8))
        last = product(6 * rows, rows + 2 * half)
        near_ref[...] = last[:rows]
        half_ref[...] = last[rows:].reshape(half_ref.shape)


def partial(fine, own_low, own_high, other_low, other_high, right, right_other):
    length, width = right.shape
    features = own_low.shape[0] + own_high.shape[0]
    rows = features // (fine[1] * fine[2] * fine[3])
    half = half_of(rows)
    shapes = [(2, rows, width)] * 3 + [(rows, width), (2, half, width)]
    return launch(
        functools.partial(partial_kernel, fine), (own_low, own_high, other_low, other_high, right, right_other),
        name="partial", micros=features / 700, grid=(4,),
        in_specs=[ANY] * 4 + [whole(length, width)] * 2,
        out_specs=[whole(*shape) for shape in shapes],
        out_shape=[array(shape) for shape in shapes],
        scratch=[pltpu.VMEM((2, 7 * rows + 2 * half, length), BF16), pltpu.SemaphoreType.DMA((2, 9))],
    )


def depth_kernel(
    near_ref, half_ref, keep_ref, pass_ref, keep_other, pass_other,
    near_out, far_out, own_out, near_got, half_got, sems,
):
    core, z = lax.axis_index("section"), lax.axis_index("z")
    depth = 4
    half = half_ref.shape[1]
    near = lax.rem(z + jnp.where(core == 0, 1, depth - 1), depth)
    part = pl.ds(pl.multiple_of(core * (near_ref.shape[0] - half), 16), half)
    copies = []
    for at, (keep, pass_, owner) in enumerate(((keep_ref, pass_ref, core), (keep_other, pass_other, 1 - core))):
        copies.append(slot_copy(near, keep, pass_, owner, near_got.at[at], sems.at[3 * at]))
        for index, slot in enumerate((z, lax.rem(z + 2, depth))):
            copies.append(slot_copy(slot, keep, pass_, owner, half_got.at[at, index], sems.at[3 * at + 1 + index], part))
    for copy in copies:
        copy.wait()
    near_total = near_ref[...].astype(F32) + near_got[0].astype(F32) + near_got[1].astype(F32)
    near_out[...] = near_total.astype(BF16)
    for index, out in enumerate((own_out, far_out)):
        total = half_ref[index].astype(F32) + half_got[0, index].astype(F32) + half_got[1, index].astype(F32)
        out[...] = total.astype(BF16)


def depth_sums(near, halves, keep, passed, keep_other, passed_other):
    rows, width = near.shape
    half = halves.shape[1]
    return launch(
        depth_kernel, (near, halves, keep, passed, keep_other, passed_other), name="depth", micros=2,
        in_specs=[VMEM] * 2 + [ANY] * 4, out_specs=[VMEM] * 3,
        out_shape=[array((rows, width)), array((half, width)), array((half, width))],
        scratch=[
            pltpu.VMEM((2, rows, width), BF16),
            pltpu.VMEM((2, 2, half, width), BF16),
            pltpu.SemaphoreType.DMA((6,)),
        ],
    )


def total_kernel(near_ref, near_other, far_ref, far_other, own_ref, own_other, *refs):
    second, out_ref = refs[:-1], refs[-1]
    core = lax.axis_index("section")
    rows, half = near_ref.shape[0], far_ref.shape[0]
    near = near_ref[...].astype(F32) + near_other[...].astype(F32)
    mine = far_ref[...].astype(F32) + own_ref[...].astype(F32)
    other = far_other[...].astype(F32) + own_other[...].astype(F32)
    low, high = jnp.where(core == 0, mine, other), jnp.where(core == 0, other, mine)
    out_ref[:half] = near[:half] + low
    out_ref[half:] = near[half:] + high[2 * half - rows :]
    if second:

        @pl.when(core == 1)
        def _():
            out_ref[...] = second[0][...]


def total(near, near_other, far, far_other, own, own_other, *second):
    values = (near, near_other, far, far_other, own, own_other, *second)
    return launch(
        total_kernel, values, name="total", micros=1.5,
        in_specs=[VMEM] * len(values), out_specs=VMEM, out_shape=array(near.shape, F32),
    )


class Order:
    def __init__(self, first):
        self.last = first
        self.moving = []

    def run(self, function, *values):
        values, _ = lax.optimization_barrier((values, self.last))
        return self.fence(function(*values))

    def fence(self, *result):
        due = [value for value, left in self.moving if left == 0]
        self.moving = [(value, left - 1) for value, left in self.moving if left > 0]
        result, self.last, _ = lax.optimization_barrier((result, self.last, due))
        if result:
            self.last = jax.tree.leaves(result)[0]
            return result[0]

    def move(self, way, *values, count=1):
        values, _ = lax.optimization_barrier((values, self.last))
        moved = [way(value) for value in values]
        self.moving += [(value, count - 1) for value in moved]
        return moved if len(values) > 1 else moved[0]

    def swap(self, *values, count=1):
        return self.move(swap, *values, count=count)


def total_along(value, axis, size):
    return sum([lax.ppermute(value, axis, [(i, (i + k) % size) for i in range(size)]) for k in range(1, size)], value)


def total_of(value, fine):
    for axis, size in zip(ALL, fine):
        value = total_along(value, axis, size) if size < 8 else lax.psum(value, axis)
    return value


def added(first, second):
    return (first.astype(F32) + second.astype(F32)).astype(BF16)


class Gather:
    def __init__(self, order, fine, shard, half):
        self.order, self.fine, self.shard, self.half = order, fine, shard, half

    def along(self, count=1):
        self.near = self.order.move(functools.partial(along, fine=self.fine), self.shard, count=count)
        self.far = self.order.move(functools.partial(opposite, fine=self.fine), self.half, count=count)

    def across(self, count=1):
        self.near_other, self.far_other = self.order.swap(self.near, self.far, count=count)

    def line(self):
        self.keep, self.passed = self.order.run(
            line_of, self.shard, self.near, self.near_other, self.far, self.far_other
        )

    def side(self, count=1):
        self.side_passed = self.order.move(functools.partial(sideways, fine=self.fine), self.passed, count=count)
        self.side_keep = self.order.move(functools.partial(sideways, fine=self.fine), self.keep, count=count)

    def turn(self, count=1):
        self.corner = self.order.move(functools.partial(turned, fine=self.fine), self.side_passed, count=count)

    def rest(self, count=1):
        self.turn_keep, self.turn_passed = self.order.swap(self.side_keep, self.side_passed, count=count)

    def meet(self):
        self.corner_other = self.order.swap(self.corner)

    def pieces(self):
        return (
            self.keep, self.passed, self.side_keep, self.side_passed, self.turn_keep, self.turn_passed,
            self.corner, self.corner_other,
        )


class Scatter:
    def __init__(self, order, fine, values):
        self.order, self.fine = order, fine
        self.turn, self.keep, self.passed, self.near, self.halves = values

    def start(self, count=1):
        self.turn = self.order.move(functools.partial(turned, fine=self.fine), self.turn, count=count)
        self.keep = self.order.move(functools.partial(sideways, fine=self.fine), self.keep, count=count)

    def add(self):
        self.passed = self.order.run(added, self.passed, self.turn)

    def pass_on(self):
        self.passed = self.order.move(functools.partial(sideways, fine=self.fine), self.passed)

    def keep_across(self):
        self.keep_other = self.order.swap(self.keep)

    def meet(self):
        self.passed_other = self.order.swap(self.passed)

    def parts(self):
        return self.near, self.halves, self.keep, self.passed, self.keep_other, self.passed_other

    def along(self, values, count=1):
        near, far, self.own = values
        self.near = self.order.move(functools.partial(along, fine=self.fine), near, count=count)
        self.far = self.order.move(functools.partial(opposite, fine=self.fine), far, count=count)

    def own_across(self):
        self.own_other = self.order.swap(self.own)

    def across(self):
        self.near_other, self.far_other = self.order.swap(self.near, self.far)

    def ends(self):
        return self.near, self.near_other, self.far, self.far_other, self.own, self.own_other


def body(fine, inputs, cotangent, lengths, weight_in, weight_out, scales):
    length, width = inputs.shape[2], inputs.shape[3]
    core, z, y, x = place()
    depth = fine[1]
    device = (z * fine[2] + y) * fine[3] + x
    pair = lax.dynamic_index_in_dim(lengths, core, 0, False)
    scale_count = scales.shape[1]
    whole_scales = scale_count * depth * fine[2] * fine[3]
    by_core = lambda first, second: (jnp.where(core == 0, first, second), jnp.where(core == 0, second, first))

    shift = lambda axis: lambda value: lax.ppermute(value, axis, [(0, 1), (1, 0)])
    spread = lambda mine, other: jnp.stack(by_core(mine, other))[None, :, None]
    chip = functools.partial(partial, fine)

    def padded(flat):
        return jnp.pad(flat, (0, -flat.shape[0] % 1024)).reshape(-1, 128)

    own_scales = lax.dynamic_update_slice(
        jnp.zeros((2 * whole_scales,), F32), scales[0].astype(F32), (core * whole_scales + device * scale_count,)
    )
    scale = padded(own_scales)

    def vectors_of(scale):
        scale = scale.reshape(-1)[: 2 * whole_scales].reshape(2, whole_scales)
        return [(s[None, :width], s[width : width + HEAD, None], s[width + HEAD :, None]) for s in scale]

    def own_rows(inputs, cotangent):
        rows = lax.dynamic_index_in_dim(inputs, core, 0, False)[0]
        grad = lax.dynamic_index_in_dim(cotangent, core, 0, False)[0]
        position = lax.broadcasted_iota(jnp.int32, (length, 1), 0)
        return rows, jnp.where(position < pair[0, 0] + pair[0, 1], grad, jnp.zeros_like(grad))

    order = Order(scale)
    butterfly = lambda by: lambda value: lax.ppermute(value, "z", [(i, i ^ by) for i in range(depth)])
    out = functools.partial(output, pair)
    if depth == 4:
        in_rows, out_rows = weight_in.shape[1], weight_out.shape[1]
        gather = lambda values: Gather(order, fine, *values)
        other_in, other_out, got = order.swap(weight_in[0], weight_out[0], scale)
        order.fence()
        first = gather(order.run(functools.partial(pick, 0), weight_in[0], other_in))
        first.along()
        scale = scale + got
        got = order.move(shift("x"), scale)
        picked = order.run(
            lambda own_in, other_in, own_out, other_out, *values: (
                pick(0, own_out, other_out), pick(1, own_in, other_in), pick(1, own_out, other_out), own_rows(*values)
            ),
            weight_in[0], other_in, weight_out[0], other_out, inputs, cotangent,
        )
        second, third, fourth = [gather(values) for values in picked[:3]]
        rows_0, grad_1 = picked[3]
        first.across()
        scale = scale + got
        got = order.move(shift("y"), scale)
        order.fence()
        first.line()
        first.side()
        second.along()
        scale = scale + got
        got = order.move(butterfly(1), scale)
        order.fence()
        first.turn(count=3)
        second.across()
        first.rest(count=2)
        order.fence()
        scale = scale + got
        got = order.move(butterfly(2), scale)
        second.line()
        vectors_0, vectors_1 = order.run(vectors_of, scale + got)
        second.side(count=2)
        third.along(count=2)
        first.meet()
        order.fence()
        front, out = functools.partial(attend, in_rows, pair), functools.partial(output, pair, out_rows)
        normed_0, raw_0, value_0, attended_0, logs_0, weight_in_0 = order.run(front, rows_0, *vectors_0, *first.pieces())
        second.turn()
        second.rest()
        third.across()
        hidden_0, slope_0 = order.run(hidden, normed_0, weight_in_0)
        second.meet()
        third.line()
        third.side()
        fourth.along()
        rows_1, squares_0, weight_out_0 = order.run(out, rows_0, attended_0, hidden_0, *second.pieces())
        third.turn(count=3)
        fourth.across()
        third.rest(count=2)
        order.fence()
        fourth.line()
        grad_1_other = order.swap(grad_1)
        order.fence()
        fourth.side(count=2)
        third.meet()
        order.fence()
        attended_0_other, normed_0_other, hidden_0_other = order.swap(attended_0, normed_0, hidden_0)
        normed_1, raw_1, value_1, attended_1, logs_1, weight_in_1 = order.run(front, rows_1, *vectors_1, *third.pieces())
        fourth.turn()
        fourth.rest()
        attended_1_other, normed_1_other = order.swap(attended_1, normed_1)
        hidden_1, slope_1 = order.run(hidden, normed_1, weight_in_1)
        fourth.meet()
        order.fence()
        hidden_1_other, rows_1_other = order.swap(hidden_1, rows_1)
        feed_1, low_1, weight_out_1 = order.run(
            functools.partial(feed_back, out_rows), grad_1, slope_1, weight_in_1, *fourth.pieces()
        )
    else:
        weight_in_0, weight_in_1 = jnp.split(lax.all_gather(weight_in[0], ALL, axis=0, tiled=True), 2)
        weight_out_0, weight_out_1 = jnp.split(lax.all_gather(weight_out[0], ALL, axis=0, tiled=True), 2)
        vectors_0, vectors_1 = vectors_of(total_of(scale, fine))
        rows_0, grad_1 = own_rows(inputs, cotangent)
        front, out = functools.partial(attend, None, pair), functools.partial(output, pair, None)
        normed_0, raw_0, value_0, attended_0, logs_0 = order.run(front, rows_0, *vectors_0, weight_in_0)
        hidden_0, slope_0 = order.run(hidden, normed_0, weight_in_0)
        rows_1, squares_0 = order.run(out, rows_0, attended_0, hidden_0, weight_out_0)
        normed_1, raw_1, value_1, attended_1, logs_1 = order.run(front, rows_1, *vectors_1, weight_in_1)
        hidden_1, slope_1 = order.run(hidden, normed_1, weight_in_1)
        feed_1, low_1 = order.run(functools.partial(feed_back, None), grad_1, slope_1, weight_in_1, weight_out_1)
    out, back, feed = functools.partial(output, pair, None), functools.partial(attend_back, pair), functools.partial(feed_back, None)
    kept_1 = (rows_1, grad_1, *vectors_1, raw_1, value_1, attended_1, logs_1, weight_out_1, weight_in_1)

    def small_sums(squares_0, squares_1, gain_0, heads_0, gain_1, heads_1):
        sums = [jnp.sum(squares, axis=(1, 2)) for squares in (squares_0, squares_1)]
        scale_grads = [
            jnp.concatenate([jnp.sum(gain, axis=0), jnp.sum(heads, axis=2).reshape(-1)])
            for gain, heads in ((gain_0, heads_0), (gain_1, heads_1))
        ]
        return padded(jnp.concatenate([jnp.sum(pair).astype(F32)[None], *sums, *scale_grads]))

    if depth == 4:
        low_1_other = order.swap(low_1)
        out_1 = Scatter(order, fine, order.run(
            chip, attended_1, hidden_1, attended_1_other, hidden_1_other, grad_1, grad_1_other
        ))
        out_1.start()
        top_1, grad_0, gain_1, heads_1 = order.run(back, *kept_1, feed_1)
        grad_0_other = order.swap(grad_0)
        top_1_other = order.swap(top_1, count=3)
        out_1.add()
        out_1.pass_on()
        out_1.keep_across()
        out_0 = Scatter(order, fine, order.run(
            chip, attended_0, hidden_0, attended_0_other, hidden_0_other, grad_0, grad_0_other
        ))
        out_0.start()
        out_1.meet()
        feed_0, low_0 = order.run(feed, grad_0, slope_0, weight_in_0, weight_out_0)
        out_0.add()
        out_0.pass_on()
        out_0.keep_across()
        low_0_other = order.swap(low_0)
        in_1, ends = order.run(
            lambda values, parts: (chip(*values), depth_sums(*parts)),
            (top_1, low_1, top_1_other, low_1_other, normed_1, normed_1_other), out_1.parts(),
        )
        in_1 = Scatter(order, fine, in_1)
        in_1.start()
        out_1.along(ends)
        out_0.meet()
        kept_0 = (rows_0, grad_0, *vectors_0, raw_0, value_0, attended_0, logs_0, weight_out_0, weight_in_0)
        top_0, grad_first, gain_0, heads_0 = order.run(back, *kept_0, feed_0)
        top_0_other = order.swap(top_0)
        ends, in_1.passed = order.run(
            lambda parts, first, second: (depth_sums(*parts), added(first, second)), out_0.parts(), in_1.passed, in_1.turn
        )
        in_1.pass_on()
        out_0.along(ends)
        in_1.keep_across()
        in_0 = Scatter(order, fine, order.run(chip, top_0, low_0, top_0_other, low_0_other, normed_0, normed_0_other))
        in_1.meet()
        out_1.across()
        order.fence()
        ends = order.run(depth_sums, *in_1.parts())
        in_0.start()
        in_1.along(ends)
        out_1.own_across()
        result_1, squares_1 = order.run(out, rows_1, attended_1, hidden_1, weight_out_1)
        in_0.add()
        in_0.pass_on()
        in_0.keep_across()
        out_0.across()
        out_0.own_across()
        small, out_grad_1 = order.run(
            lambda sums, values: (small_sums(*values), total(*sums)),
            out_1.ends(), (squares_0, squares_1, gain_0, heads_0, gain_1, heads_1),
        )
        in_0.meet()
        got = order.move(shift("x"), small)
        order.fence()
        small = small + got
        got = order.move(shift("y"), small)
        in_1.across()
        in_1.own_across()
        ends = order.run(depth_sums, *in_0.parts())
        in_0.along(ends)
        small = small + got
        result_1_other, grad_first_other = order.swap(result_1, grad_first)
        in_0.own_across()
        def spread_both(rows_1, rows_other, result, result_other, first, first_other, grad_0, grad_other):
            outputs = jnp.where(core == 0, rows_1, result), jnp.where(core == 0, rows_other, result_other)
            grads = jnp.where(core == 0, first, grad_0), jnp.where(core == 0, first_other, grad_other)
            return spread(*outputs), spread(*grads)

        out_grad, in_grad_1 = order.run(
            lambda first, second: (total(*first), total(*second)), (*out_0.ends(), out_grad_1), in_1.ends()
        )
        in_0.across()
        got = order.move(butterfly(1), small)
        outputs, input_grads = order.run(
            spread_both, rows_1, rows_1_other, result_1, result_1_other, grad_first, grad_first_other, grad_0, grad_0_other
        )
        small = small + got
        got = order.move(butterfly(2), small)
        in_grad = order.run(total, *in_0.ends(), in_grad_1)[None]
        small = small + got
        small = small + order.swap(small)
        out_grad = out_grad[None]
    else:
        top_1, grad_0, gain_1, heads_1 = order.run(back, *kept_1, feed_1)
        feed_0, low_0 = order.run(feed, grad_0, slope_0, weight_in_0, weight_out_0)
        kept_0 = (rows_0, grad_0, *vectors_0, raw_0, value_0, attended_0, logs_0, weight_out_0, weight_in_0)
        top_0, grad_first, gain_0, heads_0 = order.run(back, *kept_0, feed_0)
        result_1, squares_1 = order.run(out, rows_1, attended_1, hidden_1, weight_out_1)
        own = lambda low, high, right: nn(jnp.concatenate([low, high]), right).astype(BF16)
        summed = lambda first, second: lax.psum_scatter(
            jnp.concatenate([first, second]), ALL, scatter_dimension=0, tiled=True
        ).astype(F32)[None]
        in_grad = summed(own(top_0, low_0, normed_0), own(top_1, low_1, normed_1))
        out_grad = summed(own(attended_0, hidden_0, grad_0), own(attended_1, hidden_1, grad_1))
        small = small_sums(squares_0, squares_1, gain_0, heads_0, gain_1, heads_1)
        for axis in ALL:
            small = lax.psum(small, axis)
        outputs, input_grads = [
            spread(mine, swap(given)) for mine, given in (by_core(rows_1, result_1), by_core(grad_first, grad_0))
        ]
    small = small.reshape(-1)
    statistics = jnp.sqrt(lax.dynamic_slice(small, (1 + 3 * core,), (3,)) / (small[0] * width))
    scale_grad = lax.dynamic_slice(small, (7 + core * whole_scales + device * scale_count,), (scale_count,))
    return outputs, input_grads, in_grad, out_grad, scale_grad[None], statistics[None]


def solution(mesh):
    count = mesh.shape["dp"]
    fine = Mesh(mesh.devices.reshape(2, count // 4, 2, 2), ALL)
    return jax.shard_map(
        functools.partial(body, (2, count // 4, 2, 2)),
        mesh=fine,
        in_specs=(
            P(None, DP, None, None),
            P(None, DP, None, None),
            P(None, DP, None),
            P("section", DP, None),
            P("section", DP, None),
            P("section", DP),
        ),
        out_specs=(
            P("section", None, DP, None, None),
            P("section", None, DP, None, None),
            P("section", DP, None),
            P("section", DP, None),
            P("section", DP),
            P("section", None),
        ),
        check_vma=False,
    )
```

```python
import functools

import jax
import jax.numpy as jnp
from jax import lax
from jax.experimental import pallas as pl
from jax.experimental.pallas import tpu as pltpu
from jax.sharding import Mesh, PartitionSpec as P

HEADS = 12
HEAD = 64
GROUP = 4
GROUPS = HEADS // GROUP
LANES = GROUP * HEAD
EPSILON = 1e-06
MASKED = -1e30
FACTOR = HEAD**-0.5
F32 = jnp.float32
BF16 = jnp.bfloat16
DP = ("z", "y", "x")
ALL = ("section",) + DP
VMEM_MIB = 60
ANY = pl.BlockSpec(memory_space=pl.ANY)
VMEM = pl.BlockSpec(memory_space=pltpu.VMEM)


def nn(left, right):
    return lax.dot_general(left, right, (((1,), (0,)), ((), ())), preferred_element_type=F32)


def nt(left, right):
    return lax.dot_general(left, right, (((1,), (1,)), ((), ())), preferred_element_type=F32)


def tn(left, right):
    return lax.dot_general(left, right, (((0,), (0,)), ((), ())), preferred_element_type=F32)


def launch(kernel, values, *, name, micros, grid=(), in_specs, out_specs, out_shape, scratch=()):
    return pl.pallas_call(
        kernel,
        grid=grid,
        in_specs=in_specs,
        out_specs=out_specs,
        out_shape=out_shape,
        scratch_shapes=scratch,
        cost_estimate=pl.CostEstimate(flops=int(micros * 1150000000.0), bytes_accessed=int(micros * 1000000.0), transcendentals=0),
        compiler_params=pltpu.CompilerParams(
            vmem_limit_bytes=VMEM_MIB * 1024 * 1024, dimension_semantics=("arbitrary",) * len(grid)
        ),
        name=name,
    )(*values)


def array(shape, dtype=BF16):
    return jax.ShapeDtypeStruct(shape, dtype)


def row_norm(rows):
    average = jnp.mean(rows, axis=1, keepdims=True)
    centred = rows - average
    inverse = lax.rsqrt(jnp.mean(centred * centred, axis=1, keepdims=True) + EPSILON)
    return centred * inverse, inverse


def column_norm(columns):
    average = jnp.mean(columns, axis=0, keepdims=True)
    centred = columns - average
    inverse = lax.rsqrt(jnp.mean(centred * centred, axis=0, keepdims=True) + EPSILON)
    return centred * inverse, inverse


def norm_back(normal, inverse, grad, scale, axis):
    scaled = grad * scale
    average = jnp.mean(scaled, axis=axis, keepdims=True)
    along_normal = jnp.mean(scaled * normal, axis=axis, keepdims=True)
    return inverse * (scaled - average - normal * along_normal)


def segment_at(pair_ref, position):
    first_end = pair_ref[0, 0]
    second_end = first_end + pair_ref[0, 1]
    return (position >= first_end).astype(jnp.int32) + (position >= second_end).astype(jnp.int32)


def fill_bias(pair_ref, bias_ref):
    length = bias_ref.shape[0]
    down = segment_at(pair_ref, lax.broadcasted_iota(jnp.int32, (length, length), 0))
    sideways = segment_at(pair_ref, lax.broadcasted_iota(jnp.int32, (length, length), 1))
    bias_ref[...] = jnp.where(down == sideways, 0.0, MASKED).astype(F32)


def whole(*shape):
    return pl.BlockSpec(shape, lambda *_: (0,) * len(shape))


def attend_kernel(in_rows, pair_ref, rows_ref, gain_ref, query_scale_ref, key_scale_ref, *refs):
    step = pl.program_id(0)
    if in_rows is None:
        weight_ref, normed_ref, raw_ref, value_ref, attended_ref, log_ref, bias_ref = refs
        weight = weight_ref[...].reshape(3 * LANES, rows_ref.shape[1])
    else:
        pieces, refs = refs[:8], refs[8:]
        normed_ref, raw_ref, value_ref, attended_ref, log_ref, full_ref, bias_ref, weight_ref, sems, full_sems = refs
        load_weight(step, pieces, weight_ref, sems, in_rows, full_ref, full_sems, (0, 0, 1, 1))
        starts = [pl.multiple_of(rows_ref.shape[1] * third + LANES * step, LANES) for third in range(3)]
        weight = jnp.concatenate([weight_ref[pl.ds(start, LANES)] for start in starts])

    @pl.when(step == 0)
    def _():
        normal, _ = row_norm(rows_ref[...].astype(F32))
        normed_ref[...] = (normal * gain_ref[...]).astype(BF16)
        fill_bias(pair_ref, bias_ref)

    normed = normed_ref[...]
    projected = nt(weight, normed)
    raw_ref[...] = projected[: 2 * LANES].reshape(raw_ref.shape)
    value_ref[...] = projected[2 * LANES :].astype(BF16)
    for head in range(GROUP):
        at = slice(head * HEAD, (head + 1) * HEAD)
        query = column_norm(projected[:LANES][at])[0] * query_scale_ref[...]
        query = query.astype(BF16) * BF16(FACTOR)
        key = (column_norm(projected[LANES : 2 * LANES][at])[0] * key_scale_ref[...]).astype(BF16)
        scores = tn(key, query) + bias_ref[...]
        peak = jnp.max(scores, axis=0, keepdims=True)
        exponent = jnp.exp(scores - peak)
        total = jnp.sum(exponent, axis=0, keepdims=True)
        attended = nn(value_ref[at, :], exponent.astype(BF16)) * (1.0 / total)
        attended_ref[at, :] = attended.astype(BF16)
        log_ref[0, head : head + 1, :] = peak + jnp.log(total)


def attend(in_rows, pair, rows, gain, query_scale, key_scale, *weights):
    length, width = rows.shape
    gathered = in_rows is not None
    features = 16 * in_rows if gathered else weights[0].shape[0]
    if not gathered:
        weights = (weights[0].reshape(-1, GROUPS, LANES, width),)
    return launch(
        functools.partial(attend_kernel, in_rows),
        (pair, rows, gain, query_scale, key_scale, *weights),
        name="attend",
        micros=13,
        grid=(GROUPS,),
        in_specs=[
            pl.BlockSpec(memory_space=pltpu.SMEM),
            whole(length, width),
            whole(1, width),
            whole(HEAD, 1),
            whole(HEAD, 1),
            *([ANY] * 8 if gathered else [pl.BlockSpec((3, 1, LANES, width), lambda g: (0, g, 0, 0))]),
        ],
        out_specs=[
            whole(length, width),
            pl.BlockSpec((2, 1, LANES, length), lambda g: (0, g, 0, 0)),
            pl.BlockSpec((LANES, length), lambda g: (g, 0)),
            pl.BlockSpec((LANES, length), lambda g: (g, 0)),
            pl.BlockSpec((1, 8, length), lambda g: (g, 0, 0)),
            *[ANY] * gathered,
        ],
        out_shape=[
            array((length, width)),
            array((2, GROUPS, LANES, length), F32),
            array((width, length)),
            array((width, length)),
            array((GROUPS, 8, length), F32),
            *[array((features, width))] * gathered,
        ],
        scratch=[
            pltpu.VMEM((length, length), F32),
            *(weight_scratch(features, width) if gathered else ()),
        ],
    )


def hidden_kernel(normed_ref, weight_ref, hidden_ref, slope_ref):
    feed = nt(weight_ref[...], normed_ref[...])
    half = 0.5 * lax.erf(feed * (0.5**0.5)) + 0.5
    hidden_ref[...] = (feed * half).astype(BF16)
    density = jnp.exp(feed * feed * -0.5) * ((2.0 * jnp.pi) ** -0.5)
    slope_ref[...] = (half + feed * density).astype(BF16)


def hidden(normed, weight_in):
    length, width = normed.shape
    count = weight_in.shape[0] // width - 3
    return launch(
        hidden_kernel,
        (normed, weight_in),
        name="hidden",
        micros=8,
        grid=(count,),
        in_specs=[whole(length, width), pl.BlockSpec((width, width), lambda i: (i + 3, 0))],
        out_specs=[pl.BlockSpec((width, length), lambda i: (i, 0))] * 2,
        out_shape=[array((count * width, length))] * 2,
    )


def load_weight(step, pieces, target, sems, rows, full_ref, full_sems, steps):
    @pl.when(step == 0)
    def _():
        piece_copies(pieces, target, sems, rows)

    size = 4 * rows
    out = [
        pltpu.make_async_copy(target.at[pl.ds(size * slot, size)], full_ref.at[pl.ds(size * slot, size)], full_sems.at[slot])
        for slot in range(4)
    ]
    for slot in range(4):

        @pl.when(step == steps[slot])
        def _():
            for at in range(4):
                goal = target.at[pl.ds(size * slot + rows * at, rows)]
                pltpu.make_async_copy(pieces[0].at[0, pl.ds(0, rows)], goal, sems.at[4 * slot + at]).wait()
            out[slot].start()

    @pl.when(step == pl.num_programs(0) - 1)
    def _():
        for copy in out:
            copy.wait()


def output_kernel(out_rows, pair_ref, rows_ref, attended_ref, hidden_ref, *refs):
    step, last = pl.program_id(0), pl.num_programs(0) - 1
    width = rows_ref.shape[1]
    if out_rows is None:
        weight_ref, result_ref, sums_ref, attend_ref, feed_ref = refs
        weight = weight_ref[...]
    else:
        pieces, (result_ref, sums_ref, full_ref, attend_ref, feed_ref, all_ref, sems, full_sems) = refs[:8], refs[8:]
        load_weight(step, pieces, all_ref, sems, out_rows, full_ref, full_sems, (0, 1, 2, 3))
        weight = all_ref[pl.ds(pl.multiple_of(step * width, width), width)]

    @pl.when(step == 0)
    def _():
        attend_ref[...] = tn(attended_ref[...], weight)

    @pl.when(step == 1)
    def _():
        feed_ref[...] = tn(hidden_ref[...], weight)

    @pl.when(step > 1)
    def _():
        feed_ref[...] += tn(hidden_ref[...], weight)

    @pl.when(step == last)
    def _():
        length = attend_ref.shape[0]
        position = lax.broadcasted_iota(jnp.int32, (length, 1), 0)
        valid = (segment_at(pair_ref, position) < 2).astype(F32)
        branch, feed = attend_ref[...], feed_ref[...]
        result = rows_ref[...].astype(F32) + branch + feed
        result_ref[...] = result.astype(BF16)
        for at, value in enumerate((result, branch, feed)):
            squares = (value * value * valid).reshape(length // 8, 8, width)
            sums_ref[at] = jnp.sum(squares, axis=0)


def weight_scratch(features, width):
    return [pltpu.VMEM((features, width), BF16), pltpu.SemaphoreType.DMA((16,)), pltpu.SemaphoreType.DMA((4,))]


def output(pair, out_rows, rows, attended, hid, *weights):
    length, width = rows.shape
    features = hid.shape[0] + width
    count = features // width
    gathered = out_rows is not None
    return launch(
        functools.partial(output_kernel, out_rows),
        (pair, rows, attended, hid, *weights),
        name="output",
        micros=9,
        grid=(count,),
        in_specs=[
            pl.BlockSpec(memory_space=pltpu.SMEM),
            whole(length, width),
            whole(width, length),
            pl.BlockSpec((width, length), lambda i: (jnp.maximum(i - 1, 0), 0)),
            *([ANY] * 8 if gathered else [pl.BlockSpec((width, width), lambda i: (i, 0))]),
        ],
        out_specs=[whole(length, width), whole(3, 8, width), *[ANY] * gathered],
        out_shape=[array((length, width)), array((3, 8, width), F32), *[array((features, width))] * gathered],
        scratch=[
            *[pltpu.VMEM((length, width), F32)] * 2,
            *(weight_scratch(features, width) if gathered else ()),
        ],
    )


def feed_back_kernel(out_rows, grad_ref, slope_ref, weight_in_ref, *refs):
    step = pl.program_id(0)
    width = grad_ref.shape[1]
    if out_rows is None:
        weight_ref, grad_normed_ref, grad_feed_ref = refs
        weight_out = weight_ref[...]
    else:
        pieces, (grad_normed_ref, grad_feed_ref, full_ref, all_ref, sems, full_sems) = refs[:8], refs[8:]
        load_weight(step, pieces, all_ref, sems, out_rows, full_ref, full_sems, (0, 0, 1, 2))
        weight_out = all_ref[pl.ds(pl.multiple_of((step + 1) * width, width), width)]
    grad_hidden = nt(weight_out, grad_ref[...]).astype(BF16).astype(F32)
    grad_feed = (grad_hidden * slope_ref[...].astype(F32)).astype(BF16)
    grad_feed_ref[...] = grad_feed
    part = tn(grad_feed, weight_in_ref[...])

    @pl.when(step == 0)
    def _():
        grad_normed_ref[...] = part

    @pl.when(step > 0)
    def _():
        grad_normed_ref[...] += part


def feed_back(out_rows, grad, slope, weight_in, *weights):
    length, width = grad.shape
    features = slope.shape[0] + width
    count = slope.shape[0] // width
    gathered = out_rows is not None
    rows = pl.BlockSpec((width, length), lambda i: (i, 0))
    return launch(
        functools.partial(feed_back_kernel, out_rows),
        (grad, slope, weight_in, *weights),
        name="feed_back",
        micros=11,
        grid=(count,),
        in_specs=[
            whole(length, width),
            rows,
            pl.BlockSpec((width, width), lambda i: (i + 3, 0)),
            *([ANY] * 8 if gathered else [pl.BlockSpec((width, width), lambda i: (i + 1, 0))]),
        ],
        out_specs=[whole(length, width), rows, *[ANY] * gathered],
        out_shape=[array((length, width), F32), array(slope.shape), *[array((features, width))] * gathered],
        scratch=weight_scratch(features, width) if gathered else (),
    )


def attend_back_kernel(
    pair_ref, rows_ref, grad_ref, gain_ref, query_scale_ref, key_scale_ref, raw_ref, value_ref,
    attended_ref, log_ref, weight_out_ref, weight_in_ref, feed_grad_ref,
    projected_ref, grad_in_ref, gain_grad_ref, scale_grad_ref, bias_ref, grad_normed_ref,
):
    step = pl.program_id(0)

    @pl.when(step == 0)
    def _():
        fill_bias(pair_ref, bias_ref)
        grad_normed_ref[...] = feed_grad_ref[...]
        scale_grad_ref[...] = jnp.zeros_like(scale_grad_ref)

    length, width = grad_ref.shape
    query_scale, key_scale = query_scale_ref[...], key_scale_ref[...]
    grad_attended = nt(weight_out_ref[0], grad_ref[...]).astype(BF16)
    for head in range(GROUP):
        at = slice(head * HEAD, (head + 1) * HEAD)
        query_normal, query_inverse = column_norm(raw_ref[0, 0, at, :])
        key_normal, key_inverse = column_norm(raw_ref[1, 0, at, :])
        query = (query_normal * query_scale).astype(BF16) * BF16(FACTOR)
        key = (key_normal * key_scale).astype(BF16)
        value = value_ref[at, :]
        probs = jnp.exp(tn(key, query) + bias_ref[...] - log_ref[0, head : head + 1, :])
        grad_out = grad_attended[at]
        grad_probs = tn(value, grad_out)
        grad_value = nt(grad_out, probs.astype(BF16))
        delta = jnp.sum(grad_out.astype(F32) * attended_ref[at, :].astype(F32), axis=0, keepdims=True)
        grad_scores = (probs * (grad_probs - delta)).astype(BF16)
        grad_query = nn(key, grad_scores) * FACTOR
        grad_key = nt(query, grad_scores)
        for place_at, term in enumerate((grad_query * query_normal, grad_key * key_normal)):
            for lane in range(0, length, 128):
                scale_grad_ref[place_at] += term[:, lane : lane + 128]
        projected_ref[0, 0, at, :] = norm_back(query_normal, query_inverse, grad_query, query_scale, 0).astype(BF16)
        projected_ref[1, 0, at, :] = norm_back(key_normal, key_inverse, grad_key, key_scale, 0).astype(BF16)
        projected_ref[2, 0, at, :] = grad_value.astype(BF16)
    projected = projected_ref[...].reshape(3 * LANES, length)
    grad_normed_ref[...] += tn(projected, weight_in_ref[...].reshape(3 * LANES, width))

    @pl.when(step == pl.num_programs(0) - 1)
    def _():
        normal, inverse = row_norm(rows_ref[...].astype(F32))
        grad_normed = grad_normed_ref[...]
        grad_rows = norm_back(normal, inverse, grad_normed, gain_ref[...], 1)
        grad_in_ref[...] = (grad_ref[...].astype(F32) + grad_rows).astype(BF16)
        gain_grad_ref[...] = jnp.sum((grad_normed * normal).reshape(length // 8, 8, width), axis=0)


def attend_back(pair, rows, grad, gain, query_scale, key_scale, raw, value, attended, logs, weight_out,
                weight_in, feed_grad):
    length, width = grad.shape
    group_rows = pl.BlockSpec((LANES, length), lambda g: (g, 0))
    projected, *others = launch(
        attend_back_kernel,
        (pair, rows, grad, gain, query_scale, key_scale, raw, value, attended, logs,
         weight_out.reshape(-1, LANES, width), weight_in.reshape(-1, GROUPS, LANES, width), feed_grad),
        name="attend_back",
        micros=17,
        grid=(GROUPS,),
        in_specs=[
            pl.BlockSpec(memory_space=pltpu.SMEM),
            whole(length, width),
            whole(length, width),
            whole(1, width),
            whole(HEAD, 1),
            whole(HEAD, 1),
            pl.BlockSpec((2, 1, LANES, length), lambda g: (0, g, 0, 0)),
            group_rows,
            group_rows,
            pl.BlockSpec((1, 8, length), lambda g: (g, 0, 0)),
            pl.BlockSpec((1, LANES, width), lambda g: (g, 0, 0)),
            pl.BlockSpec((3, 1, LANES, width), lambda g: (0, g, 0, 0)),
            whole(length, width),
        ],
        out_specs=[
            pl.BlockSpec((3, 1, LANES, length), lambda g: (0, g, 0, 0)),
            whole(length, width),
            whole(8, width),
            whole(2, HEAD, 128),
        ],
        out_shape=[
            array((3, GROUPS, LANES, length)),
            array((length, width)),
            array((8, width), F32),
            array((2, HEAD, 128), F32),
        ],
        scratch=[pltpu.VMEM((length, length), F32), pltpu.VMEM((length, width), F32)],
    )
    return projected.reshape(3 * width, length), *others


def sends(fine, first, second):
    _, depth, high, wide = fine
    number = lambda c, z, y, x: ((c * depth + z) * high + y) * wide + x
    return [
        (number(c, z, y, x), number(c, *(first, second)[c](z, y, x)))
        for c in range(2)
        for z in range(depth)
        for y in range(high)
        for x in range(wide)
    ]


def next_x(z, y, x):
    return z, y, 1 - x


def next_y(z, y, x):
    return z, 1 - y, x


def sideways(value, fine):
    return lax.ppermute(value, ALL, sends(fine, next_x, next_y))


def turned(value, fine):
    return lax.ppermute(value, ALL, sends(fine, next_y, next_x))


def along(value, fine):
    depth = fine[1]
    return lax.ppermute(
        value, ALL, sends(fine, lambda z, y, x: ((z + 1) % depth, y, x), lambda z, y, x: ((z - 1) % depth, y, x))
    )


def opposite(value, fine):
    depth = fine[1]
    return lax.ppermute(value, "z", [(z, (z + 2) % depth) for z in range(depth)])


def swap(value):
    return lax.ppermute(value, "section", [(0, 1), (1, 0)])


def place():
    return [lax.axis_index(axis) for axis in ALL]


def either(condition, make_first, make_second):
    @pl.when(condition)
    def _():
        make_first().start()

    @pl.when(jnp.logical_not(condition))
    def _():
        make_second().start()


def slot_copy(slot, keep_ref, pass_ref, owner, target, sem, rows=None):
    index = slot % 2 if isinstance(slot, int) else lax.rem(slot, 2)
    view = (lambda ref: ref.at[index]) if rows is None else (lambda ref: ref.at[index, rows])
    kept = pltpu.make_async_copy(view(keep_ref), target, sem)
    either(slot // 2 == owner, lambda: kept, lambda: pltpu.make_async_copy(view(pass_ref), target, sem))
    return kept


def half_of(rows):
    return -(-rows // 32) * 16


def pick_kernel(layer, own_ref, other_ref, *refs):
    extra, (shard_ref, half_ref, sem) = refs[:-3], refs[-3:]
    core = lax.axis_index("section")
    count, rows, half = own_ref.shape[0], shard_ref.shape[0], half_ref.shape[0]
    goal = shard_ref.at[pl.ds(0, count)]
    copy = pltpu.make_async_copy(own_ref, goal, sem)
    either(core == layer, lambda: copy, lambda: pltpu.make_async_copy(other_ref, goal, sem))
    if extra:
        shard_ref[count:] = extra[0][...]
    copy.wait()

    @pl.when(core == 0)
    def _():
        half_ref[...] = shard_ref[:half]

    @pl.when(core == 1)
    def _():
        half_ref[...] = shard_ref[rows - half :]


def pick(layer, own, other, *extra):
    rows, width = own.shape[0] + sum(value.shape[0] for value in extra), own.shape[1]
    return launch(
        functools.partial(pick_kernel, layer), (own, other, *extra), name="pick", micros=1.5,
        in_specs=[ANY] * 2 + [VMEM] * len(extra), out_specs=[VMEM] * 2,
        out_shape=[array((rows, width)), array((half_of(rows), width))],
        scratch=[pltpu.SemaphoreType.DMA],
    )


def line_kernel(own_ref, near_ref, other_ref, far_ref, far_other_ref, keep_ref, pass_ref, sems):
    core, z = lax.axis_index("section"), lax.axis_index("z")
    depth = 4
    rows, half = own_ref.shape[0], far_ref.shape[0]
    below, above, far = lax.rem(z + depth - 1, depth), lax.rem(z + 1, depth), lax.rem(z + 2, depth)
    near_at, other_at = jnp.where(core == 0, below, above), jnp.where(core == 0, above, below)
    rest = rows - half
    first, second = pl.multiple_of(core * rest, 16), pl.multiple_of((1 - core) * half, 16)
    skipped = pl.multiple_of((1 - core) * (half - rest), 16)
    moves = (
        (own_ref, z, pl.ds(0, rows)),
        (near_ref, near_at, pl.ds(0, rows)),
        (other_ref, other_at, pl.ds(0, rows)),
        (far_ref, far, pl.ds(first, half)),
        (far_other_ref.at[pl.ds(skipped, rest)], far, pl.ds(second, rest)),
    )
    copies = []
    for at, (source, slot, part) in enumerate(moves):
        index = lax.rem(slot, 2)
        kept = pltpu.make_async_copy(source, keep_ref.at[index, part], sems.at[at])
        passed = pltpu.make_async_copy(source, pass_ref.at[index, part], sems.at[at])
        either(slot // 2 == core, lambda: kept, lambda: passed)
        copies.append(kept)
    for copy in copies:
        copy.wait()


def line_of(own, near, near_other, far, far_other):
    rows, width = own.shape
    return launch(
        line_kernel, (own, near, near_other, far, far_other), name="line", micros=2.5,
        in_specs=[ANY] * 5, out_specs=[VMEM] * 2, out_shape=[array((2, rows, width))] * 2,
        scratch=[pltpu.SemaphoreType.DMA((5,))],
    )


def piece_copies(pieces, target, sems, rows):
    line_keep, line_pass, side_keep, side_pass, turn_keep, turn_pass, corner, corner_other = pieces
    core, _, y, x = place()
    high, wide = 2, 2
    take = pl.ds(0, rows)
    side_y, side_x = jnp.where(core == 0, y, 1 - y), jnp.where(core == 0, 1 - x, x)
    copies = []
    for slot in range(4):
        lines = (
            (line_keep, line_pass, core, y, x),
            (side_keep, side_pass, core, side_y, side_x),
            (turn_keep, turn_pass, 1 - core, 1 - side_y, 1 - side_x),
            (corner_other, corner, core, 1 - y, 1 - x),
        )
        for at, (keep, passed, owner, line_y, line_x) in enumerate(lines):
            start = pl.multiple_of(((slot * high + line_y) * wide + line_x) * rows, 8)
            goal = target.at[pl.ds(start, rows)]
            copies.append(slot_copy(slot, keep, passed, owner, goal, sems.at[4 * slot + at], take))
    return copies


def rows_copy(low_ref, high_ref, start, count, target_ref, at, sem, crossing):
    split = low_ref.shape[0]
    goal = target_ref.at[pl.ds(at, count)]
    copy = pltpu.make_async_copy(low_ref.at[pl.ds(0, count)], goal, sem)

    @pl.when(start + count <= split)
    def _():
        pltpu.make_async_copy(low_ref.at[pl.ds(pl.multiple_of(start, 16), count)], goal, sem).start()

    @pl.when(start >= split)
    def _():
        pltpu.make_async_copy(high_ref.at[pl.ds(pl.multiple_of(start - split, 16), count)], goal, sem).start()

    for first in crossing:
        if first < split < first + count:
            low = split - first

            @pl.when(start == first)
            def _():
                pltpu.make_async_copy(low_ref.at[pl.ds(first, low)], target_ref.at[pl.ds(at, low)], sem).start()
                rest = target_ref.at[pl.ds(at + low, count - low)]
                pltpu.make_async_copy(high_ref.at[pl.ds(0, count - low)], rest, sem).start()

    return copy


def partial_kernel(
    fine, own_low, own_high, other_low, other_high, right_ref, right_other_ref,
    turn_any, keep_any, pass_any, near_any, half_any, turn_ref, keep_ref, pass_ref, near_ref, half_ref, left_ref, sems,
    out_sems,
):
    core, z, y, x = place()
    depth, high, wide = fine[1:]
    outs = [
        pltpu.make_async_copy(source, goal, out_sems.at[at])
        for at, (source, goal) in enumerate(
            ((turn_ref, turn_any), (keep_ref, keep_any), (pass_ref, pass_any), (near_ref, near_any), (half_ref, half_any))
        )
    ]
    split = own_low.shape[0]
    rows = keep_ref.shape[1]
    half = half_ref.shape[1]
    step = pl.program_id(0)
    side_y, side_x = jnp.where(core == 0, y, 1 - y), jnp.where(core == 0, 1 - x, x)
    near, far = lax.rem(z + jnp.where(core == 0, 1, depth - 1), depth), lax.rem(z + 2, depth)
    whole_at = (split // rows) * rows
    crossing = (whole_at, whole_at + rows - half)

    def row(slot, line_y, line_x):
        return ((slot * high + line_y) * wide + line_x) * rows

    kept, passed = 2 * core, 2 - 2 * core
    parts = [(row(passed + at, 1 - y, 1 - x), rows) for at in range(2)]
    parts += [(row(kept + at, side_y, side_x), rows) for at in range(2)]
    parts += [(row(passed + at, side_y, side_x), rows) for at in range(2)]
    parts += [(row(near, y, x), rows)]
    parts += [(row(slot, y, x) + core * (rows - half), half) for slot in (z, far)]
    sides = ((own_low, own_high), (other_low, other_high))

    def copies():
        at = 0
        for index, (start, count) in enumerate(parts):
            for side, (low, up) in enumerate(sides):
                yield index, low, up, start, count, left_ref.at[side], at, sems.at[side, index]
            at += count

    @pl.when(step == 0)
    def _():
        for _, *what in copies():
            rows_copy(*what, crossing)

    def wait(indices):
        for index, low, _, _, count, target, at, sem in copies():
            if index in indices:
                pltpu.make_async_copy(low.at[pl.ds(0, count)], target.at[pl.ds(at, count)], sem).wait()

    def product(first, count):
        own = nn(left_ref[0, first : first + count], right_ref[...])
        return (own + nn(left_ref[1, first : first + count], right_other_ref[...])).astype(BF16)

    for at, out in enumerate((turn_ref, keep_ref, pass_ref)):

        @pl.when(step == at)
        def _():
            wait((2 * at, 2 * at + 1))
            out[...] = product(2 * at * rows, 2 * rows).reshape(out.shape)
            outs[at].start()

    @pl.when(step == 3)
    def _():
        wait((6, 7, 8))
        last = product(6 * rows, rows + 2 * half)
        near_ref[...] = last[:rows]
        half_ref[...] = last[rows:].reshape(half_ref.shape)
        outs[3].start()
        outs[4].start()
        for copy in outs:
            copy.wait()


def partial(fine, own_low, own_high, other_low, other_high, right, right_other):
    length, width = right.shape
    features = own_low.shape[0] + own_high.shape[0]
    rows = features // (fine[1] * fine[2] * fine[3])
    half = half_of(rows)
    shapes = [(2, rows, width)] * 3 + [(rows, width), (2, half, width)]
    return launch(
        functools.partial(partial_kernel, fine), (own_low, own_high, other_low, other_high, right, right_other),
        name="partial", micros=features / 700, grid=(4,),
        in_specs=[ANY] * 4 + [whole(length, width)] * 2,
        out_specs=[ANY] * 5,
        out_shape=[array(shape) for shape in shapes],
        scratch=[
            *[pltpu.VMEM(shape, BF16) for shape in shapes],
            pltpu.VMEM((2, 7 * rows + 2 * half, length), BF16),
            pltpu.SemaphoreType.DMA((2, 9)),
            pltpu.SemaphoreType.DMA((5,)),
        ],
    )


def depth_kernel(
    near_ref, half_ref, keep_ref, pass_ref, keep_other, pass_other,
    near_out, far_out, own_out, near_got, half_got, sems,
):
    core, z = lax.axis_index("section"), lax.axis_index("z")
    depth = 4
    half = half_ref.shape[1]
    near = lax.rem(z + jnp.where(core == 0, 1, depth - 1), depth)
    part = pl.ds(pl.multiple_of(core * (near_ref.shape[0] - half), 16), half)
    copies = []
    for at, (keep, pass_, owner) in enumerate(((keep_ref, pass_ref, core), (keep_other, pass_other, 1 - core))):
        copies.append(slot_copy(near, keep, pass_, owner, near_got.at[at], sems.at[3 * at]))
        for index, slot in enumerate((z, lax.rem(z + 2, depth))):
            copies.append(slot_copy(slot, keep, pass_, owner, half_got.at[at, index], sems.at[3 * at + 1 + index], part))
    for copy in copies:
        copy.wait()
    near_total = near_ref[...].astype(F32) + near_got[0].astype(F32) + near_got[1].astype(F32)
    near_out[...] = near_total.astype(BF16)
    for index, out in enumerate((own_out, far_out)):
        total = half_ref[index].astype(F32) + half_got[0, index].astype(F32) + half_got[1, index].astype(F32)
        out[...] = total.astype(BF16)


def depth_sums(near, halves, keep, passed, keep_other, passed_other):
    rows, width = near.shape
    half = halves.shape[1]
    return launch(
        depth_kernel, (near, halves, keep, passed, keep_other, passed_other), name="depth", micros=2,
        in_specs=[VMEM] * 2 + [ANY] * 4, out_specs=[VMEM] * 3,
        out_shape=[array((rows, width)), array((half, width)), array((half, width))],
        scratch=[
            pltpu.VMEM((2, rows, width), BF16),
            pltpu.VMEM((2, 2, half, width), BF16),
            pltpu.SemaphoreType.DMA((6,)),
        ],
    )


def total_kernel(near_ref, near_other, far_ref, far_other, own_ref, own_other, *refs):
    second, out_ref = refs[:-1], refs[-1]
    core = lax.axis_index("section")
    rows, half = near_ref.shape[0], far_ref.shape[0]
    near = near_ref[...].astype(F32) + near_other[...].astype(F32)
    mine = far_ref[...].astype(F32) + own_ref[...].astype(F32)
    other = far_other[...].astype(F32) + own_other[...].astype(F32)
    low, high = jnp.where(core == 0, mine, other), jnp.where(core == 0, other, mine)
    out_ref[:half] = near[:half] + low
    out_ref[half:] = near[half:] + high[2 * half - rows :]
    if second:

        @pl.when(core == 1)
        def _():
            out_ref[...] = second[0][...]


def total(near, near_other, far, far_other, own, own_other, *second):
    values = (near, near_other, far, far_other, own, own_other, *second)
    return launch(
        total_kernel, values, name="total", micros=1.5,
        in_specs=[VMEM] * len(values), out_specs=VMEM, out_shape=array(near.shape, F32),
    )


class Order:
    def __init__(self, first):
        self.last = first
        self.moving = []

    def run(self, function, *values):
        values, _ = lax.optimization_barrier((values, self.last))
        return self.fence(function(*values))

    def fence(self, *result):
        due = [value for value, left in self.moving if left == 0]
        self.moving = [(value, left - 1) for value, left in self.moving if left > 0]
        result, self.last, _ = lax.optimization_barrier((result, self.last, due))
        if result:
            self.last = jax.tree.leaves(result)[0]
            return result[0]

    def move(self, way, *values, count=1):
        values, _ = lax.optimization_barrier((values, self.last))
        moved = [way(value) for value in values]
        self.moving += [(value, count - 1) for value in moved]
        return moved if len(values) > 1 else moved[0]

    def swap(self, *values, count=1):
        return self.move(swap, *values, count=count)


def total_along(value, axis, size):
    return sum([lax.ppermute(value, axis, [(i, (i + k) % size) for i in range(size)]) for k in range(1, size)], value)


def total_of(value, fine):
    for axis, size in zip(ALL, fine):
        value = total_along(value, axis, size) if size < 8 else lax.psum(value, axis)
    return value


def added(first, second):
    return (first.astype(F32) + second.astype(F32)).astype(BF16)


class Gather:
    def __init__(self, order, fine, shard, half):
        self.order, self.fine, self.shard, self.half = order, fine, shard, half

    def along(self, count=1):
        self.near = self.order.move(functools.partial(along, fine=self.fine), self.shard, count=count)
        self.far = self.order.move(functools.partial(opposite, fine=self.fine), self.half, count=count)

    def across(self, count=1):
        self.near_other, self.far_other = self.order.swap(self.near, self.far, count=count)

    def line(self):
        self.keep, self.passed = self.order.run(
            line_of, self.shard, self.near, self.near_other, self.far, self.far_other
        )

    def side(self, count=1):
        self.side_passed = self.order.move(functools.partial(sideways, fine=self.fine), self.passed, count=count)
        self.side_keep = self.order.move(functools.partial(sideways, fine=self.fine), self.keep, count=count)

    def turn(self, count=1):
        self.corner = self.order.move(functools.partial(turned, fine=self.fine), self.side_passed, count=count)

    def rest(self, count=1):
        self.turn_keep, self.turn_passed = self.order.swap(self.side_keep, self.side_passed, count=count)

    def meet(self):
        self.corner_other = self.order.swap(self.corner)

    def pieces(self):
        return (
            self.keep, self.passed, self.side_keep, self.side_passed, self.turn_keep, self.turn_passed,
            self.corner, self.corner_other,
        )


class Scatter:
    def __init__(self, order, fine, values):
        self.order, self.fine = order, fine
        self.turn, self.keep, self.passed, self.near, self.halves = values

    def start(self, count=1):
        self.turn = self.order.move(functools.partial(turned, fine=self.fine), self.turn, count=count)
        self.keep = self.order.move(functools.partial(sideways, fine=self.fine), self.keep, count=count)

    def add(self):
        self.passed = self.order.run(added, self.passed, self.turn)

    def pass_on(self):
        self.passed = self.order.move(functools.partial(sideways, fine=self.fine), self.passed)

    def keep_across(self):
        self.keep_other = self.order.swap(self.keep)

    def meet(self):
        self.passed_other = self.order.swap(self.passed)

    def parts(self):
        return self.near, self.halves, self.keep, self.passed, self.keep_other, self.passed_other

    def along(self, values, count=1):
        near, far, self.own = values
        self.near = self.order.move(functools.partial(along, fine=self.fine), near, count=count)
        self.far = self.order.move(functools.partial(opposite, fine=self.fine), far, count=count)

    def own_across(self):
        self.own_other = self.order.swap(self.own)

    def across(self):
        self.near_other, self.far_other = self.order.swap(self.near, self.far)

    def ends(self):
        return self.near, self.near_other, self.far, self.far_other, self.own, self.own_other


def body(fine, inputs, cotangent, lengths, weight_in, weight_out, scales):
    length, width = inputs.shape[2], inputs.shape[3]
    core, z, y, x = place()
    depth = fine[1]
    device = (z * fine[2] + y) * fine[3] + x
    pair = lax.dynamic_index_in_dim(lengths, core, 0, False)
    scale_count = scales.shape[1]
    whole_scales = scale_count * depth * fine[2] * fine[3]
    by_core = lambda first, second: (jnp.where(core == 0, first, second), jnp.where(core == 0, second, first))

    shift = lambda axis: lambda value: lax.ppermute(value, axis, [(0, 1), (1, 0)])
    spread = lambda mine, other: jnp.stack(by_core(mine, other))[None, :, None]
    chip = functools.partial(partial, fine)

    def padded(flat):
        return jnp.pad(flat, (0, -flat.shape[0] % 1024)).reshape(-1, 128)

    own_scales = lax.dynamic_update_slice(
        jnp.zeros((2 * whole_scales,), F32), scales[0].astype(F32), (core * whole_scales + device * scale_count,)
    )
    scale = padded(own_scales)

    def vectors_of(scale):
        scale = scale.reshape(-1)[: 2 * whole_scales].reshape(2, whole_scales)
        return [(s[None, :width], s[width : width + HEAD, None], s[width + HEAD :, None]) for s in scale]

    def own_rows(inputs, cotangent):
        rows = lax.dynamic_index_in_dim(inputs, core, 0, False)[0]
        grad = lax.dynamic_index_in_dim(cotangent, core, 0, False)[0]
        position = lax.broadcasted_iota(jnp.int32, (length, 1), 0)
        return rows, jnp.where(position < pair[0, 0] + pair[0, 1], grad, jnp.zeros_like(grad))

    order = Order(scale)
    butterfly = lambda by: lambda value: lax.ppermute(value, "z", [(i, i ^ by) for i in range(depth)])
    out = functools.partial(output, pair)
    if depth == 4:
        in_rows, out_rows = weight_in.shape[1], weight_out.shape[1]
        gather = lambda values: Gather(order, fine, *values)
        other_in, other_out, got = order.swap(weight_in[0], weight_out[0], scale)
        order.fence()
        first = gather(order.run(functools.partial(pick, 0), weight_in[0], other_in))
        first.along()
        scale = scale + got
        got = order.move(shift("x"), scale)
        order.fence()
        first.across()
        scale = scale + got
        got = order.move(shift("y"), scale)
        second = gather(order.run(functools.partial(pick, 0), weight_out[0], other_out))
        first.line()
        first.side()
        second.along()
        third, fourth, (rows_0, grad_1) = order.run(
            lambda own_in, other_in, own_out, other_out, *values: (
                pick(1, own_in, other_in), pick(1, own_out, other_out), own_rows(*values)
            ),
            weight_in[0], other_in, weight_out[0], other_out, inputs, cotangent,
        )
        third, fourth = gather(third), gather(fourth)
        first.turn(count=3)
        second.across()
        first.rest(count=2)
        scale = scale + got
        got = order.move(butterfly(1), scale, count=2)
        order.fence()
        second.line()
        scale = scale + got
        got = order.move(butterfly(2), scale)
        order.fence()
        vectors_0, vectors_1 = order.run(vectors_of, scale + got)
        second.side(count=2)
        third.along(count=2)
        first.meet()
        order.fence()
        front, out = functools.partial(attend, in_rows, pair), functools.partial(output, pair, out_rows)
        normed_0, raw_0, value_0, attended_0, logs_0, weight_in_0 = order.run(front, rows_0, *vectors_0, *first.pieces())
        second.turn()
        second.rest()
        third.across()
        hidden_0, slope_0 = order.run(hidden, normed_0, weight_in_0)
        second.meet()
        third.line()
        third.side()
        fourth.along()
        rows_1, squares_0, weight_out_0 = order.run(out, rows_0, attended_0, hidden_0, *second.pieces())
        third.turn(count=3)
        fourth.across()
        third.rest(count=2)
        order.fence()
        fourth.line()
        grad_1_other = order.swap(grad_1)
        order.fence()
        fourth.side(count=2)
        third.meet()
        order.fence()
        attended_0_other, normed_0_other, hidden_0_other = order.swap(attended_0, normed_0, hidden_0)
        normed_1, raw_1, value_1, attended_1, logs_1, weight_in_1 = order.run(front, rows_1, *vectors_1, *third.pieces())
        fourth.turn()
        fourth.rest()
        attended_1_other, normed_1_other = order.swap(attended_1, normed_1)
        hidden_1, slope_1 = order.run(hidden, normed_1, weight_in_1)
        fourth.meet()
        order.fence()
        hidden_1_other, rows_1_other = order.swap(hidden_1, rows_1)
        feed_1, low_1, weight_out_1 = order.run(
            functools.partial(feed_back, out_rows), grad_1, slope_1, weight_in_1, *fourth.pieces()
        )
    else:
        weight_in_0, weight_in_1 = jnp.split(lax.all_gather(weight_in[0], ALL, axis=0, tiled=True), 2)
        weight_out_0, weight_out_1 = jnp.split(lax.all_gather(weight_out[0], ALL, axis=0, tiled=True), 2)
        vectors_0, vectors_1 = vectors_of(total_of(scale, fine))
        rows_0, grad_1 = own_rows(inputs, cotangent)
        front, out = functools.partial(attend, None, pair), functools.partial(output, pair, None)
        normed_0, raw_0, value_0, attended_0, logs_0 = order.run(front, rows_0, *vectors_0, weight_in_0)
        hidden_0, slope_0 = order.run(hidden, normed_0, weight_in_0)
        rows_1, squares_0 = order.run(out, rows_0, attended_0, hidden_0, weight_out_0)
        normed_1, raw_1, value_1, attended_1, logs_1 = order.run(front, rows_1, *vectors_1, weight_in_1)
        hidden_1, slope_1 = order.run(hidden, normed_1, weight_in_1)
        feed_1, low_1 = order.run(functools.partial(feed_back, None), grad_1, slope_1, weight_in_1, weight_out_1)
    out, back, feed = functools.partial(output, pair, None), functools.partial(attend_back, pair), functools.partial(feed_back, None)
    kept_1 = (rows_1, grad_1, *vectors_1, raw_1, value_1, attended_1, logs_1, weight_out_1, weight_in_1)

    def small_sums(squares_0, squares_1, gain_0, heads_0, gain_1, heads_1):
        sums = [jnp.sum(squares, axis=(1, 2)) for squares in (squares_0, squares_1)]
        scale_grads = [
            jnp.concatenate([jnp.sum(gain, axis=0), jnp.sum(heads, axis=2).reshape(-1)])
            for gain, heads in ((gain_0, heads_0), (gain_1, heads_1))
        ]
        return padded(jnp.concatenate([jnp.sum(pair).astype(F32)[None], *sums, *scale_grads]))

    if depth == 4:
        low_1_other = order.swap(low_1)
        out_1 = Scatter(order, fine, order.run(
            chip, attended_1, hidden_1, attended_1_other, hidden_1_other, grad_1, grad_1_other
        ))
        out_1.start()
        top_1, grad_0, gain_1, heads_1 = order.run(back, *kept_1, feed_1)
        grad_0_other = order.swap(grad_0)
        top_1_other = order.swap(top_1, count=3)
        out_1.add()
        out_1.pass_on()
        out_1.keep_across()
        out_0 = Scatter(order, fine, order.run(
            chip, attended_0, hidden_0, attended_0_other, hidden_0_other, grad_0, grad_0_other
        ))
        out_0.start()
        out_1.meet()
        feed_0, low_0 = order.run(feed, grad_0, slope_0, weight_in_0, weight_out_0)
        out_0.add()
        out_0.pass_on()
        out_0.keep_across()
        low_0_other = order.swap(low_0)
        in_1, ends = order.run(
            lambda values, parts: (chip(*values), depth_sums(*parts)),
            (top_1, low_1, top_1_other, low_1_other, normed_1, normed_1_other), out_1.parts(),
        )
        in_1 = Scatter(order, fine, in_1)
        in_1.start()
        out_1.along(ends)
        out_0.meet()
        kept_0 = (rows_0, grad_0, *vectors_0, raw_0, value_0, attended_0, logs_0, weight_out_0, weight_in_0)
        top_0, grad_first, gain_0, heads_0 = order.run(back, *kept_0, feed_0)
        top_0_other = order.swap(top_0)
        ends, in_1.passed = order.run(
            lambda parts, first, second: (depth_sums(*parts), added(first, second)), out_0.parts(), in_1.passed, in_1.turn
        )
        in_1.pass_on()
        out_0.along(ends)
        in_1.keep_across()
        out_0.own_across()
        in_0 = Scatter(order, fine, order.run(chip, top_0, low_0, top_0_other, low_0_other, normed_0, normed_0_other))
        in_1.meet()
        out_1.across()
        order.fence()
        ends = order.run(depth_sums, *in_1.parts())
        in_0.start()
        in_1.along(ends)
        out_1.own_across()
        grad_first_other = order.swap(grad_first)

        def last_output(values, squares_0, *others):
            result, squares = out(*values)
            return result, small_sums(squares_0, squares, *others)

        result_1, small = order.run(
            last_output, (rows_1, attended_1, hidden_1, weight_out_1), squares_0, gain_0, heads_0, gain_1, heads_1
        )
        in_0.add()
        in_0.pass_on()
        in_0.keep_across()
        out_0.across()
        got = order.move(shift("x"), small)
        out_grad_1 = order.run(total, *out_1.ends())
        small = small + got
        in_0.meet()
        order.fence()
        got = order.move(shift("y"), small)
        result_1_other = order.swap(result_1)
        in_1.across()
        in_1.own_across()
        ends = order.run(depth_sums, *in_0.parts())
        in_0.along(ends)
        small = small + got
        got = order.move(butterfly(1), small)
        in_0.own_across()
        def spread_both(rows_1, rows_other, result, result_other, first, first_other, grad_0, grad_other):
            outputs = jnp.where(core == 0, rows_1, result), jnp.where(core == 0, rows_other, result_other)
            grads = jnp.where(core == 0, first, grad_0), jnp.where(core == 0, first_other, grad_other)
            return spread(*outputs), spread(*grads)

        out_grad, in_grad_1, (outputs, input_grads) = order.run(
            lambda first, second, values: (total(*first), total(*second), spread_both(*values)),
            (*out_0.ends(), out_grad_1), in_1.ends(),
            (rows_1, rows_1_other, result_1, result_1_other, grad_first, grad_first_other, grad_0, grad_0_other),
        )
        in_0.across()
        small = small + got
        got = order.move(butterfly(2), small)
        order.fence()
        small = small + got
        got = order.swap(small)
        in_grad = order.run(total, *in_0.ends(), in_grad_1)[None]
        out_grad = out_grad[None]
        small = small + got
    else:
        top_1, grad_0, gain_1, heads_1 = order.run(back, *kept_1, feed_1)
        feed_0, low_0 = order.run(feed, grad_0, slope_0, weight_in_0, weight_out_0)
        kept_0 = (rows_0, grad_0, *vectors_0, raw_0, value_0, attended_0, logs_0, weight_out_0, weight_in_0)
        top_0, grad_first, gain_0, heads_0 = order.run(back, *kept_0, feed_0)
        result_1, squares_1 = order.run(out, rows_1, attended_1, hidden_1, weight_out_1)
        own = lambda low, high, right: nn(jnp.concatenate([low, high]), right).astype(BF16)
        summed = lambda first, second: lax.psum_scatter(
            jnp.concatenate([first, second]), ALL, scatter_dimension=0, tiled=True
        ).astype(F32)[None]
        in_grad = summed(own(top_0, low_0, normed_0), own(top_1, low_1, normed_1))
        out_grad = summed(own(attended_0, hidden_0, grad_0), own(attended_1, hidden_1, grad_1))
        small = small_sums(squares_0, squares_1, gain_0, heads_0, gain_1, heads_1)
        for axis in ALL:
            small = lax.psum(small, axis)
        outputs, input_grads = [
            spread(mine, swap(given)) for mine, given in (by_core(rows_1, result_1), by_core(grad_first, grad_0))
        ]
    small = small.reshape(-1)
    statistics = jnp.sqrt(lax.dynamic_slice(small, (1 + 3 * core,), (3,)) / (small[0] * width))
    scale_grad = lax.dynamic_slice(small, (7 + core * whole_scales + device * scale_count,), (scale_count,))
    return outputs, input_grads, in_grad, out_grad, scale_grad[None], statistics[None]


def solution(mesh):
    count = mesh.shape["dp"]
    fine = Mesh(mesh.devices.reshape(2, count // 4, 2, 2), ALL)
    return jax.shard_map(
        functools.partial(body, (2, count // 4, 2, 2)),
        mesh=fine,
        in_specs=(
            P(None, DP, None, None),
            P(None, DP, None, None),
            P(None, DP, None),
            P("section", DP, None),
            P("section", DP, None),
            P("section", DP),
        ),
        out_specs=(
            P("section", None, DP, None, None),
            P("section", None, DP, None, None),
            P("section", DP, None),
            P("section", DP, None),
            P("section", DP),
            P("section", None),
        ),
        check_vma=False,
    )
```

```python
import functools

import jax
import jax.numpy as jnp
from jax import lax
from jax.experimental import pallas as pl
from jax.experimental.pallas import tpu as pltpu
from jax.sharding import Mesh, PartitionSpec as P

HEADS = 12
HEAD = 64
GROUP = 4
GROUPS = HEADS // GROUP
LANES = GROUP * HEAD
EPSILON = 1e-06
MASKED = -1e30
FACTOR = HEAD**-0.5
F32 = jnp.float32
BF16 = jnp.bfloat16
DP = ("z", "y", "x")
ALL = ("section",) + DP
VMEM_MIB = 60
ANY = pl.BlockSpec(memory_space=pl.ANY)
VMEM = pl.BlockSpec(memory_space=pltpu.VMEM)


def nn(left, right):
    return lax.dot_general(left, right, (((1,), (0,)), ((), ())), preferred_element_type=F32)


def nt(left, right):
    return lax.dot_general(left, right, (((1,), (1,)), ((), ())), preferred_element_type=F32)


def tn(left, right):
    return lax.dot_general(left, right, (((0,), (0,)), ((), ())), preferred_element_type=F32)


def launch(kernel, values, *, name, micros, grid=(), in_specs, out_specs, out_shape, scratch=()):
    return pl.pallas_call(
        kernel,
        grid=grid,
        in_specs=in_specs,
        out_specs=out_specs,
        out_shape=out_shape,
        scratch_shapes=scratch,
        cost_estimate=pl.CostEstimate(flops=int(micros * 1150000000.0), bytes_accessed=int(micros * 1000000.0), transcendentals=0),
        compiler_params=pltpu.CompilerParams(
            vmem_limit_bytes=VMEM_MIB * 1024 * 1024, dimension_semantics=("arbitrary",) * len(grid)
        ),
        name=name,
    )(*values)


def array(shape, dtype=BF16):
    return jax.ShapeDtypeStruct(shape, dtype)


def row_norm(rows):
    average = jnp.mean(rows, axis=1, keepdims=True)
    centred = rows - average
    inverse = lax.rsqrt(jnp.mean(centred * centred, axis=1, keepdims=True) + EPSILON)
    return centred * inverse, inverse


def column_norm(columns):
    average = jnp.mean(columns, axis=0, keepdims=True)
    centred = columns - average
    inverse = lax.rsqrt(jnp.mean(centred * centred, axis=0, keepdims=True) + EPSILON)
    return centred * inverse, inverse


def norm_back(normal, inverse, grad, scale, axis):
    scaled = grad * scale
    average = jnp.mean(scaled, axis=axis, keepdims=True)
    along_normal = jnp.mean(scaled * normal, axis=axis, keepdims=True)
    return inverse * (scaled - average - normal * along_normal)


def segment_at(pair_ref, position):
    first_end = pair_ref[0, 0]
    second_end = first_end + pair_ref[0, 1]
    return (position >= first_end).astype(jnp.int32) + (position >= second_end).astype(jnp.int32)


def fill_bias(pair_ref, bias_ref):
    length = bias_ref.shape[0]
    down = segment_at(pair_ref, lax.broadcasted_iota(jnp.int32, (length, length), 0))
    sideways = segment_at(pair_ref, lax.broadcasted_iota(jnp.int32, (length, length), 1))
    bias_ref[...] = jnp.where(down == sideways, 0.0, MASKED).astype(F32)


def whole(*shape):
    return pl.BlockSpec(shape, lambda *_: (0,) * len(shape))


def attend_kernel(in_rows, pair_ref, rows_ref, gain_ref, query_scale_ref, key_scale_ref, *refs):
    step = pl.program_id(0)
    if in_rows is None:
        weight_ref, normed_ref, raw_ref, value_ref, attended_ref, log_ref, bias_ref = refs
        weight = weight_ref[...].reshape(3 * LANES, rows_ref.shape[1])
    else:
        pieces, refs = refs[:8], refs[8:]
        normed_ref, raw_ref, value_ref, attended_ref, log_ref, full_ref, bias_ref, weight_ref, sems, full_sems = refs
        load_weight(step, pieces, weight_ref, sems, in_rows, full_ref, full_sems, (0, 0, 1, 1))
        starts = [pl.multiple_of(rows_ref.shape[1] * third + LANES * step, LANES) for third in range(3)]
        weight = jnp.concatenate([weight_ref[pl.ds(start, LANES)] for start in starts])

    @pl.when(step == 0)
    def _():
        normal, _ = row_norm(rows_ref[...].astype(F32))
        normed_ref[...] = (normal * gain_ref[...]).astype(BF16)
        fill_bias(pair_ref, bias_ref)

    normed = normed_ref[...]
    projected = nt(weight, normed)
    raw_ref[...] = projected[: 2 * LANES].reshape(raw_ref.shape)
    value_ref[...] = projected[2 * LANES :].astype(BF16)
    for head in range(GROUP):
        at = slice(head * HEAD, (head + 1) * HEAD)
        query = column_norm(projected[:LANES][at])[0] * query_scale_ref[...]
        query = query.astype(BF16) * BF16(FACTOR)
        key = (column_norm(projected[LANES : 2 * LANES][at])[0] * key_scale_ref[...]).astype(BF16)
        scores = tn(key, query) + bias_ref[...]
        peak = jnp.max(scores, axis=0, keepdims=True)
        exponent = jnp.exp(scores - peak)
        total = jnp.sum(exponent, axis=0, keepdims=True)
        attended = nn(value_ref[at, :], exponent.astype(BF16)) * (1.0 / total)
        attended_ref[at, :] = attended.astype(BF16)
        log_ref[0, head : head + 1, :] = peak + jnp.log(total)


def attend(in_rows, pair, rows, gain, query_scale, key_scale, *weights):
    length, width = rows.shape
    gathered = in_rows is not None
    features = 16 * in_rows if gathered else weights[0].shape[0]
    if not gathered:
        weights = (weights[0].reshape(-1, GROUPS, LANES, width),)
    return launch(
        functools.partial(attend_kernel, in_rows),
        (pair, rows, gain, query_scale, key_scale, *weights),
        name="attend",
        micros=13,
        grid=(GROUPS,),
        in_specs=[
            pl.BlockSpec(memory_space=pltpu.SMEM),
            whole(length, width),
            whole(1, width),
            whole(HEAD, 1),
            whole(HEAD, 1),
            *([ANY] * 8 if gathered else [pl.BlockSpec((3, 1, LANES, width), lambda g: (0, g, 0, 0))]),
        ],
        out_specs=[
            whole(length, width),
            pl.BlockSpec((2, 1, LANES, length), lambda g: (0, g, 0, 0)),
            pl.BlockSpec((LANES, length), lambda g: (g, 0)),
            pl.BlockSpec((LANES, length), lambda g: (g, 0)),
            pl.BlockSpec((1, 8, length), lambda g: (g, 0, 0)),
            *[ANY] * gathered,
        ],
        out_shape=[
            array((length, width)),
            array((2, GROUPS, LANES, length), F32),
            array((width, length)),
            array((width, length)),
            array((GROUPS, 8, length), F32),
            *[array((features, width))] * gathered,
        ],
        scratch=[
            pltpu.VMEM((length, length), F32),
            *(weight_scratch(features, width) if gathered else ()),
        ],
    )


def hidden_kernel(normed_ref, weight_ref, hidden_ref, slope_ref):
    feed = nt(weight_ref[...], normed_ref[...])
    half = 0.5 * lax.erf(feed * (0.5**0.5)) + 0.5
    hidden_ref[...] = (feed * half).astype(BF16)
    density = jnp.exp(feed * feed * -0.5) * ((2.0 * jnp.pi) ** -0.5)
    slope_ref[...] = (half + feed * density).astype(BF16)


def hidden(normed, weight_in):
    length, width = normed.shape
    count = weight_in.shape[0] // width - 3
    return launch(
        hidden_kernel,
        (normed, weight_in),
        name="hidden",
        micros=8,
        grid=(count,),
        in_specs=[whole(length, width), pl.BlockSpec((width, width), lambda i: (i + 3, 0))],
        out_specs=[pl.BlockSpec((width, length), lambda i: (i, 0))] * 2,
        out_shape=[array((count * width, length))] * 2,
    )


def load_weight(step, pieces, target, sems, rows, full_ref, full_sems, steps):
    @pl.when(step == 0)
    def _():
        piece_copies(pieces, target, sems, rows)

    size = 4 * rows
    out = [
        pltpu.make_async_copy(target.at[pl.ds(size * slot, size)], full_ref.at[pl.ds(size * slot, size)], full_sems.at[slot])
        for slot in range(4)
    ]
    for slot in range(4):

        @pl.when(step == steps[slot])
        def _():
            for at in range(4):
                goal = target.at[pl.ds(size * slot + rows * at, rows)]
                pltpu.make_async_copy(pieces[0].at[0, pl.ds(0, rows)], goal, sems.at[4 * slot + at]).wait()
            out[slot].start()

    @pl.when(step == pl.num_programs(0) - 1)
    def _():
        for copy in out:
            copy.wait()


def output_kernel(out_rows, pair_ref, rows_ref, attended_ref, hidden_ref, *refs):
    step, last = pl.program_id(0), pl.num_programs(0) - 1
    width = rows_ref.shape[1]
    if out_rows is None:
        weight_ref, result_ref, sums_ref, attend_ref, feed_ref = refs
        weight = weight_ref[...]
    else:
        pieces, (result_ref, sums_ref, full_ref, attend_ref, feed_ref, all_ref, sems, full_sems) = refs[:8], refs[8:]
        load_weight(step, pieces, all_ref, sems, out_rows, full_ref, full_sems, (0, 1, 2, 3))
        weight = all_ref[pl.ds(pl.multiple_of(step * width, width), width)]

    @pl.when(step == 0)
    def _():
        attend_ref[...] = tn(attended_ref[...], weight)

    @pl.when(step == 1)
    def _():
        feed_ref[...] = tn(hidden_ref[...], weight)

    @pl.when(step > 1)
    def _():
        feed_ref[...] += tn(hidden_ref[...], weight)

    @pl.when(step == last)
    def _():
        length = attend_ref.shape[0]
        position = lax.broadcasted_iota(jnp.int32, (length, 1), 0)
        valid = (segment_at(pair_ref, position) < 2).astype(F32)
        branch, feed = attend_ref[...], feed_ref[...]
        result = rows_ref[...].astype(F32) + branch + feed
        result_ref[...] = result.astype(BF16)
        for at, value in enumerate((result, branch, feed)):
            squares = (value * value * valid).reshape(length // 8, 8, width)
            sums_ref[at] = jnp.sum(squares, axis=0)


def weight_scratch(features, width):
    return [pltpu.VMEM((features, width), BF16), pltpu.SemaphoreType.DMA((16,)), pltpu.SemaphoreType.DMA((4,))]


def output(pair, out_rows, rows, attended, hid, *weights):
    length, width = rows.shape
    features = hid.shape[0] + width
    count = features // width
    gathered = out_rows is not None
    return launch(
        functools.partial(output_kernel, out_rows),
        (pair, rows, attended, hid, *weights),
        name="output",
        micros=9,
        grid=(count,),
        in_specs=[
            pl.BlockSpec(memory_space=pltpu.SMEM),
            whole(length, width),
            whole(width, length),
            pl.BlockSpec((width, length), lambda i: (jnp.maximum(i - 1, 0), 0)),
            *([ANY] * 8 if gathered else [pl.BlockSpec((width, width), lambda i: (i, 0))]),
        ],
        out_specs=[whole(length, width), whole(3, 8, width), *[ANY] * gathered],
        out_shape=[array((length, width)), array((3, 8, width), F32), *[array((features, width))] * gathered],
        scratch=[
            *[pltpu.VMEM((length, width), F32)] * 2,
            *(weight_scratch(features, width) if gathered else ()),
        ],
    )


def feed_back_kernel(out_rows, grad_ref, slope_ref, weight_in_ref, *refs):
    step = pl.program_id(0)
    width = grad_ref.shape[1]
    if out_rows is None:
        weight_ref, grad_normed_ref, grad_feed_ref = refs
        weight_out = weight_ref[...]
    else:
        pieces, (grad_normed_ref, grad_feed_ref, full_ref, all_ref, sems, full_sems) = refs[:8], refs[8:]
        load_weight(step, pieces, all_ref, sems, out_rows, full_ref, full_sems, (0, 0, 1, 2))
        weight_out = all_ref[pl.ds(pl.multiple_of((step + 1) * width, width), width)]
    grad_hidden = nt(weight_out, grad_ref[...]).astype(BF16).astype(F32)
    grad_feed = (grad_hidden * slope_ref[...].astype(F32)).astype(BF16)
    grad_feed_ref[...] = grad_feed
    part = tn(grad_feed, weight_in_ref[...])

    @pl.when(step == 0)
    def _():
        grad_normed_ref[...] = part

    @pl.when(step > 0)
    def _():
        grad_normed_ref[...] += part


def feed_back(out_rows, grad, slope, weight_in, *weights):
    length, width = grad.shape
    features = slope.shape[0] + width
    count = slope.shape[0] // width
    gathered = out_rows is not None
    rows = pl.BlockSpec((width, length), lambda i: (i, 0))
    return launch(
        functools.partial(feed_back_kernel, out_rows),
        (grad, slope, weight_in, *weights),
        name="feed_back",
        micros=11,
        grid=(count,),
        in_specs=[
            whole(length, width),
            rows,
            pl.BlockSpec((width, width), lambda i: (i + 3, 0)),
            *([ANY] * 8 if gathered else [pl.BlockSpec((width, width), lambda i: (i + 1, 0))]),
        ],
        out_specs=[whole(length, width), rows, *[ANY] * gathered],
        out_shape=[array((length, width), F32), array(slope.shape), *[array((features, width))] * gathered],
        scratch=weight_scratch(features, width) if gathered else (),
    )


def attend_back_kernel(
    pair_ref, rows_ref, grad_ref, gain_ref, query_scale_ref, key_scale_ref, raw_ref, value_ref,
    attended_ref, log_ref, weight_out_ref, weight_in_ref, feed_grad_ref,
    projected_ref, grad_in_ref, gain_grad_ref, scale_grad_ref, bias_ref, grad_normed_ref,
):
    step = pl.program_id(0)

    @pl.when(step == 0)
    def _():
        fill_bias(pair_ref, bias_ref)
        grad_normed_ref[...] = feed_grad_ref[...]
        scale_grad_ref[...] = jnp.zeros_like(scale_grad_ref)

    length, width = grad_ref.shape
    query_scale, key_scale = query_scale_ref[...], key_scale_ref[...]
    grad_attended = nt(weight_out_ref[0], grad_ref[...]).astype(BF16)
    for head in range(GROUP):
        at = slice(head * HEAD, (head + 1) * HEAD)
        query_normal, query_inverse = column_norm(raw_ref[0, 0, at, :])
        key_normal, key_inverse = column_norm(raw_ref[1, 0, at, :])
        query = (query_normal * query_scale).astype(BF16) * BF16(FACTOR)
        key = (key_normal * key_scale).astype(BF16)
        value = value_ref[at, :]
        probs = jnp.exp(tn(key, query) + bias_ref[...] - log_ref[0, head : head + 1, :])
        grad_out = grad_attended[at]
        grad_probs = tn(value, grad_out)
        grad_value = nt(grad_out, probs.astype(BF16))
        delta = jnp.sum(grad_out.astype(F32) * attended_ref[at, :].astype(F32), axis=0, keepdims=True)
        grad_scores = (probs * (grad_probs - delta)).astype(BF16)
        grad_query = nn(key, grad_scores) * FACTOR
        grad_key = nt(query, grad_scores)
        for place_at, term in enumerate((grad_query * query_normal, grad_key * key_normal)):
            for lane in range(0, length, 128):
                scale_grad_ref[place_at] += term[:, lane : lane + 128]
        projected_ref[0, 0, at, :] = norm_back(query_normal, query_inverse, grad_query, query_scale, 0).astype(BF16)
        projected_ref[1, 0, at, :] = norm_back(key_normal, key_inverse, grad_key, key_scale, 0).astype(BF16)
        projected_ref[2, 0, at, :] = grad_value.astype(BF16)
    projected = projected_ref[...].reshape(3 * LANES, length)
    grad_normed_ref[...] += tn(projected, weight_in_ref[...].reshape(3 * LANES, width))

    @pl.when(step == pl.num_programs(0) - 1)
    def _():
        normal, inverse = row_norm(rows_ref[...].astype(F32))
        grad_normed = grad_normed_ref[...]
        grad_rows = norm_back(normal, inverse, grad_normed, gain_ref[...], 1)
        grad_in_ref[...] = (grad_ref[...].astype(F32) + grad_rows).astype(BF16)
        gain_grad_ref[...] = jnp.sum((grad_normed * normal).reshape(length // 8, 8, width), axis=0)


def attend_back(pair, rows, grad, gain, query_scale, key_scale, raw, value, attended, logs, weight_out,
                weight_in, feed_grad):
    length, width = grad.shape
    group_rows = pl.BlockSpec((LANES, length), lambda g: (g, 0))
    projected, *others = launch(
        attend_back_kernel,
        (pair, rows, grad, gain, query_scale, key_scale, raw, value, attended, logs,
         weight_out.reshape(-1, LANES, width), weight_in.reshape(-1, GROUPS, LANES, width), feed_grad),
        name="attend_back",
        micros=17,
        grid=(GROUPS,),
        in_specs=[
            pl.BlockSpec(memory_space=pltpu.SMEM),
            whole(length, width),
            whole(length, width),
            whole(1, width),
            whole(HEAD, 1),
            whole(HEAD, 1),
            pl.BlockSpec((2, 1, LANES, length), lambda g: (0, g, 0, 0)),
            group_rows,
            group_rows,
            pl.BlockSpec((1, 8, length), lambda g: (g, 0, 0)),
            pl.BlockSpec((1, LANES, width), lambda g: (g, 0, 0)),
            pl.BlockSpec((3, 1, LANES, width), lambda g: (0, g, 0, 0)),
            whole(length, width),
        ],
        out_specs=[
            pl.BlockSpec((3, 1, LANES, length), lambda g: (0, g, 0, 0)),
            whole(length, width),
            whole(8, width),
            whole(2, HEAD, 128),
        ],
        out_shape=[
            array((3, GROUPS, LANES, length)),
            array((length, width)),
            array((8, width), F32),
            array((2, HEAD, 128), F32),
        ],
        scratch=[pltpu.VMEM((length, length), F32), pltpu.VMEM((length, width), F32)],
    )
    return projected.reshape(3 * width, length), *others


def sends(fine, first, second):
    _, depth, high, wide = fine
    number = lambda c, z, y, x: ((c * depth + z) * high + y) * wide + x
    return [
        (number(c, z, y, x), number(c, *(first, second)[c](z, y, x)))
        for c in range(2)
        for z in range(depth)
        for y in range(high)
        for x in range(wide)
    ]


def next_x(z, y, x):
    return z, y, 1 - x


def next_y(z, y, x):
    return z, 1 - y, x


def sideways(value, fine):
    return lax.ppermute(value, ALL, sends(fine, next_x, next_y))


def turned(value, fine):
    return lax.ppermute(value, ALL, sends(fine, next_y, next_x))


def along(value, fine):
    depth = fine[1]
    return lax.ppermute(
        value, ALL, sends(fine, lambda z, y, x: ((z + 1) % depth, y, x), lambda z, y, x: ((z - 1) % depth, y, x))
    )


def opposite(value, fine):
    depth = fine[1]
    return lax.ppermute(value, "z", [(z, (z + 2) % depth) for z in range(depth)])


def swap(value):
    return lax.ppermute(value, "section", [(0, 1), (1, 0)])


def place():
    return [lax.axis_index(axis) for axis in ALL]


def either(condition, make_first, make_second):
    @pl.when(condition)
    def _():
        make_first().start()

    @pl.when(jnp.logical_not(condition))
    def _():
        make_second().start()


def slot_copy(slot, keep_ref, pass_ref, owner, target, sem, rows=None):
    index = slot % 2 if isinstance(slot, int) else lax.rem(slot, 2)
    view = (lambda ref: ref.at[index]) if rows is None else (lambda ref: ref.at[index, rows])
    kept = pltpu.make_async_copy(view(keep_ref), target, sem)
    either(slot // 2 == owner, lambda: kept, lambda: pltpu.make_async_copy(view(pass_ref), target, sem))
    return kept


def half_of(rows):
    return -(-rows // 32) * 16


def pick_kernel(layer, own_ref, other_ref, *refs):
    extra, (shard_ref, half_ref, sem) = refs[:-3], refs[-3:]
    core = lax.axis_index("section")
    count, rows, half = own_ref.shape[0], shard_ref.shape[0], half_ref.shape[0]
    goal = shard_ref.at[pl.ds(0, count)]
    copy = pltpu.make_async_copy(own_ref, goal, sem)
    either(core == layer, lambda: copy, lambda: pltpu.make_async_copy(other_ref, goal, sem))
    if extra:
        shard_ref[count:] = extra[0][...]
    copy.wait()

    @pl.when(core == 0)
    def _():
        half_ref[...] = shard_ref[:half]

    @pl.when(core == 1)
    def _():
        half_ref[...] = shard_ref[rows - half :]


def pick(layer, own, other, *extra):
    rows, width = own.shape[0] + sum(value.shape[0] for value in extra), own.shape[1]
    return launch(
        functools.partial(pick_kernel, layer), (own, other, *extra), name="pick", micros=1.5,
        in_specs=[ANY] * 2 + [VMEM] * len(extra), out_specs=[VMEM] * 2,
        out_shape=[array((rows, width)), array((half_of(rows), width))],
        scratch=[pltpu.SemaphoreType.DMA],
    )


def line_kernel(own_ref, near_ref, other_ref, far_ref, far_other_ref, keep_ref, pass_ref, sems):
    core, z = lax.axis_index("section"), lax.axis_index("z")
    depth = 4
    rows, half = own_ref.shape[0], far_ref.shape[0]
    below, above, far = lax.rem(z + depth - 1, depth), lax.rem(z + 1, depth), lax.rem(z + 2, depth)
    near_at, other_at = jnp.where(core == 0, below, above), jnp.where(core == 0, above, below)
    rest = rows - half
    first, second = pl.multiple_of(core * rest, 16), pl.multiple_of((1 - core) * half, 16)
    skipped = pl.multiple_of((1 - core) * (half - rest), 16)
    moves = (
        (own_ref, z, pl.ds(0, rows)),
        (near_ref, near_at, pl.ds(0, rows)),
        (other_ref, other_at, pl.ds(0, rows)),
        (far_ref, far, pl.ds(first, half)),
        (far_other_ref.at[pl.ds(skipped, rest)], far, pl.ds(second, rest)),
    )
    copies = []
    for at, (source, slot, part) in enumerate(moves):
        index = lax.rem(slot, 2)
        kept = pltpu.make_async_copy(source, keep_ref.at[index, part], sems.at[at])
        passed = pltpu.make_async_copy(source, pass_ref.at[index, part], sems.at[at])
        either(slot // 2 == core, lambda: kept, lambda: passed)
        copies.append(kept)
    for copy in copies:
        copy.wait()


def line_of(own, near, near_other, far, far_other):
    rows, width = own.shape
    return launch(
        line_kernel, (own, near, near_other, far, far_other), name="line", micros=2.5,
        in_specs=[ANY] * 5, out_specs=[VMEM] * 2, out_shape=[array((2, rows, width))] * 2,
        scratch=[pltpu.SemaphoreType.DMA((5,))],
    )


def piece_copies(pieces, target, sems, rows):
    line_keep, line_pass, side_keep, side_pass, turn_keep, turn_pass, corner, corner_other = pieces
    core, _, y, x = place()
    high, wide = 2, 2
    take = pl.ds(0, rows)
    side_y, side_x = jnp.where(core == 0, y, 1 - y), jnp.where(core == 0, 1 - x, x)
    copies = []
    for slot in range(4):
        lines = (
            (line_keep, line_pass, core, y, x),
            (side_keep, side_pass, core, side_y, side_x),
            (turn_keep, turn_pass, 1 - core, 1 - side_y, 1 - side_x),
            (corner_other, corner, core, 1 - y, 1 - x),
        )
        for at, (keep, passed, owner, line_y, line_x) in enumerate(lines):
            start = pl.multiple_of(((slot * high + line_y) * wide + line_x) * rows, 8)
            goal = target.at[pl.ds(start, rows)]
            copies.append(slot_copy(slot, keep, passed, owner, goal, sems.at[4 * slot + at], take))
    return copies


def rows_copy(low_ref, high_ref, start, count, target_ref, at, sem, crossing):
    split = low_ref.shape[0]
    goal = target_ref.at[pl.ds(at, count)]
    copy = pltpu.make_async_copy(low_ref.at[pl.ds(0, count)], goal, sem)

    @pl.when(start + count <= split)
    def _():
        pltpu.make_async_copy(low_ref.at[pl.ds(pl.multiple_of(start, 16), count)], goal, sem).start()

    @pl.when(start >= split)
    def _():
        pltpu.make_async_copy(high_ref.at[pl.ds(pl.multiple_of(start - split, 16), count)], goal, sem).start()

    for first in crossing:
        if first < split < first + count:
            low = split - first

            @pl.when(start == first)
            def _():
                pltpu.make_async_copy(low_ref.at[pl.ds(first, low)], target_ref.at[pl.ds(at, low)], sem).start()
                rest = target_ref.at[pl.ds(at + low, count - low)]
                pltpu.make_async_copy(high_ref.at[pl.ds(0, count - low)], rest, sem).start()

    return copy


def partial_kernel(
    fine, own_low, own_high, other_low, other_high, right_ref, right_other_ref,
    turn_any, keep_any, pass_any, near_any, half_any, turn_ref, keep_ref, pass_ref, near_ref, half_ref, left_ref, sems,
    out_sems,
):
    core, z, y, x = place()
    depth, high, wide = fine[1:]
    outs = [
        pltpu.make_async_copy(source, goal, out_sems.at[at])
        for at, (source, goal) in enumerate(
            ((turn_ref, turn_any), (keep_ref, keep_any), (pass_ref, pass_any), (near_ref, near_any), (half_ref, half_any))
        )
    ]
    split = own_low.shape[0]
    rows = keep_ref.shape[1]
    half = half_ref.shape[1]
    step = pl.program_id(0)
    side_y, side_x = jnp.where(core == 0, y, 1 - y), jnp.where(core == 0, 1 - x, x)
    near, far = lax.rem(z + jnp.where(core == 0, 1, depth - 1), depth), lax.rem(z + 2, depth)
    whole_at = (split // rows) * rows
    crossing = (whole_at, whole_at + rows - half)

    def row(slot, line_y, line_x):
        return ((slot * high + line_y) * wide + line_x) * rows

    kept, passed = 2 * core, 2 - 2 * core
    parts = [(row(passed + at, 1 - y, 1 - x), rows) for at in range(2)]
    parts += [(row(kept + at, side_y, side_x), rows) for at in range(2)]
    parts += [(row(passed + at, side_y, side_x), rows) for at in range(2)]
    parts += [(row(near, y, x), rows)]
    parts += [(row(slot, y, x) + core * (rows - half), half) for slot in (z, far)]
    sides = ((own_low, own_high), (other_low, other_high))

    def copies():
        at = 0
        for index, (start, count) in enumerate(parts):
            for side, (low, up) in enumerate(sides):
                yield index, low, up, start, count, left_ref.at[side], at, sems.at[side, index]
            at += count

    @pl.when(step == 0)
    def _():
        for _, *what in copies():
            rows_copy(*what, crossing)

    def wait(indices):
        for index, low, _, _, count, target, at, sem in copies():
            if index in indices:
                pltpu.make_async_copy(low.at[pl.ds(0, count)], target.at[pl.ds(at, count)], sem).wait()

    def product(first, count):
        own = nn(left_ref[0, first : first + count], right_ref[...])
        return (own + nn(left_ref[1, first : first + count], right_other_ref[...])).astype(BF16)

    for at, out in enumerate((turn_ref, keep_ref, pass_ref)):

        @pl.when(step == at)
        def _():
            wait((2 * at, 2 * at + 1))
            out[...] = product(2 * at * rows, 2 * rows).reshape(out.shape)
            outs[at].start()

    @pl.when(step == 3)
    def _():
        wait((6, 7, 8))
        last = product(6 * rows, rows + 2 * half)
        near_ref[...] = last[:rows]
        half_ref[...] = last[rows:].reshape(half_ref.shape)
        outs[3].start()
        outs[4].start()
        for copy in outs:
            copy.wait()


def partial(fine, own_low, own_high, other_low, other_high, right, right_other):
    length, width = right.shape
    features = own_low.shape[0] + own_high.shape[0]
    rows = features // (fine[1] * fine[2] * fine[3])
    half = half_of(rows)
    shapes = [(2, rows, width)] * 3 + [(rows, width), (2, half, width)]
    return launch(
        functools.partial(partial_kernel, fine), (own_low, own_high, other_low, other_high, right, right_other),
        name="partial", micros=features / 700, grid=(4,),
        in_specs=[ANY] * 4 + [whole(length, width)] * 2,
        out_specs=[ANY] * 5,
        out_shape=[array(shape) for shape in shapes],
        scratch=[
            *[pltpu.VMEM(shape, BF16) for shape in shapes],
            pltpu.VMEM((2, 7 * rows + 2 * half, length), BF16),
            pltpu.SemaphoreType.DMA((2, 9)),
            pltpu.SemaphoreType.DMA((5,)),
        ],
    )


def depth_kernel(
    near_ref, half_ref, keep_ref, pass_ref, keep_other, pass_other,
    near_out, far_out, own_out, near_got, half_got, sems,
):
    core, z = lax.axis_index("section"), lax.axis_index("z")
    depth = 4
    half = half_ref.shape[1]
    near = lax.rem(z + jnp.where(core == 0, 1, depth - 1), depth)
    part = pl.ds(pl.multiple_of(core * (near_ref.shape[0] - half), 16), half)
    copies = []
    for at, (keep, pass_, owner) in enumerate(((keep_ref, pass_ref, core), (keep_other, pass_other, 1 - core))):
        copies.append(slot_copy(near, keep, pass_, owner, near_got.at[at], sems.at[3 * at]))
        for index, slot in enumerate((z, lax.rem(z + 2, depth))):
            copies.append(slot_copy(slot, keep, pass_, owner, half_got.at[at, index], sems.at[3 * at + 1 + index], part))
    for copy in copies:
        copy.wait()
    near_total = near_ref[...].astype(F32) + near_got[0].astype(F32) + near_got[1].astype(F32)
    near_out[...] = near_total.astype(BF16)
    for index, out in enumerate((own_out, far_out)):
        total = half_ref[index].astype(F32) + half_got[0, index].astype(F32) + half_got[1, index].astype(F32)
        out[...] = total.astype(BF16)


def depth_sums(near, halves, keep, passed, keep_other, passed_other):
    rows, width = near.shape
    half = halves.shape[1]
    return launch(
        depth_kernel, (near, halves, keep, passed, keep_other, passed_other), name="depth", micros=2,
        in_specs=[VMEM] * 2 + [ANY] * 4, out_specs=[VMEM] * 3,
        out_shape=[array((rows, width)), array((half, width)), array((half, width))],
        scratch=[
            pltpu.VMEM((2, rows, width), BF16),
            pltpu.VMEM((2, 2, half, width), BF16),
            pltpu.SemaphoreType.DMA((6,)),
        ],
    )


def total_kernel(near_ref, near_other, far_ref, far_other, own_ref, own_other, *refs):
    second, out_ref = refs[:-1], refs[-1]
    core = lax.axis_index("section")
    rows, half = near_ref.shape[0], far_ref.shape[0]
    near = near_ref[...].astype(F32) + near_other[...].astype(F32)
    mine = far_ref[...].astype(F32) + own_ref[...].astype(F32)
    other = far_other[...].astype(F32) + own_other[...].astype(F32)
    low, high = jnp.where(core == 0, mine, other), jnp.where(core == 0, other, mine)
    out_ref[:half] = near[:half] + low
    out_ref[half:] = near[half:] + high[2 * half - rows :]
    if second:

        @pl.when(core == 1)
        def _():
            out_ref[...] = second[0][...]


def total(near, near_other, far, far_other, own, own_other, *second):
    values = (near, near_other, far, far_other, own, own_other, *second)
    return launch(
        total_kernel, values, name="total", micros=1.5,
        in_specs=[VMEM] * len(values), out_specs=VMEM, out_shape=array(near.shape, F32),
    )


class Order:
    def __init__(self, first):
        self.last = first
        self.moving = []

    def run(self, function, *values):
        values, _ = lax.optimization_barrier((values, self.last))
        return self.fence(function(*values))

    def fence(self, *result):
        due = [value for value, left in self.moving if left == 0]
        self.moving = [(value, left - 1) for value, left in self.moving if left > 0]
        result, self.last, _ = lax.optimization_barrier((result, self.last, due))
        if result:
            self.last = jax.tree.leaves(result)[0]
            return result[0]

    def move(self, way, *values, count=1):
        values, _ = lax.optimization_barrier((values, self.last))
        moved = [way(value) for value in values]
        self.moving += [(value, count - 1) for value in moved]
        return moved if len(values) > 1 else moved[0]

    def swap(self, *values, count=1):
        return self.move(swap, *values, count=count)


def total_along(value, axis, size):
    return sum([lax.ppermute(value, axis, [(i, (i + k) % size) for i in range(size)]) for k in range(1, size)], value)


def total_of(value, fine):
    for axis, size in zip(ALL, fine):
        value = total_along(value, axis, size) if size < 8 else lax.psum(value, axis)
    return value


def added(first, second):
    return (first.astype(F32) + second.astype(F32)).astype(BF16)


class Gather:
    def __init__(self, order, fine, shard, half):
        self.order, self.fine, self.shard, self.half = order, fine, shard, half

    def along(self, count=1):
        self.near = self.order.move(functools.partial(along, fine=self.fine), self.shard, count=count)
        self.far = self.order.move(functools.partial(opposite, fine=self.fine), self.half, count=count)

    def across(self, count=1):
        self.near_other, self.far_other = self.order.swap(self.near, self.far, count=count)

    def line(self):
        self.keep, self.passed = self.order.run(
            line_of, self.shard, self.near, self.near_other, self.far, self.far_other
        )

    def side(self, count=1):
        self.side_passed = self.order.move(functools.partial(sideways, fine=self.fine), self.passed, count=count)
        self.side_keep = self.order.move(functools.partial(sideways, fine=self.fine), self.keep, count=count)

    def turn(self, count=1):
        self.corner = self.order.move(functools.partial(turned, fine=self.fine), self.side_passed, count=count)

    def rest(self, count=1):
        self.turn_keep, self.turn_passed = self.order.swap(self.side_keep, self.side_passed, count=count)

    def meet(self):
        self.corner_other = self.order.swap(self.corner)

    def pieces(self):
        return (
            self.keep, self.passed, self.side_keep, self.side_passed, self.turn_keep, self.turn_passed,
            self.corner, self.corner_other,
        )


class Scatter:
    def __init__(self, order, fine, values):
        self.order, self.fine = order, fine
        self.turn, self.keep, self.passed, self.near, self.halves = values

    def start(self, count=1):
        self.turn = self.order.move(functools.partial(turned, fine=self.fine), self.turn, count=count)
        self.keep = self.order.move(functools.partial(sideways, fine=self.fine), self.keep, count=count)

    def add(self):
        self.passed = self.order.run(added, self.passed, self.turn)

    def pass_on(self):
        self.passed = self.order.move(functools.partial(sideways, fine=self.fine), self.passed)

    def keep_across(self):
        self.keep_other = self.order.swap(self.keep)

    def meet(self):
        self.passed_other = self.order.swap(self.passed)

    def parts(self):
        return self.near, self.halves, self.keep, self.passed, self.keep_other, self.passed_other

    def along(self, values, count=1):
        near, far, self.own = values
        self.near = self.order.move(functools.partial(along, fine=self.fine), near, count=count)
        self.far = self.order.move(functools.partial(opposite, fine=self.fine), far, count=count)

    def own_across(self):
        self.own_other = self.order.swap(self.own)

    def across(self):
        self.near_other, self.far_other = self.order.swap(self.near, self.far)

    def ends(self):
        return self.near, self.near_other, self.far, self.far_other, self.own, self.own_other


def body(fine, inputs, cotangent, lengths, weight_in, weight_out, scales):
    length, width = inputs.shape[2], inputs.shape[3]
    core, z, y, x = place()
    depth = fine[1]
    device = (z * fine[2] + y) * fine[3] + x
    pair = lax.dynamic_index_in_dim(lengths, core, 0, False)
    scale_count = scales.shape[1]
    whole_scales = scale_count * depth * fine[2] * fine[3]
    by_core = lambda first, second: (jnp.where(core == 0, first, second), jnp.where(core == 0, second, first))

    shift = lambda axis: lambda value: lax.ppermute(value, axis, [(0, 1), (1, 0)])
    spread = lambda mine, other: jnp.stack(by_core(mine, other))[None, :, None]
    chip = functools.partial(partial, fine)

    def padded(flat):
        return jnp.pad(flat, (0, -flat.shape[0] % 1024)).reshape(-1, 128)

    own_scales = lax.dynamic_update_slice(
        jnp.zeros((2 * whole_scales,), F32), scales[0].astype(F32), (core * whole_scales + device * scale_count,)
    )
    scale = padded(own_scales)

    def vectors_of(scale):
        scale = scale.reshape(-1)[: 2 * whole_scales].reshape(2, whole_scales)
        return [(s[None, :width], s[width : width + HEAD, None], s[width + HEAD :, None]) for s in scale]

    def own_rows(inputs, cotangent):
        rows = lax.dynamic_index_in_dim(inputs, core, 0, False)[0]
        grad = lax.dynamic_index_in_dim(cotangent, core, 0, False)[0]
        position = lax.broadcasted_iota(jnp.int32, (length, 1), 0)
        return rows, jnp.where(position < pair[0, 0] + pair[0, 1], grad, jnp.zeros_like(grad))

    order = Order(scale)
    butterfly = lambda by: lambda value: lax.ppermute(value, "z", [(i, i ^ by) for i in range(depth)])
    out = functools.partial(output, pair)
    if depth == 4:
        in_rows, out_rows = weight_in.shape[1], weight_out.shape[1]
        gather = lambda values: Gather(order, fine, *values)
        other_in, other_out, got = order.swap(weight_in[0], weight_out[0], scale)
        order.fence()
        first = gather(order.run(functools.partial(pick, 0), weight_in[0], other_in))
        first.along()
        scale = scale + got
        got = order.move(shift("x"), scale)
        order.fence()
        first.across()
        scale = scale + got
        got = order.move(shift("y"), scale)
        second = gather(order.run(functools.partial(pick, 0), weight_out[0], other_out))
        first.line()
        first.side()
        second.along()
        third, fourth, (rows_0, grad_1) = order.run(
            lambda own_in, other_in, own_out, other_out, *values: (
                pick(1, own_in, other_in), pick(1, own_out, other_out), own_rows(*values)
            ),
            weight_in[0], other_in, weight_out[0], other_out, inputs, cotangent,
        )
        third, fourth = gather(third), gather(fourth)
        first.turn(count=3)
        second.across()
        first.rest(count=2)
        scale = scale + got
        got = order.move(butterfly(1), scale, count=2)
        order.fence()
        second.line()
        scale = scale + got
        got = order.move(butterfly(2), scale)
        order.fence()
        vectors_0, vectors_1 = order.run(vectors_of, scale + got)
        second.side(count=2)
        third.along(count=2)
        first.meet()
        order.fence()
        front, out = functools.partial(attend, in_rows, pair), functools.partial(output, pair, out_rows)
        normed_0, raw_0, value_0, attended_0, logs_0, weight_in_0 = order.run(front, rows_0, *vectors_0, *first.pieces())
        second.turn()
        second.rest()
        third.across()
        hidden_0, slope_0 = order.run(hidden, normed_0, weight_in_0)
        second.meet()
        third.line()
        third.side()
        fourth.along()
        rows_1, squares_0, weight_out_0 = order.run(out, rows_0, attended_0, hidden_0, *second.pieces())
        third.turn(count=3)
        fourth.across()
        third.rest(count=2)
        order.fence()
        fourth.line()
        grad_1_other = order.swap(grad_1)
        order.fence()
        fourth.side(count=2)
        third.meet()
        order.fence()
        attended_0_other, normed_0_other, hidden_0_other = order.swap(attended_0, normed_0, hidden_0)
        normed_1, raw_1, value_1, attended_1, logs_1, weight_in_1 = order.run(front, rows_1, *vectors_1, *third.pieces())
        fourth.turn()
        fourth.rest()
        attended_1_other, normed_1_other = order.swap(attended_1, normed_1)
        hidden_1, slope_1 = order.run(hidden, normed_1, weight_in_1)
        fourth.meet()
        order.fence()
        hidden_1_other, rows_1_other = order.swap(hidden_1, rows_1)
        feed_1, low_1, weight_out_1 = order.run(
            functools.partial(feed_back, out_rows), grad_1, slope_1, weight_in_1, *fourth.pieces()
        )
    else:
        weight_in_0, weight_in_1 = jnp.split(lax.all_gather(weight_in[0], ALL, axis=0, tiled=True), 2)
        weight_out_0, weight_out_1 = jnp.split(lax.all_gather(weight_out[0], ALL, axis=0, tiled=True), 2)
        vectors_0, vectors_1 = vectors_of(total_of(scale, fine))
        rows_0, grad_1 = own_rows(inputs, cotangent)
        front, out = functools.partial(attend, None, pair), functools.partial(output, pair, None)
        normed_0, raw_0, value_0, attended_0, logs_0 = order.run(front, rows_0, *vectors_0, weight_in_0)
        hidden_0, slope_0 = order.run(hidden, normed_0, weight_in_0)
        rows_1, squares_0 = order.run(out, rows_0, attended_0, hidden_0, weight_out_0)
        normed_1, raw_1, value_1, attended_1, logs_1 = order.run(front, rows_1, *vectors_1, weight_in_1)
        hidden_1, slope_1 = order.run(hidden, normed_1, weight_in_1)
        feed_1, low_1 = order.run(functools.partial(feed_back, None), grad_1, slope_1, weight_in_1, weight_out_1)
    out, back, feed = functools.partial(output, pair, None), functools.partial(attend_back, pair), functools.partial(feed_back, None)
    kept_1 = (rows_1, grad_1, *vectors_1, raw_1, value_1, attended_1, logs_1, weight_out_1, weight_in_1)

    def small_sums(squares_0, squares_1, gain_0, heads_0, gain_1, heads_1):
        sums = [jnp.sum(squares, axis=(1, 2)) for squares in (squares_0, squares_1)]
        scale_grads = [
            jnp.concatenate([jnp.sum(gain, axis=0), jnp.sum(heads, axis=2).reshape(-1)])
            for gain, heads in ((gain_0, heads_0), (gain_1, heads_1))
        ]
        return padded(jnp.concatenate([jnp.sum(pair).astype(F32)[None], *sums, *scale_grads]))

    if depth == 4:
        low_1_other = order.swap(low_1)
        out_1 = Scatter(order, fine, order.run(
            chip, attended_1, hidden_1, attended_1_other, hidden_1_other, grad_1, grad_1_other
        ))
        out_1.start()
        top_1, grad_0, gain_1, heads_1 = order.run(back, *kept_1, feed_1)
        grad_0_other = order.swap(grad_0)
        top_1_other = order.swap(top_1, count=3)
        out_1.add()
        out_1.pass_on()
        out_1.keep_across()
        out_0 = Scatter(order, fine, order.run(
            chip, attended_0, hidden_0, attended_0_other, hidden_0_other, grad_0, grad_0_other
        ))
        out_0.start()
        out_1.meet()
        feed_0, low_0 = order.run(feed, grad_0, slope_0, weight_in_0, weight_out_0)
        out_0.add()
        out_0.pass_on()
        out_0.keep_across()
        low_0_other = order.swap(low_0)
        in_1, ends = order.run(
            lambda values, parts: (chip(*values), depth_sums(*parts)),
            (top_1, low_1, top_1_other, low_1_other, normed_1, normed_1_other), out_1.parts(),
        )
        in_1 = Scatter(order, fine, in_1)
        in_1.start()
        out_1.along(ends)
        out_0.meet()
        kept_0 = (rows_0, grad_0, *vectors_0, raw_0, value_0, attended_0, logs_0, weight_out_0, weight_in_0)
        top_0, grad_first, gain_0, heads_0 = order.run(back, *kept_0, feed_0)
        top_0_other = order.swap(top_0)
        ends, in_1.passed = order.run(
            lambda parts, first, second: (depth_sums(*parts), added(first, second)), out_0.parts(), in_1.passed, in_1.turn
        )
        in_1.pass_on()
        out_0.along(ends)
        in_1.keep_across()
        out_0.own_across()
        in_0 = Scatter(order, fine, order.run(chip, top_0, low_0, top_0_other, low_0_other, normed_0, normed_0_other))
        in_1.meet()
        out_1.across()
        order.fence()
        ends = order.run(depth_sums, *in_1.parts())
        in_0.start()
        in_1.along(ends)
        out_1.own_across()
        grad_first_other = order.swap(grad_first)

        def last_output(values, squares_0, *others):
            result, squares = out(*values)
            return result, small_sums(squares_0, squares, *others)

        result_1, small = order.run(
            last_output, (rows_1, attended_1, hidden_1, weight_out_1), squares_0, gain_0, heads_0, gain_1, heads_1
        )
        in_0.add()
        in_0.pass_on()
        in_0.keep_across()
        out_0.across()
        got = order.move(shift("x"), small)
        out_grad_1 = order.run(total, *out_1.ends())
        small = small + got
        in_0.meet()
        order.fence()
        got = order.move(shift("y"), small)
        result_1_other = order.swap(result_1)
        in_1.across()
        in_1.own_across()
        ends = order.run(depth_sums, *in_0.parts())
        in_0.along(ends)
        small = small + got
        got = order.move(butterfly(1), small)
        in_0.own_across()
        def spread_both(rows_1, rows_other, result, result_other, first, first_other, grad_0, grad_other):
            outputs = jnp.where(core == 0, rows_1, result), jnp.where(core == 0, rows_other, result_other)
            grads = jnp.where(core == 0, first, grad_0), jnp.where(core == 0, first_other, grad_other)
            return spread(*outputs), spread(*grads)

        out_grad, in_grad_1, (outputs, input_grads) = order.run(
            lambda first, second, values: (total(*first), total(*second), spread_both(*values)),
            (*out_0.ends(), out_grad_1), in_1.ends(),
            (rows_1, rows_1_other, result_1, result_1_other, grad_first, grad_first_other, grad_0, grad_0_other),
        )
        in_0.across()
        small = small + got
        got = order.move(butterfly(2), small, count=2)
        order.fence()
        in_grad = order.run(total, *in_0.ends(), in_grad_1)[None]
        out_grad = out_grad[None]
        small = small + got
        small = small + order.swap(small)
    else:
        top_1, grad_0, gain_1, heads_1 = order.run(back, *kept_1, feed_1)
        feed_0, low_0 = order.run(feed, grad_0, slope_0, weight_in_0, weight_out_0)
        kept_0 = (rows_0, grad_0, *vectors_0, raw_0, value_0, attended_0, logs_0, weight_out_0, weight_in_0)
        top_0, grad_first, gain_0, heads_0 = order.run(back, *kept_0, feed_0)
        result_1, squares_1 = order.run(out, rows_1, attended_1, hidden_1, weight_out_1)
        own = lambda low, high, right: nn(jnp.concatenate([low, high]), right).astype(BF16)
        summed = lambda first, second: lax.psum_scatter(
            jnp.concatenate([first, second]), ALL, scatter_dimension=0, tiled=True
        ).astype(F32)[None]
        in_grad = summed(own(top_0, low_0, normed_0), own(top_1, low_1, normed_1))
        out_grad = summed(own(attended_0, hidden_0, grad_0), own(attended_1, hidden_1, grad_1))
        small = small_sums(squares_0, squares_1, gain_0, heads_0, gain_1, heads_1)
        for axis in ALL:
            small = lax.psum(small, axis)
        outputs, input_grads = [
            spread(mine, swap(given)) for mine, given in (by_core(rows_1, result_1), by_core(grad_first, grad_0))
        ]
    small = small.reshape(-1)
    statistics = jnp.sqrt(lax.dynamic_slice(small, (1 + 3 * core,), (3,)) / (small[0] * width))
    scale_grad = lax.dynamic_slice(small, (7 + core * whole_scales + device * scale_count,), (scale_count,))
    return outputs, input_grads, in_grad, out_grad, scale_grad[None], statistics[None]


def solution(mesh):
    count = mesh.shape["dp"]
    fine = Mesh(mesh.devices.reshape(2, count // 4, 2, 2), ALL)
    return jax.shard_map(
        functools.partial(body, (2, count // 4, 2, 2)),
        mesh=fine,
        in_specs=(
            P(None, DP, None, None),
            P(None, DP, None, None),
            P(None, DP, None),
            P("section", DP, None),
            P("section", DP, None),
            P("section", DP),
        ),
        out_specs=(
            P("section", None, DP, None, None),
            P("section", None, DP, None, None),
            P("section", DP, None),
            P("section", DP, None),
            P("section", DP),
            P("section", None),
        ),
        check_vma=False,
    )
```
